128 devices in a mesh: seq: 32 (over x, y, core), tp: 4 (over z).
Axes of the slice: x: 4, y: 4, z: 4, core: 2. Of those that a mesh axis runs over, the one named last changes fastest.
Arguments:
- tokens: bfloat16 [2, 4096, 2048], P(None, 'seq'), may hold values from -6 to 6
- gain_mix: float32 [2048], replicated, may hold values from 0.5 to 1.5
- w_in: bfloat16 [2048, 3, 2048], P(None, None, 'tp'), may hold values from -0.125 to 0.125
- conv_weight: float32 [3, 2048], P(None, 'tp'), may hold values from -2.5 to 2.5
- w_out: bfloat16 [2048, 2048], P('tp'), may hold values from -0.125 to 0.125
- gain_ffn: float32 [2048], replicated, may hold values from 0.5 to 1.5
- w_gate: bfloat16 [2048, 8192], P(None, 'tp'), may hold values from -0.125 to 0.125
- w_up: bfloat16 [2048, 8192], P(None, 'tp'), may hold values from -0.125 to 0.125
- w_down: bfloat16 [8192, 2048], P('tp'), may hold values from -0.0625 to 0.0625
- cotangent: bfloat16 [2, 4096, 2048], P(None, 'seq'), may hold values from -6 to 6
- lengths: int32 [2], replicated, may hold values from 1024 to 4096, as said below
Outputs:
- output: bfloat16 [2, 4096, 2048], P(None, 'seq')
- grad_tokens: bfloat16 [2, 4096, 2048], P(None, 'seq')
- grad_gain_mix: float32 [2048], replicated
- grad_w_in: float32 [2048, 3, 2048], P('seq', None, 'tp')
- grad_conv: float32 [3, 2048], P(None, 'tp')
- grad_w_out: float32 [2048, 2048], P('tp', 'seq')
- grad_gain_ffn: float32 [2048], replicated
- grad_w_gate: float32 [2048, 8192], P('seq', 'tp')
- grad_w_up: float32 [2048, 8192], P('seq', 'tp')
- grad_w_down: float32 [8192, 2048], P('tp', 'seq')
The draws below stay inside these ranges and needn't reach their ends.
Inputs may be any that keep to these rules, and one draw needn't show every extreme that they name: `lengths`: one of the two sequences, which one drawn from the seed, has length 4096; the other between 1024 and 3072.
All inputs are finite; a program needn't handle non-finite values.
Results may differ from the reference program's by a relative error of at most 0.017.
Values may be sent and summed in bfloat16 or wider, within the bound.
No kernel may reach another device: no remote copies, remote signals or barrier semaphores. Data moves between devices by JAX's collectives and lax.ppermute only.
A program may use at most 192 MiB of HBM per device.

```python
import jax
import jax.numpy as jnp
from jax import lax

D = 2048
FF = 8192
KERNEL = 3
SEQS = 2
LEN = 4096


def draw_lengths(key, part):
    key = jax.random.fold_in(key, 7)
    first_key, second_key = jax.random.split(key)
    longest = jax.random.randint(first_key, (), 0, 2)
    shorter = jax.random.randint(second_key, (), LEN // 4, 3 * LEN // 4 + 1)
    return jnp.where(jnp.arange(2) == longest, LEN, shorter).astype(jnp.int32)


def steps_of(rng, dims, shards, least, high):
    loudness = 1.0
    for axis_at, blocks in shards:
        draws = jax.random.uniform(jax.random.fold_in(jax.random.fold_in(rng, 6), axis_at), (blocks,), jnp.float32, least / len(shards), high / len(shards))
        loudness = loudness * jnp.repeat(jnp.exp(draws), dims[axis_at] // blocks).reshape((-1,) + (1,) * (len(dims) - 1 - axis_at))
    return loudness


def gaussian(rng, shape, width, reach, pieces=(), kind=jnp.bfloat16):
    values = jax.random.normal(rng, shape, jnp.float32) * width
    if len(pieces) > 0:
        values = steps_of(rng, shape, pieces, -0.22, 0.18) * values
    return jnp.clip(values, min=-reach, max=reach).astype(kind)


def setup_inputs(seed: int = 0) -> dict:
    seeds = jax.random.split(jax.random.key(seed), 12)
    return {
        "tokens": gaussian(seeds[0], (SEQS, LEN, D), 1.0, 6.0, ((1, 32),)),
        "gain_mix": jnp.clip(1.0 + 0.1 * jax.random.normal(seeds[1], (D,), jnp.float32), 0.5, 1.5),
        "w_in": gaussian(seeds[2], (D, 3, D), D ** -0.5, 0.125, ((2, 4),)),
        "conv_weight": gaussian(seeds[3], (KERNEL, D), 0.6, 2.5, ((1, 4),), jnp.float32),
        "w_out": gaussian(seeds[4], (D, D), D ** -0.5, 0.125, ((0, 4),)),
        "gain_ffn": jnp.clip(1.0 + 0.1 * jax.random.normal(seeds[5], (D,), jnp.float32), 0.5, 1.5),
        "w_gate": gaussian(seeds[6], (D, FF), D ** -0.5, 0.125, ((1, 4),)),
        "w_up": gaussian(seeds[7], (D, FF), D ** -0.5, 0.125, ((1, 4),)),
        "w_down": gaussian(seeds[8], (FF, D), FF ** -0.5, 0.0625, ((0, 4),)),
        "cotangent": gaussian(seeds[9], (SEQS, LEN, D), 1.0, 6.0, ((1, 32),)),
        "lengths": draw_lengths(jax.random.fold_in(seeds[11], 71), 0),
    }


epsilon = 1e-05

@jax.custom_vjp
def low(v):
    return lax.optimization_barrier(v.astype(jnp.bfloat16)).astype(jnp.float32)

@jax.custom_vjp
def low_back(v):
    return v

def low_keep(v):
    return (low(v), None)

def low_pass(kept, grad):
    return (grad,)

def back_keep(v):
    return (v, None)

def back_low(kept, grad):
    return (low(grad),)
low.defvjp(low_keep, low_pass)
low_back.defvjp(back_keep, back_low)

def normalize(values):
    return lax.rsqrt(lax.optimization_barrier(jnp.mean(values * values, -1, keepdims=True)) + epsilon)

def forward(tokens_f, gain_mix, w_in, conv_weight, w_out, gain_ffn, w_gate, w_up, w_down):
    precise = lax.Precision.HIGHEST
    length = tokens_f.shape[1]
    normed = low(tokens_f * normalize(tokens_f) * gain_mix)
    triple = low_back(jnp.einsum('bsd,dkc->bskc', normed, w_in, precision=precise))
    b_gate = triple[:, :, 0]
    c_gate = triple[:, :, 1]
    x_part = triple[:, :, 2]
    product = low(b_gate * x_part)
    padded = jnp.pad(product, ((0, 0), (2, 0), (0, 0)))
    convolved = conv_weight[0] * padded[:, 0:length] + conv_weight[1] * padded[:, 1:length + 1] + conv_weight[2] * padded[:, 2:length + 2]
    mixed_in = low(c_gate * convolved)
    hidden_res = low_back(tokens_f + jnp.einsum('bsc,cd->bsd', mixed_in, w_out, precision=precise))
    normed_two = low(hidden_res * normalize(hidden_res) * gain_ffn)
    gate_val = low_back(jnp.einsum('bsd,df->bsf', normed_two, w_gate, precision=precise))
    up_val = low_back(jnp.einsum('bsd,df->bsf', normed_two, w_up, precision=precise))
    activ = low(jax.nn.silu(gate_val) * up_val)
    return hidden_res + jnp.einsum('bsf,fd->bsd', activ, w_down, precision=precise)

def reference(tokens, gain_mix, w_in, conv_weight, w_out, gain_ffn, w_gate, w_up, w_down, cotangent, lengths):
    floats = (tokens.astype(jnp.float32), gain_mix, w_in.astype(jnp.float32), conv_weight, w_out.astype(jnp.float32), gain_ffn, w_gate.astype(jnp.float32), w_up.astype(jnp.float32), w_down.astype(jnp.float32))
    positions = jnp.arange(LEN, dtype=jnp.int32)
    valid = (positions[None, :] < lengths[:, None]).astype(jnp.float32)
    result, pullback = jax.vjp(forward, *floats)
    grads = pullback(cotangent.astype(jnp.float32) * valid[:, :, None])
    return (result.astype(jnp.bfloat16), grads[0].astype(jnp.bfloat16), grads[1], grads[2], grads[3], grads[4], grads[5], grads[6], grads[7], grads[8])
```

```python
import jax
import jax.numpy as jnp
import numpy as np
from jax import lax
from jax.experimental import pallas as pl
from jax.experimental.pallas import tpu as pltpu
from jax.sharding import PartitionSpec as P

epsilon = 1e-05
f32 = jnp.float32
bf16 = jnp.bfloat16

ROWS = 256
PIECE = 64
D = 2048
MiB = 1 << 20

FLIP = {"a": (1, 0, 3, 2), "b": (3, 2, 1, 0)}
CODE = {0: (0, 0), 1: (1, 0), 2: (1, 1), 3: (0, 1)}
PLACE = {bits: at for at, bits in CODE.items()}
ORDER = (
    (("xa", "xb", "ya", "yb"), ("ya", "yb", "xa", "xb")),
    (("xb", "xa", "yb", "ya"), ("yb", "ya", "xb", "xa")),
)


def seq_index(x, y, core):
    return (x * 4 + y) * 2 + core


def flipped(x, y, dim):
    ring = FLIP[dim[1]]
    return (ring[x], y) if dim[0] == "x" else (x, ring[y])


def stage_pairs(half, stage):
    pairs = []
    for x in range(4):
        for y in range(4):
            for core in range(2):
                to = flipped(x, y, ORDER[half][core][stage])
                pairs.append((seq_index(x, y, core), seq_index(*to, core)))
    return pairs


CORE_PAIRS = [(i, i ^ 1) for i in range(32)]


def block_table():
    table = np.zeros((32, 2, 16), np.int32)
    for x in range(4):
        for y in range(4):
            for core in range(2):
                for half in range(2):
                    for position in range(16):
                        bits = {"x": list(CODE[x]), "y": list(CODE[y])}
                        for stage, dim in enumerate(ORDER[half][core]):
                            if (position >> (3 - stage)) & 1:
                                bits[dim[0]]["ab".index(dim[1])] ^= 1
                        owner = PLACE[tuple(bits["x"])] * 4 + PLACE[tuple(bits["y"])]
                        table[seq_index(x, y, core), half, position] = owner
    return table


BLOCKS = block_table()


def cost(flops, moved):
    return pl.CostEstimate(flops=int(flops), bytes_accessed=int(moved), transcendentals=0)


def params(mib):
    return pltpu.CompilerParams(vmem_limit_bytes=mib * MiB)


def whole(shape):
    return pl.BlockSpec(shape, lambda *_: (0,) * len(shape))


def smem():
    return pl.BlockSpec(memory_space=pltpu.SMEM)


def shaped(shape, kind):
    return jax.ShapeDtypeStruct(shape, kind)


def matmul(left, right):
    return lax.dot_general(left, right, (((1,), (0,)), ((), ())), preferred_element_type=f32)


def matmul_t(left, right):
    return lax.dot_general(left, right, (((1,), (1,)), ((), ())), preferred_element_type=f32)


def normalize(values):
    return lax.rsqrt(jnp.mean(values * values, -1, keepdims=True) + epsilon)


def rotated(z, piece):
    return pl.multiple_of(lax.rem(z + piece, 4) * PIECE, PIECE)


def project_in(tokens, gain, w_in):
    cols = 256

    def body(tok, gain_ref, w, normed, b_out, c_out, v_out, q_out, tail):
        @pl.when(pl.program_id(0) == 0)
        def _():
            values = tok[...].astype(f32)
            normed[...] = (values * normalize(values) * gain_ref[...]).astype(bf16)

        left = normed[...]
        b = matmul(left, w[0])
        c_out[...] = matmul(left, w[1])
        v = matmul(left, w[2])
        b_out[...] = b
        v_out[...] = v
        q = (b * v).astype(bf16)
        q_out[...] = q
        last = q.astype(f32)
        tail[0] = last[120:128]
        tail[1] = last[248:256]

    part = pl.BlockSpec((ROWS, cols), lambda j: (0, j))
    return pl.pallas_call(
        body,
        grid=(512 // cols,),
        in_specs=[whole((ROWS, D)), whole((1, D)), pl.BlockSpec((3, D, cols), lambda j: (0, 0, j))],
        out_specs=[whole((ROWS, D)), part, part, part, part, pl.BlockSpec((2, 8, cols), lambda j: (0, 0, j))],
        out_shape=[
            shaped((ROWS, D), bf16),
            shaped((ROWS, 512), f32),
            shaped((ROWS, 512), f32),
            shaped((ROWS, 512), f32),
            shaped((ROWS, 512), bf16),
            shaped((2, 8, 512), f32),
        ],
        compiler_params=params(24),
        cost_estimate=cost(2 * ROWS * D * 1536, 10 * MiB),
        name="project_in",
    )(tokens, gain, w_in)


def project_out(place, q, carried, c_gate, conv_weight, w_out):
    def body(at, q_ref, carried_ref, c_ref, cw, w, conv_out, y_out, own, one, two, three, pad):
        z = at[0]
        for seq in range(2):
            rows = slice(seq * 128, seq * 128 + 128)
            pad[0:8] = carried_ref[seq]
            pad[8:136] = q_ref[rows].astype(f32)
            conv = cw[0:1] * pad[6:134] + cw[1:2] * pad[7:135] + cw[2:3] * pad[8:136]
            conv_out[rows] = conv
        for piece in range(4):
            start = rotated(z, piece)
            y_out[piece * PIECE : (piece + 1) * PIECE] = (
                c_ref[pl.ds(start, PIECE)] * conv_out[pl.ds(start, PIECE)]
            ).astype(bf16)
        for at_col in range(0, D, 512):
            cols = slice(at_col, at_col + 512)
            total = matmul(y_out[...], w[:, cols])
            own[:, cols] = total[0:64]
            one[:, cols] = total[64:128].astype(bf16)
            two[:, cols] = total[128:192].astype(bf16)
            three[:, cols] = total[192:256].astype(bf16)

    return pl.pallas_call(
        body,
        in_specs=[smem()] + [pl.BlockSpec(memory_space=pltpu.VMEM)] * 5,
        out_specs=[pl.BlockSpec(memory_space=pltpu.VMEM)] * 6,
        out_shape=[
            shaped((ROWS, 512), f32),
            shaped((ROWS, 512), bf16),
            shaped((PIECE, D), f32),
            shaped((PIECE, D), bf16),
            shaped((PIECE, D), bf16),
            shaped((PIECE, D), bf16),
        ],
        scratch_shapes=[pltpu.VMEM((136, 512), f32)],
        compiler_params=params(16),
        cost_estimate=cost(2 * ROWS * D * 512, 5 * MiB),
        name="project_out",
    )(place, q, carried, c_gate, conv_weight, w_out)


def residual_norm(place, own, received, tokens, gain):
    def body(at, own_ref, r1, r2, r3, tok, gain_ref, hidden, normed):
        values = (
            tok[...].astype(f32)
            + own_ref[...]
            + r1[...].astype(f32)
            + r2[...].astype(f32)
            + r3[...].astype(f32)
        )
        hidden[...] = values
        normed[...] = (values * normalize(values) * gain_ref[...]).astype(bf16)

    tall = pl.BlockSpec((PIECE, D), lambda i, at: (0, 0))
    return pl.pallas_call(
        body,
        grid_spec=pltpu.PrefetchScalarGridSpec(
            num_scalar_prefetch=1,
            grid=(1,),
            in_specs=[tall] * 4
            + [pl.BlockSpec((PIECE, D), lambda i, at: (at[0], 0)), pl.BlockSpec((1, D), lambda i, at: (0, 0))],
            out_specs=[tall, tall],
        ),
        out_shape=[shaped((PIECE, D), f32), shaped((PIECE, D), bf16)],
        compiler_params=params(16),
        cost_estimate=cost(PIECE * D * 10, 3 * MiB),
        name="residual_norm",
    )(place, own, *received, tokens, gain)


def mask_cotangent(place, lengths, cotangent):
    def body(at, len_ref, cot, out):
        z, position = at[0], at[1] * 128
        for piece in range(4):
            block = lax.rem(z + piece, 4)
            seq, half = block // 2, lax.rem(block, 2)
            first = position + half * PIECE
            rows = first + lax.broadcasted_iota(jnp.int32, (PIECE, D), 0)
            values = cot[pl.ds(rotated(z, piece), PIECE)].astype(f32)
            out[piece * PIECE : (piece + 1) * PIECE] = jnp.where(
                rows < len_ref[seq], values, 0.0
            ).astype(bf16)

    return pl.pallas_call(
        body,
        in_specs=[smem(), smem(), pl.BlockSpec(memory_space=pltpu.VMEM)],
        out_specs=pl.BlockSpec(memory_space=pltpu.VMEM),
        out_shape=shaped((ROWS, D), bf16),
        compiler_params=params(16),
        cost_estimate=cost(ROWS * D * 4, 2 * MiB),
        name="mask_cotangent",
    )(place, lengths, cotangent)


def turn(place, parts):
    count = len(parts)
    tall = ROWS // count

    def body(at, *refs):
        parts_ref, (mine, other, flat) = refs[:count], refs[count:]
        core = at[2]
        for piece in range(count):
            flat[:, piece * tall : (piece + 1) * tall] = parts_ref[piece][...].astype(f32).T.astype(bf16)
        for block in range(16):
            rows = slice(block * 64, block * 64 + 64)
            mine[rows] = flat[pl.ds(pl.multiple_of(block * 128 + core * 64, 64), 64)]
            other[rows] = flat[pl.ds(pl.multiple_of(block * 128 + (1 - core) * 64, 64), 64)]

    return pl.pallas_call(
        body,
        in_specs=[smem()] + [pl.BlockSpec(memory_space=pltpu.VMEM)] * count,
        out_specs=[pl.BlockSpec(memory_space=pltpu.VMEM)] * 2,
        out_shape=[shaped((1024, ROWS), bf16)] * 2,
        scratch_shapes=[pltpu.VMEM((D, ROWS), bf16)],
        compiler_params=params(16),
        cost_estimate=cost(ROWS * D * 8, 2 * MiB),
        name="turn",
    )(place, *parts)


def activation_grad(grad_low, w_down):
    cols = 512

    def body(grad, w, out):
        out[...] = matmul_t(grad[...], w[...])

    return pl.pallas_call(
        body,
        grid=(2048 // cols,),
        in_specs=[whole((ROWS, D)), pl.BlockSpec((cols, D), lambda j: (j, 0))],
        out_specs=pl.BlockSpec((ROWS, cols), lambda j: (0, j)),
        out_shape=shaped((ROWS, 2048), f32),
        compiler_params=params(16),
        cost_estimate=cost(2 * ROWS * D * 2048, 11 * MiB),
        name="activation_grad",
    )(grad_low, w_down)


def feed_forward(pieces, w_gate, w_up, grad_act):
    cols = 256
    steps = 2048 // cols

    def body(n0, n1, n2, n3, wg, wu, ga, act, dgate, dup, own, one, two, three, normed, total):
        step = pl.program_id(0)

        @pl.when(step == 0)
        def _():
            for piece, ref in enumerate((n0, n1, n2, n3)):
                normed[piece * PIECE : (piece + 1) * PIECE] = ref[...]

        left = normed[...]
        gate = matmul(left, wg[...])
        up = matmul(left, wu[...])
        sigma = jax.nn.sigmoid(gate)
        swish = gate * sigma
        grad = ga[...]
        act[...] = (swish * up).astype(bf16)
        low_gate = (grad * up * sigma * (1.0 + gate * (1.0 - sigma))).astype(bf16)
        low_up = (grad * swish).astype(bf16)
        dgate[...] = low_gate
        dup[...] = low_up
        part = matmul_t(low_gate, wg[...]) + matmul_t(low_up, wu[...])

        @pl.when(step == 0)
        def _():
            total[...] = part

        @pl.when(step > 0)
        def _():
            total[...] += part

        @pl.when(step == steps - 1)
        def _():
            own[...] = total[0:64]
            one[...] = total[64:128].astype(bf16)
            two[...] = total[128:192].astype(bf16)
            three[...] = total[192:256].astype(bf16)

    tall = whole((PIECE, D))
    wide = pl.BlockSpec((D, cols), lambda j: (0, j))
    part = pl.BlockSpec((ROWS, cols), lambda j: (0, j))
    return pl.pallas_call(
        body,
        grid=(steps,),
        in_specs=[tall] * 4 + [wide, wide, part],
        out_specs=[part] * 3 + [tall] * 4,
        out_shape=[shaped((ROWS, 2048), bf16)] * 3
        + [shaped((PIECE, D), f32)]
        + [shaped((PIECE, D), bf16)] * 3,
        scratch_shapes=[pltpu.VMEM((ROWS, D), bf16), pltpu.VMEM((ROWS, D), f32)],
        compiler_params=params(32),
        cost_estimate=cost(8 * ROWS * D * 2048, 24 * MiB),
        name="feed_forward",
    )(*pieces, w_gate, w_up, grad_act)


def down(act, w_down):
    cols = 512

    def body(a, w, own, one, two, three):
        total = matmul(a[...], w[...])
        own[...] = total[0:64]
        one[...] = total[64:128].astype(bf16)
        two[...] = total[128:192].astype(bf16)
        three[...] = total[192:256].astype(bf16)

    part = pl.BlockSpec((PIECE, cols), lambda j: (0, j))
    return pl.pallas_call(
        body,
        grid=(D // cols,),
        in_specs=[whole((ROWS, 2048)), pl.BlockSpec((2048, cols), lambda j: (0, j))],
        out_specs=[part] * 4,
        out_shape=[shaped((PIECE, D), f32)] + [shaped((PIECE, D), bf16)] * 3,
        compiler_params=params(16),
        cost_estimate=cost(2 * ROWS * D * 2048, 11 * MiB),
        name="down",
    )(act, w_down)


def block_output(hidden, own, received):
    def body(h, own_ref, r1, r2, r3, out):
        out[...] = (
            h[...] + (own_ref[...] + r1[...].astype(f32) + r2[...].astype(f32) + r3[...].astype(f32))
        ).astype(bf16)

    return pl.pallas_call(
        body,
        in_specs=[pl.BlockSpec(memory_space=pltpu.VMEM)] * 5,
        out_specs=pl.BlockSpec(memory_space=pltpu.VMEM),
        out_shape=shaped((PIECE, D), bf16),
        compiler_params=params(16),
        cost_estimate=cost(PIECE * D * 5, 3 * MiB),
        name="block_output",
    )(hidden, own, *received)


def hidden_grad(own, received, hidden, gain, grad_low):
    def body(own_ref, r1, r2, r3, h, gain_ref, grad, out, gain_part):
        total = own_ref[...] + r1[...].astype(f32) + r2[...].astype(f32) + r3[...].astype(f32)
        values = h[...]
        rate = normalize(values)
        unit = values * rate
        gain_part[...] = jnp.sum(total * unit, axis=0, keepdims=True)
        scaled = total * gain_ref[...]
        inner = jnp.mean(scaled * unit, -1, keepdims=True)
        out[...] = (grad[...].astype(f32) + rate * (scaled - unit * inner)).astype(bf16)

    tall = whole((PIECE, D))
    return pl.pallas_call(
        body,
        grid=(1,),
        in_specs=[tall] * 5 + [whole((1, D)), tall],
        out_specs=[tall, whole((1, D))],
        out_shape=[shaped((PIECE, D), bf16), shaped((1, D), f32)],
        compiler_params=params(16),
        cost_estimate=cost(PIECE * D * 20, 3 * MiB),
        name="hidden_grad",
    )(own, *received, hidden, gain, grad_low)


def mixed_grad(place, pieces, w_out, convolved, c_gate, q, carried):
    def body(at, h0, h1, h2, h3, w, conv, c_ref, q_ref, carried_ref, dconv, dc, head, taps, grad, pad):
        z = at[0]
        for piece, ref in enumerate((h0, h1, h2, h3)):
            grad[pl.ds(rotated(z, piece), PIECE)] = matmul_t(ref[...], w[...])
        mixed = grad[...]
        dc[...] = (mixed * conv[...]).astype(bf16)
        dconv[...] = mixed * c_ref[...]
        sums = []
        for seq in range(2):
            rows = slice(seq * 128, seq * 128 + 128)
            head[seq] = dconv[seq * 128 : seq * 128 + 8]
            pad[0:8] = carried_ref[seq]
            pad[8:136] = q_ref[rows].astype(f32)
            here = dconv[rows]
            sums.append([jnp.sum(here * pad[6 + tap : 134 + tap], axis=0, keepdims=True) for tap in range(3)])
        for tap in range(3):
            taps[tap : tap + 1] = sums[0][tap] + sums[1][tap]

    return pl.pallas_call(
        body,
        in_specs=[smem()] + [pl.BlockSpec(memory_space=pltpu.VMEM)] * 9,
        out_specs=[pl.BlockSpec(memory_space=pltpu.VMEM)] * 4,
        out_shape=[
            shaped((ROWS, 512), f32),
            shaped((ROWS, 512), bf16),
            shaped((2, 8, 512), f32),
            shaped((3, 512), f32),
        ],
        scratch_shapes=[pltpu.VMEM((ROWS, 512), f32), pltpu.VMEM((136, 512), f32)],
        compiler_params=params(16),
        cost_estimate=cost(2 * ROWS * D * 512, 5 * MiB),
        name="mixed_grad",
    )(place, *pieces, w_out, convolved, c_gate, q, carried)


def input_grad(place, dconv, returned, dc, b_gate, x_part, conv_weight, w_in, tokens):
    cols = 512

    def body(at, dk, ret, dc_ref, b, v, cw, w, tok, whole_tok, dp, own, one, two, three, gain_part, pad, total, rate):
        z = at[0]

        @pl.when(pl.program_id(0) == 0)
        def _():
            for seq in range(2):
                rows = slice(seq * 128, seq * 128 + 128)
                pad[0:128] = dk[rows]
                pad[128:136] = ret[seq]
                dq = cw[2:3] * pad[0:128] + cw[1:2] * pad[1:129] + cw[0:1] * pad[2:130]
                dp[rows, 0:512] = (dq * v[rows]).astype(bf16)
                dp[rows, 512:1024] = dc_ref[rows]
                dp[rows, 1024:1536] = (dq * b[rows]).astype(bf16)
            values = whole_tok[...].astype(f32)
            rate[...] = jnp.broadcast_to(normalize(values), (ROWS, 128))

        part = (
            matmul_t(dp[:, 0:512], w[0])
            + matmul_t(dp[:, 512:1024], w[1])
            + matmul_t(dp[:, 1024:1536], w[2])
        )
        unit = tok[...].astype(f32) * rate[:, 0:1]
        gain_part[...] = jnp.sum(part * unit, axis=0, keepdims=True)
        total[...] = part
        own[...] = total[pl.ds(rotated(z, 0), PIECE)]
        one[...] = total[pl.ds(rotated(z, 1), PIECE)].astype(bf16)
        two[...] = total[pl.ds(rotated(z, 2), PIECE)].astype(bf16)
        three[...] = total[pl.ds(rotated(z, 3), PIECE)].astype(bf16)

    part = pl.BlockSpec((PIECE, cols), lambda j: (0, j))
    return pl.pallas_call(
        body,
        grid=(D // cols,),
        in_specs=[
            smem(),
            whole((ROWS, 512)),
            whole((2, 8, 512)),
            whole((ROWS, 512)),
            whole((ROWS, 512)),
            whole((ROWS, 512)),
            whole((3, 512)),
            pl.BlockSpec((3, cols, 512), lambda j: (0, j, 0)),
            pl.BlockSpec((ROWS, cols), lambda j: (0, j)),
            whole((ROWS, D)),
        ],
        out_specs=[whole((ROWS, 1536))] + [part] * 4 + [pl.BlockSpec((1, cols), lambda j: (0, j))],
        out_shape=[
            shaped((ROWS, 1536), bf16),
            shaped((PIECE, D), f32),
            shaped((PIECE, D), bf16),
            shaped((PIECE, D), bf16),
            shaped((PIECE, D), bf16),
            shaped((1, D), f32),
        ],
        scratch_shapes=[
            pltpu.VMEM((136, 512), f32),
            pltpu.VMEM((ROWS, cols), f32),
            pltpu.VMEM((ROWS, 128), f32),
        ],
        compiler_params=params(24),
        cost_estimate=cost(2 * ROWS * D * 1536, 12 * MiB),
        name="input_grad",
    )(place, dconv, returned, dc, b_gate, x_part, conv_weight, w_in, tokens, tokens)


def token_grad(place, own, received, tokens, gain, grad_hidden):
    def body(at, own_ref, r1, r2, r3, tok, gain_ref, grad, out):
        total = own_ref[...] + r1[...].astype(f32) + r2[...].astype(f32) + r3[...].astype(f32)
        values = tok[...].astype(f32)
        rate = normalize(values)
        unit = values * rate
        scaled = total * gain_ref[...]
        inner = jnp.mean(scaled * unit, -1, keepdims=True)
        out[...] = (grad[...].astype(f32) + rate * (scaled - unit * inner)).astype(bf16)

    tall = pl.BlockSpec((PIECE, D), lambda i, at: (0, 0))
    return pl.pallas_call(
        body,
        grid_spec=pltpu.PrefetchScalarGridSpec(
            num_scalar_prefetch=1,
            grid=(1,),
            in_specs=[tall] * 4
            + [
                pl.BlockSpec((PIECE, D), lambda i, at: (at[0], 0)),
                pl.BlockSpec((1, D), lambda i, at: (0, 0)),
                tall,
            ],
            out_specs=tall,
        ),
        out_shape=shaped((PIECE, D), bf16),
        compiler_params=params(16),
        cost_estimate=cost(PIECE * D * 20, 3 * MiB),
        name="token_grad",
    )(place, own, *received, tokens, gain, grad_hidden)


def in_place(place, pieces):
    def body(at, p0, p1, p2, p3, out):
        for piece, ref in enumerate((p0, p1, p2, p3)):
            out[pl.ds(rotated(at[0], piece), PIECE)] = ref[...]

    return pl.pallas_call(
        body,
        in_specs=[smem()] + [pl.BlockSpec(memory_space=pltpu.VMEM)] * 4,
        out_specs=pl.BlockSpec(memory_space=pltpu.VMEM),
        out_shape=shaped((ROWS, D), bf16),
        compiler_params=params(16),
        cost_estimate=cost(ROWS * D, 2 * MiB),
        name="in_place",
    )(place, *pieces)


def weight_grad(blocks, half, parts, tile):
    tiles = sum(part[5] for part in parts)
    starts = np.cumsum([0] + [part[5] for part in parts])

    def body(order, *refs):
        count = len(parts)
        inputs, (keep, send), lefts = refs[: 4 * count], refs[4 * count : 4 * count + 2], refs[4 * count + 2 :]
        step = pl.program_id(0)
        for n in range(count):
            mine, other, right_mine, right_other = inputs[4 * n : 4 * n + 4]
            left = lefts[n]

            @pl.when(step == int(starts[n]))
            def _():
                for position in range(16):
                    start = pl.multiple_of(order[half * 16 + position] * 64, 64)
                    rows = slice(position * 64, position * 64 + 64)
                    left[rows, 0:256] = mine[pl.ds(start, 64)]
                    left[rows, 256:512] = other[pl.ds(start, 64)]

            @pl.when((step >= int(starts[n])) & (step < int(starts[n + 1])))
            def _():
                total = matmul(left[:, 0:256], right_mine[...]) + matmul(left[:, 256:512], right_other[...])
                keep[...] = total[0:512].astype(bf16)
                send[...] = total[512:1024].astype(bf16)

    specs, operands = [smem()], [blocks]
    for n, (mine, other, right_mine, right_other, first, count) in enumerate(parts):
        begin = int(starts[n])

        def column(j, first=first, count=count, begin=begin):
            return (0, first + jnp.clip(j - begin, 0, count - 1))

        right = pl.BlockSpec((ROWS, tile), column)
        specs += [whole((1024, ROWS)), whole((1024, ROWS)), right, right]
        operands += [mine, other, right_mine, right_other]
    out = pl.BlockSpec((512, tile), lambda j: (0, j))
    return pl.pallas_call(
        body,
        grid=(tiles,),
        in_specs=specs,
        out_specs=[out, out],
        out_shape=[shaped((512, tiles * tile), bf16)] * 2,
        scratch_shapes=[pltpu.VMEM((1024, 512), bf16)] * len(parts),
        compiler_params=params(24),
        cost_estimate=cost(2 * 1024 * 512 * tiles * tile, (2 + 3 * tiles * tile / 1024) * MiB),
        name="weight_grad",
    )(*operands)


def to_next(value, axis, steps):
    count = lax.axis_size(axis)
    first, last = (max(0, -steps), min(count, count - steps))
    return lax.ppermute(value, axis, [(source, source + steps) for source in range(first, last)])


def around(value, steps):
    return lax.ppermute(value, "tp", [(source, (source + steps) % 4) for source in range(4)])


def scattered(pieces):
    return [around(piece, steps) for piece, steps in zip(pieces, (1, 2, 3))]


def gathered(shard):
    return [shard, around(shard, 3), around(shard, 2), around(shard, 1)]


def other_core(value):
    return lax.ppermute(value, "seq", CORE_PAIRS)


def reduce_half(half, keep, send):
    for stage in range(4):
        came = lax.ppermute(send, "seq", stage_pairs(half, stage))
        if stage == 3:
            return keep.astype(f32) + came.astype(f32)
        middle = keep.shape[0] // 2
        send = (keep[middle:].astype(f32) + came[middle:].astype(f32)).astype(bf16)
        keep = (keep[:middle].astype(f32) + came[:middle].astype(f32)).astype(bf16)


def sum_over(value, axis, groups):
    for pairs in groups:
        value = value + lax.ppermute(value, axis, pairs)
    return value


SEQ_GROUPS = [stage_pairs(0, stage) for stage in range(4)] + [CORE_PAIRS]
TP_GROUPS = [[(at, FLIP[flip][at]) for at in range(4)] for flip in "ab"]


def per_device(
    tokens, gain_mix, w_in, conv_weight, w_out, gain_ffn, w_gate, w_up, w_down, cotangent, lengths
):
    seq, z = lax.axis_index("seq"), lax.axis_index("tp")
    place = jnp.stack([z, seq, lax.rem(seq, 2), seq // 2]).astype(jnp.int32)
    blocks = jnp.asarray(BLOCKS.reshape(32, 32))[seq]
    tokens = tokens.reshape(ROWS, D)
    cotangent = cotangent.reshape(ROWS, D)
    w_in = jnp.transpose(w_in, (1, 0, 2))
    gain_mix = gain_mix.reshape(1, D)
    gain_ffn = gain_ffn.reshape(1, D)

    normed, b_gate, c_gate, x_part, q, tail = project_in(tokens, gain_mix, w_in)
    carried = to_next(tail, "seq", 1)
    grad_low = mask_cotangent(place, lengths, cotangent)
    convolved, mixed, own, *pieces = project_out(place, q, carried, c_gate, conv_weight, w_out)
    received = scattered(pieces)
    grad_act = activation_grad(grad_low, w_down)
    hidden, shard = residual_norm(place, own, received, tokens, gain_ffn)
    normed_two = gathered(shard)

    act, dgate, dup, own, *pieces = feed_forward(normed_two, w_gate, w_up, grad_act)
    received = scattered(pieces)

    grad_turned = turn(place, [grad_low])
    two_turned = turn(place, normed_two)
    act_other = other_core(act)
    dgate_other = other_core(dgate)
    dup_other = other_core(dup)
    grad_turned_other = other_core(grad_turned[1])
    two_turned_other = other_core(two_turned[1])

    down_halves = [
        reduce_half(
            half,
            *weight_grad(
                blocks, half, [(grad_turned[0], grad_turned_other, act, act_other, 2 * half, 2)], 512
            ),
        )
        for half in range(2)
    ]
    gate_half = reduce_half(
        0, *weight_grad(blocks, 0, [(two_turned[0], two_turned_other, dgate, dgate_other, 0, 4)], 512)
    )
    up_half = reduce_half(
        1, *weight_grad(blocks, 1, [(two_turned[0], two_turned_other, dup, dup_other, 0, 4)], 512)
    )

    own_out, *pieces_out = down(act, w_down)
    out_shard = block_output(hidden, own_out, scattered(pieces_out))
    output = in_place(place, gathered(out_shard))

    hidden_low, gain_ffn_part = hidden_grad(own, received, hidden, gain_ffn, grad_low)
    hidden_pieces = gathered(hidden_low)
    dconv, dc, head, conv_part = mixed_grad(place, hidden_pieces, w_out, convolved, c_gate, q, carried)
    returned = to_next(head, "seq", -1)
    dp, own, *pieces, gain_mix_part = input_grad(
        place, dconv, returned, dc, b_gate, x_part, conv_weight, w_in, tokens
    )
    received = scattered(pieces)
    token_shard = token_grad(place, own, received, tokens, gain_mix, hidden_low)
    grad_tokens = in_place(place, gathered(token_shard))

    one_turned = turn(place, [normed])
    hidden_turned = turn(place, hidden_pieces)
    one_turned_other = other_core(one_turned[1])
    hidden_turned_other = other_core(hidden_turned[1])
    mixed_other = other_core(mixed)
    dp_other = other_core(dp)
    mixer_halves = [
        reduce_half(
            half,
            *weight_grad(
                blocks,
                half,
                [
                    (one_turned[0], one_turned_other, dp, dp_other, 3 * half, 3),
                    (hidden_turned[0], hidden_turned_other, mixed, mixed_other, half, 1),
                ],
                256,
            ),
        )
        for half in range(2)
    ]

    conv_sum = sum_over(conv_part, "seq", SEQ_GROUPS)
    gains = jnp.concatenate([gain_mix_part, gain_ffn_part], axis=0)
    gains = sum_over(sum_over(gains, "seq", SEQ_GROUPS), "tp", TP_GROUPS)

    grad_in = jnp.concatenate([mixer_halves[0][:, :768], mixer_halves[1][:, :768]], axis=1)
    grad_out = jnp.concatenate([mixer_halves[0][:, 768:], mixer_halves[1][:, 768:]], axis=1)
    grad_down = jnp.concatenate(down_halves, axis=1)
    return (
        output.reshape(2, 128, D),
        grad_tokens.reshape(2, 128, D),
        gains[0],
        grad_in.reshape(64, 3, 512),
        conv_sum,
        grad_out.T,
        gains[1],
        gate_half,
        up_half,
        grad_down.T,
    )


def solution(mesh):
    placed = (
        P(None, "seq", None),
        P(),
        P(None, None, "tp"),
        P(None, "tp"),
        P("tp", None),
        P(),
        P(None, "tp"),
        P(None, "tp"),
        P("tp", None),
        P(None, "seq", None),
        P(),
    )
    return jax.shard_map(
        per_device,
        mesh=mesh,
        in_specs=placed,
        out_specs=(
            P(None, "seq", None),
            P(None, "seq", None),
            P(),
            P("seq", None, "tp"),
            P(None, "tp"),
            P("tp", "seq"),
            P(),
            P("seq", "tp"),
            P("seq", "tp"),
            P("tp", "seq"),
        ),
        check_vma=False,
    )
```

```python
import jax
import jax.numpy as jnp
import numpy as np
from jax import lax
from jax.experimental import pallas as pl
from jax.experimental.pallas import tpu as pltpu
from jax.sharding import PartitionSpec as P

epsilon = 1e-05
f32 = jnp.float32
bf16 = jnp.bfloat16

ROWS = 256
PIECE = 64
D = 2048
MiB = 1 << 20

FLIP = {"a": (1, 0, 3, 2), "b": (3, 2, 1, 0)}
CODE = {0: (0, 0), 1: (1, 0), 2: (1, 1), 3: (0, 1)}
PLACE = {bits: at for at, bits in CODE.items()}
ORDER = (
    (("xa", "xb", "ya", "yb"), ("ya", "yb", "xa", "xb")),
    (("xb", "xa", "yb", "ya"), ("yb", "ya", "xb", "xa")),
)


def seq_index(x, y, core):
    return (x * 4 + y) * 2 + core


def flipped(x, y, dim):
    ring = FLIP[dim[1]]
    return (ring[x], y) if dim[0] == "x" else (x, ring[y])


def stage_pairs(half, stage):
    pairs = []
    for x in range(4):
        for y in range(4):
            for core in range(2):
                to = flipped(x, y, ORDER[half][core][stage])
                pairs.append((seq_index(x, y, core), seq_index(*to, core)))
    return pairs


CORE_PAIRS = [(i, i ^ 1) for i in range(32)]


def block_table():
    table = np.zeros((32, 2, 16), np.int32)
    for x in range(4):
        for y in range(4):
            for core in range(2):
                for half in range(2):
                    for position in range(16):
                        bits = {"x": list(CODE[x]), "y": list(CODE[y])}
                        for stage, dim in enumerate(ORDER[half][core]):
                            if (position >> (3 - stage)) & 1:
                                bits[dim[0]]["ab".index(dim[1])] ^= 1
                        owner = PLACE[tuple(bits["x"])] * 4 + PLACE[tuple(bits["y"])]
                        table[seq_index(x, y, core), half, position] = owner
    return table


BLOCKS = block_table()


FULL = pl.BlockSpec(memory_space=pltpu.VMEM)
FAR = pl.BlockSpec(memory_space=pl.ANY)
NUMBERS = pl.BlockSpec(memory_space=pltpu.SMEM)


class Far:
    def __init__(self, array):
        self.array = array


class Free:
    def __init__(self, array):
        self.array = array


def size(shape, kind):
    return int(np.prod(shape)) * jnp.dtype(kind).itemsize


def call(body, name, ins, outs, numbers=(), scratch=(), after=(), more=4, weight=1):
    room = more * MiB
    operands, specs = list(numbers), [NUMBERS] * len(numbers)
    for array in ins:
        if isinstance(array, Far):
            operands.append(pltpu.with_memory_space_constraint(array.array, pltpu.HBM))
            specs.append(FAR)
        else:
            operands.append(pltpu.with_memory_space_constraint(array, pltpu.VMEM))
            specs.append(FULL)
    count = len(operands)
    shapes = []
    for out in outs:
        if isinstance(out, Free):
            room += size(*out.array)
            shapes.append(jax.ShapeDtypeStruct(*out.array))
        else:
            shapes.append(pltpu.VMEM(*out))
    for kept in scratch:
        if kept.memory_space == pltpu.VMEM:
            room += size(kept.inner_aval.shape, kept.inner_aval.dtype)

    def run(*refs):
        body(*refs[:count], *refs[count + len(after) :])

    return pl.pallas_call(
        run,
        in_specs=specs + [FAR] * len(after),
        out_specs=[FULL] * len(outs),
        out_shape=shapes,
        scratch_shapes=list(scratch),
        compiler_params=pltpu.CompilerParams(vmem_limit_bytes=int(room)),
        cost_estimate=pl.CostEstimate(flops=weight, bytes_accessed=1, transcendentals=0),
        name=name,
    )(*operands, *after)


def matmul(left, right):
    return lax.dot_general(left, right, (((1,), (0,)), ((), ())), preferred_element_type=f32)


def matmul_t(left, right):
    return lax.dot_general(left, right, (((1,), (1,)), ((), ())), preferred_element_type=f32)


def normalize(values):
    return lax.rsqrt(jnp.mean(values * values, -1, keepdims=True) + epsilon)


def spans(total, each):
    return [slice(at, at + each) for at in range(0, total, each)]


def rotated(z, piece):
    return pl.multiple_of(lax.rem(z + piece, 4) * PIECE, PIECE)


PIECE_OUTS = [((PIECE, D), f32)] + [((PIECE, D), bf16)] * 3


def cut(total, own, one, two, three, cols=slice(None)):
    own[:, cols] = total[0:64]
    one[:, cols] = total[64:128].astype(bf16)
    two[:, cols] = total[128:192].astype(bf16)
    three[:, cols] = total[192:256].astype(bf16)


def added(own, r1, r2, r3):
    return own + (r1.astype(f32) + r2.astype(f32) + r3.astype(f32))


def release(name, arrays, after):
    count = len(arrays)
    return pl.pallas_call(
        lambda *refs: None,
        in_specs=[FAR] * (count + len(after)),
        out_specs=[FAR] * count,
        out_shape=[jax.ShapeDtypeStruct(array.shape, array.dtype) for array in arrays],
        input_output_aliases={n: n for n in range(count)},
        compiler_params=pltpu.CompilerParams(vmem_limit_bytes=MiB),
        cost_estimate=pl.CostEstimate(flops=1, bytes_accessed=1, transcendentals=0),
        name=name,
    )(*arrays, *after)


LONG = 4 * 10**10


class Stream:
    def __init__(self, copies, depth=3):
        self.copies, self.started = copies, 0
        for _ in range(depth):
            self.more()

    def more(self):
        if self.started < len(self.copies):
            self.copies[self.started].start()
            self.started += 1

    def wait(self, n):
        self.copies[n].wait()
        self.more()


SUMS = (16, 512)


def pack(to, row, sums):
    high = sums.astype(bf16)
    to[row : row + 16, 0:512] = high
    to[row : row + 16, 512:1024] = (sums - high.astype(f32)).astype(bf16)


def unpack(came, row):
    return came[row : row + 16, 0:512].astype(f32) + came[row : row + 16, 512:1024].astype(f32)


TABLE = 4


def project_in(place, tokens, gain_mix, gain_ffn, conv_weight, w_in):
    order = (0, 2, 1)

    def body(at_place, tok_far, mix_far, ffn_far, conv_far, w_far, tok, mix, ffn, conv, normed, b_out, c_out, v_out, q_out, tail, w, sems):
        small = [
            pltpu.make_async_copy(far, near, sems.at[n])
            for n, (far, near) in enumerate(((tok_far, tok), (mix_far, mix), (ffn_far, ffn), (conv_far, conv)))
        ]
        for copy in small:
            copy.start()
        copies = [pltpu.make_async_copy(w_far.at[part], w.at[part], sems.at[4 + part]) for part in order]
        stream = Stream(copies)
        for copy in small:
            copy.wait()
        values = tok[...].astype(f32)
        normed[...] = (values * normalize(values) * mix[...]).astype(bf16)
        for n, part in enumerate(order):
            stream.wait(n)
            (b_out, c_out, v_out)[part][...] = matmul(normed[...], w[part])
            if part == 2:
                q = (b_out[...] * v_out[...]).astype(bf16)
                q_out[...] = q
                tail[0] = q[112:128].astype(f32)[8:16]
                tail[1] = q[240:256].astype(f32)[8:16]

    return call(
        body,
        "project_in",
        [Far(tokens), Far(gain_mix), Far(gain_ffn), Far(conv_weight), Far(w_in)],
        [
            ((ROWS, D), bf16),
            ((1, D), f32),
            ((1, D), f32),
            ((3, 512), f32),
            ((ROWS, D), bf16),
            ((ROWS, 512), f32),
            ((ROWS, 512), f32),
            ((ROWS, 512), f32),
            ((ROWS, 512), bf16),
            ((2, 8, 512), f32),
        ],
        numbers=[place],
        scratch=[pltpu.VMEM((3, D, 512), bf16), pltpu.SemaphoreType.DMA((7,))],
    )


def turn_into(core, flat, mine, other, base=0):
    for block in range(16):
        rows = slice(block * 64, block * 64 + 64)
        mine[rows] = flat[pl.ds(pl.multiple_of(block * 128 + core * 64, 64), 64)]
        other[base + block * 64 : base + block * 64 + 64] = flat[
            pl.ds(pl.multiple_of(block * 128 + (1 - core) * 64, 64), 64)
        ]


def prepare(place, lengths, cotangent, w_out, normed):
    def body(at, len_ref, cot_far, w_far, one, out, w, grad_mine, one_mine, other, cot, flat, sems):
        z, position, core = at[0], at[1] * 128, at[2]
        copies = [pltpu.make_async_copy(cot_far, cot, sems.at[0]), pltpu.make_async_copy(w_far, w, sems.at[1])]
        for copy in copies:
            copy.start()
        flat[...] = one[...].T
        turn_into(core, flat, one_mine, other, 1024)
        copies[0].wait()
        for piece in range(4):
            block = lax.rem(z + piece, 4)
            seq, half = block // 2, lax.rem(block, 2)
            first = position + half * PIECE
            rows = first + lax.broadcasted_iota(jnp.int32, (PIECE, D), 0)
            values = cot[pl.ds(rotated(z, piece), PIECE)].astype(f32)
            out[piece * PIECE : (piece + 1) * PIECE] = jnp.where(rows < len_ref[seq], values, 0.0).astype(bf16)
        flat[...] = out[...].T
        turn_into(core, flat, grad_mine, other, 0)
        copies[1].wait()

    return call(
        body,
        "prepare",
        [Far(cotangent), Far(w_out), normed],
        [
            ((ROWS, D), bf16),
            ((512, D), bf16),
            ((1024, ROWS), bf16),
            ((1024, ROWS), bf16),
            ((2048, ROWS), bf16),
        ],
        numbers=[place, lengths],
        scratch=[pltpu.VMEM((ROWS, D), bf16), pltpu.VMEM((D, ROWS), bf16), pltpu.SemaphoreType.DMA((2,))],
    )


def project_out(place, q, carried, c_gate, conv_weight, w_out, after):
    def body(at, q_ref, carried_ref, c_ref, cw, w, conv_out, y_out, own, one, two, three, pad):
        z = at[0]
        for seq in range(2):
            rows = slice(seq * 128, seq * 128 + 128)
            pad[0:8] = carried_ref[seq]
            pad[8:136] = q_ref[rows].astype(f32)
            conv_out[rows] = cw[0:1] * pad[6:134] + cw[1:2] * pad[7:135] + cw[2:3] * pad[8:136]
        for piece in range(4):
            start = rotated(z, piece)
            y_out[piece * PIECE : (piece + 1) * PIECE] = (
                c_ref[pl.ds(start, PIECE)] * conv_out[pl.ds(start, PIECE)]
            ).astype(bf16)
        for cols in spans(D, 512):
            cut(matmul(y_out[...], w[:, cols]), own, one, two, three, cols)

    return call(
        body,
        "project_out",
        [q, carried, c_gate, conv_weight, w_out],
        [((ROWS, 512), f32), ((ROWS, 512), bf16)] + PIECE_OUTS,
        numbers=[place],
        scratch=[pltpu.VMEM((136, 512), f32)],
        after=after,
    )


def activation_grad(grad_low, w_down):
    def body(grad, w_far, out, w, sems):
        stream = Stream(
            [
                pltpu.make_async_copy(w_far.at[rows], w.at[rows], sems.at[n])
                for n, rows in enumerate(spans(2048, 512))
            ]
        )
        for n, rows in enumerate(spans(2048, 512)):
            stream.wait(n)
            out[:, rows] = matmul_t(grad[...], w[rows])

    return call(
        body,
        "activation_grad",
        [grad_low, Far(w_down)],
        [((ROWS, 2048), f32)],
        scratch=[pltpu.VMEM((2048, D), bf16), pltpu.SemaphoreType.DMA((4,))],
    )[0]


def residual_norm(place, own, received, tokens, gain, after):
    def body(at, own_ref, r1, r2, r3, tok, gain_ref, hidden, normed):
        values = tok[pl.ds(rotated(at[0], 0), PIECE)].astype(f32) + added(own_ref[...], r1[...], r2[...], r3[...])
        hidden[...] = values
        normed[...] = (values * normalize(values) * gain_ref[...]).astype(bf16)

    return call(
        body,
        "residual_norm",
        [own, *received, tokens, gain],
        [((PIECE, D), f32), ((PIECE, D), bf16)],
        numbers=[place],
        after=after,
    )


def bring(name, weights, after=()):
    count = len(weights)

    def body(*refs):
        copies = [pltpu.make_async_copy(refs[n], refs[count + n], refs[-1].at[n]) for n in range(count)]
        for copy in copies:
            copy.start()
        for copy in copies:
            copy.wait()

    return call(
        body,
        name,
        [Far(weight) for weight in weights],
        [(weight.shape, weight.dtype) for weight in weights],
        scratch=[pltpu.SemaphoreType.DMA((count,))],
        after=after,
        more=1,
    )


def feed_forward(place, pieces, w_gate, w_up, grad_act, mixed):
    def body(at, n0, n1, n2, n3, gates, ups, ga, mix, mid, mine, other, normed, flat):
        for piece, ref in enumerate((n0, n1, n2, n3)):
            normed[piece * PIECE : (piece + 1) * PIECE] = ref[...]
        mid[:, 6144:6656] = mix[...]
        flat[...] = normed[...].T
        turn_into(at[2], flat, mine, other)
        for cols in spans(2048, 256):
            gate = matmul(normed[...], gates[:, cols])
            up = matmul(normed[...], ups[:, cols])
            sigma = jax.nn.sigmoid(gate)
            swish = gate * sigma
            grad = ga[:, cols]
            first = cols.start
            mid[:, first : first + 256] = (swish * up).astype(bf16)
            mid[:, 2048 + first : 2304 + first] = (grad * up * sigma * (1.0 + gate * (1.0 - sigma))).astype(bf16)
            mid[:, 4096 + first : 4352 + first] = (grad * swish).astype(bf16)

    return call(
        body,
        "feed_forward",
        [*pieces, w_gate, w_up, grad_act, mixed],
        [((ROWS, 6656), bf16), ((1024, ROWS), bf16), ((1024, ROWS), bf16)],
        numbers=[place],
        scratch=[pltpu.VMEM((ROWS, D), bf16), pltpu.VMEM((D, ROWS), bf16)],
    )


def feed_back(mid, w_gate, w_up):
    def body(mid_ref, gates, ups, own, one, two, three):
        for rows in spans(D, 256):
            total = matmul_t(mid_ref[:, 2048:4096], gates[rows]) + matmul_t(mid_ref[:, 4096:6144], ups[rows])
            cut(total, own, one, two, three, rows)

    return call(body, "feed_back", [mid, w_gate, w_up], PIECE_OUTS)


def down(mid, w_down, after=()):
    def body(mid_ref, w_far, own, one, two, three, w, sems):
        stream = Stream(
            [
                pltpu.make_async_copy(w_far.at[:, cols], w.at[:, cols], sems.at[n])
                for n, cols in enumerate(spans(D, 512))
            ]
        )
        for n, cols in enumerate(spans(D, 512)):
            stream.wait(n)
            cut(matmul(mid_ref[:, 0:2048], w[:, cols]), own, one, two, three, cols)

    return call(
        body,
        "down",
        [mid, Far(w_down)],
        PIECE_OUTS,
        scratch=[pltpu.VMEM((2048, D), bf16), pltpu.SemaphoreType.DMA((4,))],
        after=after,
    )


def hidden_grad(own, received, hidden, gain, grad_low, after):
    def body(own_ref, r1, r2, r3, h, gain_ref, grad, out, gain_part):
        total = added(own_ref[...], r1[...], r2[...], r3[...])
        values = h[...]
        rate = normalize(values)
        unit = values * rate
        gain_part[...] = jnp.sum(total * unit, axis=0, keepdims=True)
        scaled = total * gain_ref[...]
        inner = jnp.mean(scaled * unit, -1, keepdims=True)
        out[...] = (grad[0:PIECE].astype(f32) + rate * (scaled - unit * inner)).astype(bf16)

    return call(
        body,
        "hidden_grad",
        [own, *received, hidden, gain, grad_low],
        [((PIECE, D), bf16), ((1, D), f32)],
        after=after,
        weight=LONG,
    )


def mixed_grad(place, pieces, w_out, convolved, c_gate, q, carried, after):
    def body(at, h0, h1, h2, h3, w, conv, c_ref, q_ref, carried_ref, dconv, dc, head, taps, mine, other, hidden, tall, pad, flat):
        z = at[0]
        for piece, ref in enumerate((h0, h1, h2, h3)):
            hidden[pl.ds(rotated(z, piece), PIECE)] = ref[...]
            tall[piece * PIECE : (piece + 1) * PIECE] = ref[...]
        for cols in spans(512, 256):
            mixed = matmul_t(hidden[...], w[cols])
            dc[:, cols] = (mixed * conv[:, cols]).astype(bf16)
            dconv[:, cols] = mixed * c_ref[:, cols]
        flat[...] = tall[...].T
        turn_into(at[2], flat, mine, other)
        sums = []
        for seq in range(2):
            rows = slice(seq * 128, seq * 128 + 128)
            head[seq] = dconv[seq * 128 : seq * 128 + 8]
            pad[0:8] = carried_ref[seq]
            pad[8:136] = q_ref[rows].astype(f32)
            here = dconv[rows]
            sums.append([jnp.sum(here * pad[6 + tap : 134 + tap], axis=0, keepdims=True) for tap in range(3)])
        for tap in range(3):
            taps[tap : tap + 1] = sums[0][tap] + sums[1][tap]

    return call(
        body,
        "mixed_grad",
        [*pieces, w_out, convolved, c_gate, q, carried],
        [
            ((ROWS, 512), f32),
            ((ROWS, 512), bf16),
            ((2, 8, 512), f32),
            ((3, 512), f32),
            ((1024, ROWS), bf16),
            ((1024, ROWS), bf16),
        ],
        numbers=[place],
        scratch=[
            pltpu.VMEM((ROWS, D), bf16),
            pltpu.VMEM((ROWS, D), bf16),
            pltpu.VMEM((136, 512), f32),
            pltpu.VMEM((D, ROWS), bf16),
        ],
        after=after,
    )


def input_grad(place, dconv, returned, dc, b_gate, x_part, conv_weight, w_in, tokens, out_parts, gain_part, taps, after):
    def body(at, dk, ret, dc_ref, b, v, cw, w, tok, oo, o1, o2, o3, gains, taps_ref, dp, own, one, two, three, sums, pad, total):
        z = at[0]
        for seq in range(2):
            rows = slice(seq * 128, seq * 128 + 128)
            pad[0:128] = dk[rows]
            pad[128:136] = ret[seq]
            dq = cw[2:3] * pad[0:128] + cw[1:2] * pad[1:129] + cw[0:1] * pad[2:130]
            dp[rows, 0:512] = (dq * v[rows]).astype(bf16)
            dp[rows, 512:1024] = dc_ref[rows]
            dp[rows, 1024:1536] = (dq * b[rows]).astype(bf16)
        rate = normalize(tok[...].astype(f32))
        sums[...] = jnp.zeros(SUMS, f32)
        for cols in spans(D, 256):
            part = (
                matmul_t(dp[0:256, 0:512], w[0, cols])
                + matmul_t(dp[0:256, 512:1024], w[1, cols])
                + matmul_t(dp[0:256, 1024:1536], w[2, cols])
            )
            row, first = cols.start // 512, cols.start % 512
            sums[row : row + 1, first : first + 256] = jnp.sum(
                part * (tok[:, cols].astype(f32) * rate), axis=0, keepdims=True
            )
            total[...] = part
            own[0:PIECE, cols] = total[pl.ds(rotated(z, 0), PIECE)]
            one[0:PIECE, cols] = total[pl.ds(rotated(z, 1), PIECE)].astype(bf16)
            two[0:PIECE, cols] = total[pl.ds(rotated(z, 2), PIECE)].astype(bf16)
            three[0:PIECE, cols] = total[pl.ds(rotated(z, 3), PIECE)].astype(bf16)
        for part, ref in ((oo, own), (o1, one), (o2, two), (o3, three)):
            ref[PIECE:] = part[...]
        for row in range(4):
            sums[4 + row : 5 + row] = gains[:, row * 512 : row * 512 + 512]
        sums[8:11] = taps_ref[...]
        pack(dp, 256, sums[...])

    return call(
        body,
        "input_grad",
        [dconv, returned, dc, b_gate, x_part, conv_weight, w_in, tokens, *out_parts, gain_part, taps],
        [((ROWS + 16, 1536), bf16), ((2 * PIECE, D), f32)] + [((2 * PIECE, D), bf16)] * 3 + [(SUMS, f32)],
        numbers=[place],
        scratch=[pltpu.VMEM((136, 512), f32), pltpu.VMEM((ROWS, 256), f32)],
        after=after,
    )


def last_shards(place, own, received, tokens, gain, grad_hidden, hidden, after):
    def body(at, own_ref, r1, r2, r3, tok, gain_ref, grad, h, out):
        rows = slice(0, PIECE)
        total = added(own_ref[rows], r1[rows], r2[rows], r3[rows])
        values = tok[pl.ds(rotated(at[0], 0), PIECE)].astype(f32)
        rate = normalize(values)
        unit = values * rate
        scaled = total * gain_ref[...]
        inner = jnp.mean(scaled * unit, -1, keepdims=True)
        out[rows] = (grad[...].astype(f32) + rate * (scaled - unit * inner)).astype(bf16)
        rows = slice(PIECE, 2 * PIECE)
        out[rows] = (h[...] + added(own_ref[rows], r1[rows], r2[rows], r3[rows])).astype(bf16)

    return call(
        body,
        "last_shards",
        [own, *received, tokens, gain, grad_hidden, hidden],
        [((2 * PIECE, D), bf16)],
        numbers=[place],
        after=after,
        weight=LONG,
    )[0]


def in_place(place, pieces, after=()):
    def body(at, p0, p1, p2, p3, grad, out, done):
        for piece, ref in enumerate((p0, p1, p2, p3)):
            rows = pl.ds(rotated(at[0], piece), PIECE)
            grad[rows] = ref[0:PIECE]
            out[rows] = ref[PIECE:]
        done[...] = jnp.zeros((8, 128), f32)

    return call(body, "in_place", [*pieces], [Free(((ROWS, D), bf16))] * 2 + [((8, 128), f32)], numbers=[place], after=after, weight=LONG)


def weight_grad(place, name, width, plan, sums=None, after=()):
    flat = [part for half in plan for part in half]
    arrays = []
    for mine, other, _, right_mine, right_other, _, _ in flat:
        for array in (mine, other, right_mine, right_other):
            if not any(array is known for known in arrays):
                arrays.append(array)
    count = len(arrays) + (sums is not None)

    def body(order, *refs):
        def ref(array):
            return refs[[known is array for known in arrays].index(True)]

        outs = refs[count : count + 4]
        left, right = refs[-2:]
        if sums is not None:
            total = refs[count - 1][...] + unpack(ref(plan[0][0][4]), 256)
            refs[count + 4][...] = total
            pack(outs[1], 512, total)
        for half in range(2):
            keep, send = outs[2 * half : 2 * half + 2]
            to = 0
            for mine, other, base, right_mine, right_other, first, columns in plan[half]:
                mine, other, right_mine, right_other = map(ref, (mine, other, right_mine, right_other))
                for position in range(16):
                    start = order[TABLE + half * 16 + position] * 64
                    rows = slice(position * 64, position * 64 + 64)
                    left[rows, 0:256] = mine[pl.ds(pl.multiple_of(start, 64), 64)]
                    left[rows, 256:512] = other[pl.ds(pl.multiple_of(base + start, 64), 64)]
                for step, cols in enumerate(spans(columns, 256)):
                    at = slice(first + cols.start, first + cols.stop)
                    room = right.at[step % 2]
                    room[0:256] = right_mine[0:256, at]
                    room[256:512] = right_other[0:256, at]
                    to_cols = slice(to + cols.start, to + cols.stop)
                    total = matmul(left[...], room[...]).astype(bf16)
                    keep[:, to_cols] = total[0:512]
                    send[0:512, to_cols] = total[512:1024]
                to += columns

    shapes = [((512, width), bf16)] * 4
    if sums is not None:
        shapes = [shapes[0], ((528, width), bf16), *shapes[2:], (SUMS, f32)]
    keep0, send0, keep1, send1, *total = call(
        body,
        name,
        arrays + ([] if sums is None else [sums]),
        shapes,
        numbers=[place],
        scratch=[pltpu.VMEM((1024, 512), bf16), pltpu.VMEM((2, 512, 256), bf16)],
        after=after,
    )
    return [keep0, keep1], [send0, send1], *total


def halve(name, groups, sums=None, passed=(), after=()):
    rows = groups[0][0][0].shape[0]
    middle = rows // 2
    ins = [array for keeps, cames in groups for array in (*keeps, *cames)]
    width = sum(keeps[0].shape[1] for keeps, _ in groups)
    each = min(64, middle)
    count = len(ins) + (sums is not None)

    def body(*refs):
        keep, send = refs[count : count + 2], refs[count + 2 : count + 4]
        if sums is not None:
            total = refs[count - 1][...] + unpack(refs[4 * len(groups) - 2], rows)
            refs[count + 4][...] = total
            pack(send[0], middle, total)

        @pl.loop(0, middle // each)
        def _(step):
            low = pl.ds(pl.multiple_of(step * each, each), each)
            high = pl.ds(pl.multiple_of(middle + step * each, each), each)
            for half in range(2):
                to = 0
                for n in range(len(groups)):
                    k, c = (refs[4 * n + 2 * what + half] for what in range(2))
                    cols = slice(to, to + k.shape[1])
                    keep[half][low, cols] = k[low] + c[low]
                    send[half][low, cols] = k[high] + c[high]
                    to += k.shape[1]

    shapes = [((middle, width), bf16)] * 4
    if sums is not None:
        shapes = [*shapes[:2], ((middle + 16, width), bf16), shapes[3], (SUMS, f32)]
    o0, o1, s0, s1, *total = call(body, name, ins + ([] if sums is None else [sums]), shapes, after=after)
    return [o0, o1], [s0, s1], *total


def last_sums(sums, came):
    def body(own, c0, out):
        out[...] = own[...] + unpack(c0, 64)

    return call(body, "last_sums", [sums, came], [(SUMS, f32)])[0]


def finish(keeps, cames, after=()):
    def body(k0, k1, c0, c1, down_out, gate, up, grad_in, grad_out):
        for half, (k, c, pair) in enumerate(((k0, c0, gate), (k1, c1, up))):

            def total(first, count, k=k, c=c):
                cols = slice(first, first + count)
                return k[:, cols].astype(f32) + c[0:64, cols].astype(f32)

            down_out[:, half * 1024 : half * 1024 + 1024] = total(0, 1024)
            pair[...] = total(1024, 2048)
            if half == 0:
                grad_in[0] = total(3072, 512)
                grad_in[1, :, 0:256] = total(3584, 256)
            else:
                grad_in[1, :, 256:512] = total(3072, 256)
                grad_in[2] = total(3328, 512)
            grad_out[:, half * 256 : half * 256 + 256] = total(3840, 256)

    return call(
        body,
        "finish",
        [*keeps, *cames],
        [Free(((64, 2048), f32))] * 3 + [Free(((3, 64, 512), f32)), Free(((64, 512), f32))],
        after=after,
    )


def small_sums(own, received):
    def body(s0, s1, s2, s3, mix, ffn, conv):
        total = (s0[0:8] + s1[0:8]) + (s2[0:8] + s3[0:8])
        for row in range(4):
            mix[:, row * 512 : row * 512 + 512] = total[row : row + 1]
            ffn[:, row * 512 : row * 512 + 512] = total[4 + row : 5 + row]
        conv[...] = s0[8:11]

    return call(
        body,
        "small_sums",
        [own, *received],
        [Free(((1, D), f32)), Free(((1, D), f32)), Free(((3, 512), f32))],
    )


def to_next(value, axis, steps):
    count = lax.axis_size(axis)
    first, last = (max(0, -steps), min(count, count - steps))
    return lax.ppermute(value, axis, [(source, source + steps) for source in range(first, last)])


def around(value, steps):
    return lax.ppermute(value, "tp", [(source, (source + steps) % 4) for source in range(4)])


def scattered(pieces):
    return [around(piece, steps) for piece, steps in zip(pieces, (1, 2, 3))]


def gathered(shard):
    return [shard, around(shard, 3), around(shard, 2), around(shard, 1)]


def other_core(value):
    return lax.ppermute(value, "seq", CORE_PAIRS)


def exchange(stage, sends):
    return [lax.ppermute(send, "seq", stage_pairs(half, stage)) for half, send in enumerate(sends)]


def per_device(
    tokens, gain_mix, w_in, conv_weight, w_out, gain_ffn, w_gate, w_up, w_down, cotangent, lengths
):
    seq, z = lax.axis_index("seq"), lax.axis_index("tp")
    place = jnp.concatenate(
        [jnp.stack([z, seq, lax.rem(seq, 2), z]).astype(jnp.int32), jnp.asarray(BLOCKS.reshape(32, 32))[seq]]
    )
    tokens = tokens.reshape(ROWS, D)
    cotangent = cotangent.reshape(ROWS, D)
    w_in = jnp.transpose(w_in, (1, 0, 2))

    tokens, gain_mix, gain_ffn, conv_weight, normed, b_gate, c_gate, x_part, q, tail = project_in(
        place, tokens, gain_mix.reshape(1, D), gain_ffn.reshape(1, D), conv_weight, w_in
    )
    carried = to_next(tail, "seq", 1)
    grad_low, near_out, grad_turned, one_turned, turned = prepare(place, lengths, cotangent, w_out, normed)
    convolved, mixed, own, *pieces = project_out(
        place, q, carried, c_gate, conv_weight, near_out, after=[turned]
    )
    received = scattered(pieces)
    turned_other = other_core(turned)
    grad_act = activation_grad(grad_low, w_down)
    hidden, shard = residual_norm(place, own, received, tokens, gain_ffn, after=[grad_act, turned_other])
    normed_two = gathered(shard)
    gates, ups = bring("bring_ffn", [w_gate, w_up], after=[grad_act])

    mid, two_turned, two_sent = feed_forward(place, normed_two, gates, ups, grad_act, mixed)
    mid_other = other_core(mid)
    two_other = other_core(two_sent)
    own, *pieces = feed_back(mid, gates, ups)
    received = scattered(pieces)

    keep_a, send_a = weight_grad(
        place,
        "weight_grad_a",
        1024,
        [[(grad_turned, turned_other, 0, mid, mid_other, 1024 * half, 1024)] for half in range(2)],
        after=[own, two_other],
    )
    came_a = exchange(0, send_a)
    keep_b, send_b = weight_grad(
        place,
        "weight_grad_b",
        2048,
        [[(two_turned, two_other, 0, mid, mid_other, 2048 + 2048 * half, 2048)] for half in range(2)],
        after=[send_a[0]],
    )
    out_parts = down(mid, w_down, after=[send_b[0]])
    hidden_low, gain_part = hidden_grad(
        own, received, hidden, gain_ffn, grad_low, after=[send_b[0], out_parts[0]]
    )
    hidden_pieces = gathered(hidden_low)
    near_out, near_in = bring("bring_mixer", [w_out, w_in], after=[hidden_low])
    send_b = release("release", send_b, after=[*came_a, hidden_low])
    came_b = exchange(0, send_b)

    dconv, dc, head, taps, hidden_turned, hidden_sent = mixed_grad(
        place, hidden_pieces, near_out, convolved, c_gate, q, carried, after=[near_in]
    )
    returned = to_next(head, "seq", -1)
    hidden_other = other_core(hidden_sent)
    dp, own, *pieces, sums = input_grad(
        place, dconv, returned, dc, b_gate, x_part, conv_weight, near_in, tokens, out_parts, gain_part, taps,
        after=[hidden_other, *came_b],
    )
    received = scattered(pieces)
    dp_other = other_core(dp)
    keep_c, send_c, sums = weight_grad(
        place,
        "weight_grad_c",
        1024,
        [
            [
                (one_turned, turned_other, 1024, dp, dp_other, 768 * half, 768),
                (hidden_turned, hidden_other, 0, mid, mid_other, 6144 + 256 * half, 256),
            ]
            for half in range(2)
        ],
        sums=sums,
        after=[own],
    )
    came_c = exchange(0, send_c)
    shards = last_shards(place, own, received, tokens, gain_mix, hidden_low, hidden, after=[send_c[0]])
    keep, send, sums = halve(
        "halve_abc", [(keep_a, came_a), (keep_b, came_b), (keep_c, came_c)], sums=sums, after=[shards]
    )
    came = exchange(1, send)
    last = gathered(shards)
    grad_tokens, output, done = in_place(place, last)
    keep, send, sums = halve("halve_d", [(keep, came)], sums=sums)
    came = exchange(2, send)
    keep, send, sums = halve("halve_e", [(keep, came)], sums=sums, after=[done])
    came = exchange(3, send)
    sums = last_sums(sums, came[0])
    sums_received = scattered([sums] * 3)
    grad_down, grad_gate, grad_up, grad_in, grad_out = finish(keep, came, after=[sums])
    gain_mix_sum, gain_ffn_sum, conv_sum = small_sums(sums, sums_received)

    return (
        output.reshape(2, 128, D),
        grad_tokens.reshape(2, 128, D),
        gain_mix_sum.reshape(D),
        jnp.transpose(grad_in, (1, 0, 2)),
        conv_sum,
        grad_out.T,
        gain_ffn_sum.reshape(D),
        grad_gate,
        grad_up,
        grad_down.T,
    )


def solution(mesh):
    placed = (
        P(None, "seq", None),
        P(),
        P(None, None, "tp"),
        P(None, "tp"),
        P("tp", None),
        P(),
        P(None, "tp"),
        P(None, "tp"),
        P("tp", None),
        P(None, "seq", None),
        P(),
    )
    return jax.shard_map(
        per_device,
        mesh=mesh,
        in_specs=placed,
        out_specs=(
            P(None, "seq", None),
            P(None, "seq", None),
            P(),
            P("seq", None, "tp"),
            P(None, "tp"),
            P("tp", "seq"),
            P(),
            P("seq", "tp"),
            P("seq", "tp"),
            P("tp", "seq"),
        ),
        check_vma=False,
    )
```

```python
import jax
import jax.numpy as jnp
import numpy as np
from jax import lax
from jax.experimental import pallas as pl
from jax.experimental.pallas import tpu as pltpu
from jax.sharding import PartitionSpec as P

epsilon = 1e-05
f32 = jnp.float32
bf16 = jnp.bfloat16

ROWS = 256
PIECE = 64
D = 2048
MiB = 1 << 20

FLIP = {"a": (1, 0, 3, 2), "b": (3, 2, 1, 0)}
CODE = {0: (0, 0), 1: (1, 0), 2: (1, 1), 3: (0, 1)}
PLACE = {bits: at for at, bits in CODE.items()}
ORDER = (
    (("xa", "xb", "ya", "yb"), ("ya", "yb", "xa", "xb")),
    (("xb", "xa", "yb", "ya"), ("yb", "ya", "xb", "xa")),
)


def seq_index(x, y, core):
    return (x * 4 + y) * 2 + core


def flipped(x, y, dim):
    ring = FLIP[dim[1]]
    return (ring[x], y) if dim[0] == "x" else (x, ring[y])


def stage_pairs(half, stage):
    pairs = []
    for x in range(4):
        for y in range(4):
            for core in range(2):
                to = flipped(x, y, ORDER[half][core][stage])
                pairs.append((seq_index(x, y, core), seq_index(*to, core)))
    return pairs


CORE_PAIRS = [(i, i ^ 1) for i in range(32)]


def block_table():
    table = np.zeros((32, 2, 16), np.int32)
    for x in range(4):
        for y in range(4):
            for core in range(2):
                for half in range(2):
                    for position in range(16):
                        bits = {"x": list(CODE[x]), "y": list(CODE[y])}
                        for stage, dim in enumerate(ORDER[half][core]):
                            if (position >> (3 - stage)) & 1:
                                bits[dim[0]]["ab".index(dim[1])] ^= 1
                        owner = PLACE[tuple(bits["x"])] * 4 + PLACE[tuple(bits["y"])]
                        table[seq_index(x, y, core), half, position] = owner
    return table


BLOCKS = block_table()


FULL = pl.BlockSpec(memory_space=pltpu.VMEM)
FAR = pl.BlockSpec(memory_space=pl.ANY)
NUMBERS = pl.BlockSpec(memory_space=pltpu.SMEM)


class Far:
    def __init__(self, array):
        self.array = array


class Free:
    def __init__(self, array):
        self.array = array


def size(shape, kind):
    return int(np.prod(shape)) * jnp.dtype(kind).itemsize


def call(body, name, ins, outs, numbers=(), scratch=(), after=(), more=4, weight=1):
    room = more * MiB
    operands, specs = list(numbers), [NUMBERS] * len(numbers)
    for array in ins:
        if isinstance(array, Far):
            operands.append(pltpu.with_memory_space_constraint(array.array, pltpu.HBM))
            specs.append(FAR)
        else:
            operands.append(pltpu.with_memory_space_constraint(array, pltpu.VMEM))
            specs.append(FULL)
    count = len(operands)
    shapes = []
    for out in outs:
        if isinstance(out, Free):
            room += size(*out.array)
            shapes.append(jax.ShapeDtypeStruct(*out.array))
        else:
            shapes.append(pltpu.VMEM(*out))
    for kept in scratch:
        if kept.memory_space == pltpu.VMEM:
            room += size(kept.inner_aval.shape, kept.inner_aval.dtype)

    def run(*refs):
        body(*refs[:count], *refs[count + len(after) :])

    return pl.pallas_call(
        run,
        in_specs=specs + [FAR] * len(after),
        out_specs=[FULL] * len(outs),
        out_shape=shapes,
        scratch_shapes=list(scratch),
        compiler_params=pltpu.CompilerParams(vmem_limit_bytes=int(room)),
        cost_estimate=pl.CostEstimate(flops=weight, bytes_accessed=1, transcendentals=0),
        name=name,
    )(*operands, *after)


def matmul(left, right):
    return lax.dot_general(left, right, (((1,), (0,)), ((), ())), preferred_element_type=f32)


def matmul_t(left, right):
    return lax.dot_general(left, right, (((1,), (1,)), ((), ())), preferred_element_type=f32)


def normalize(values):
    return lax.rsqrt(jnp.mean(values * values, -1, keepdims=True) + epsilon)


def spans(total, each):
    return [slice(at, at + each) for at in range(0, total, each)]


def rotated(z, piece):
    return pl.multiple_of(lax.rem(z + piece, 4) * PIECE, PIECE)


PIECE_OUTS = [((PIECE, D), f32)] + [((PIECE, D), bf16)] * 3


def cut(total, own, one, two, three, cols=slice(None)):
    own[:, cols] = total[0:64]
    one[:, cols] = total[64:128].astype(bf16)
    two[:, cols] = total[128:192].astype(bf16)
    three[:, cols] = total[192:256].astype(bf16)


def added(own, r1, r2, r3):
    return own + (r1.astype(f32) + r2.astype(f32) + r3.astype(f32))


def release(name, arrays, after=(), weight=1):
    count = len(arrays)
    return pl.pallas_call(
        lambda *refs: None,
        in_specs=[FAR] * (count + len(after)),
        out_specs=[FAR] * count,
        out_shape=[jax.ShapeDtypeStruct(array.shape, array.dtype) for array in arrays],
        input_output_aliases={n: n for n in range(count)},
        compiler_params=pltpu.CompilerParams(vmem_limit_bytes=MiB),
        cost_estimate=pl.CostEstimate(flops=weight, bytes_accessed=1, transcendentals=0),
        name=name,
    )(*arrays, *after)


LONG = 4 * 10**10


class Stream:
    def __init__(self, copies, depth=3):
        self.copies, self.started = copies, 0
        for _ in range(depth):
            self.more()

    def more(self):
        if self.started < len(self.copies):
            self.copies[self.started].start()
            self.started += 1

    def wait(self, n):
        self.copies[n].wait()
        self.more()


SUMS = (16, 512)


def pack(to, row, sums):
    high = sums.astype(bf16)
    to[row : row + 16, 0:512] = high
    to[row : row + 16, 512:1024] = (sums - high.astype(f32)).astype(bf16)


def unpack(came, row):
    return came[row : row + 16, 0:512].astype(f32) + came[row : row + 16, 512:1024].astype(f32)


TABLE = 4


def turn_into(core, flat, mine, other, base=0):
    for block in range(16):
        rows = slice(block * 64, block * 64 + 64)
        mine[rows] = flat[pl.ds(pl.multiple_of(block * 128 + core * 64, 64), 64)]
        other[base + block * 64 : base + block * 64 + 64] = flat[
            pl.ds(pl.multiple_of(block * 128 + (1 - core) * 64, 64), 64)
        ]


def project_in(place, lengths, tokens, gain_mix, gain_ffn, conv_weight, w_in, cotangent, w_out):
    order = (0, 2, 1)

    def body(at, len_ref, *refs):
        tok_far, mix_far, ffn_far, conv_far, w_far, cot_far, out_far = refs[:7]
        tok, mix, ffn, conv, normed, b_out, c_out, v_out, q_out, tail = refs[7:17]
        out, w_o, grad_mine, one_mine, other, w, cot, flat, sems = refs[17:]
        z, position, core = at[0], at[1] * 128, at[2]
        small = [
            pltpu.make_async_copy(far, near, sems.at[n])
            for n, (far, near) in enumerate(((tok_far, tok), (mix_far, mix), (ffn_far, ffn), (conv_far, conv)))
        ]
        for copy in small:
            copy.start()
        cot_copy = pltpu.make_async_copy(cot_far, cot, sems.at[7])
        cot_copy.start()
        copies = [pltpu.make_async_copy(w_far.at[part], w.at[part], sems.at[4 + part]) for part in order]
        stream = Stream(copies + [pltpu.make_async_copy(out_far, w_o, sems.at[8])], 2)
        for copy in small:
            copy.wait()
        values = tok[...].astype(f32)
        normed[...] = (values * normalize(values) * mix[...]).astype(bf16)
        flat[...] = normed[...].T
        turn_into(core, flat, one_mine, other, 1024)
        cot_copy.wait()
        for piece in range(4):
            block = lax.rem(z + piece, 4)
            seq, half = block // 2, lax.rem(block, 2)
            first = position + half * PIECE
            rows = first + lax.broadcasted_iota(jnp.int32, (PIECE, D), 0)
            values = cot[pl.ds(rotated(z, piece), PIECE)].astype(f32)
            out[piece * PIECE : (piece + 1) * PIECE] = jnp.where(rows < len_ref[seq], values, 0.0).astype(bf16)
        flat[...] = out[...].T
        turn_into(core, flat, grad_mine, other, 0)
        for n, part in enumerate(order):
            stream.wait(n)
            (b_out, c_out, v_out)[part][...] = matmul(normed[...], w[part])
            if part == 2:
                q = (b_out[...] * v_out[...]).astype(bf16)
                q_out[...] = q
                tail[0] = q[112:128].astype(f32)[8:16]
                tail[1] = q[240:256].astype(f32)[8:16]
        stream.wait(3)

    return call(
        body,
        "project_in",
        [
            Far(tokens),
            Far(gain_mix),
            Far(gain_ffn),
            Far(conv_weight),
            Far(w_in),
            Far(cotangent),
            Far(w_out),
        ],
        [
            ((ROWS, D), bf16),
            ((1, D), f32),
            ((1, D), f32),
            ((3, 512), f32),
            ((ROWS, D), bf16),
            ((ROWS, 512), f32),
            ((ROWS, 512), f32),
            ((ROWS, 512), f32),
            ((ROWS, 512), bf16),
            ((2, 8, 512), f32),
            ((ROWS, D), bf16),
            ((512, D), bf16),
            ((1024, ROWS), bf16),
            ((1024, ROWS), bf16),
            ((2048, ROWS), bf16),
        ],
        numbers=[place, lengths],
        scratch=[
            pltpu.VMEM((3, D, 512), bf16),
            pltpu.VMEM((ROWS, D), bf16),
            pltpu.VMEM((D, ROWS), bf16),
            pltpu.SemaphoreType.DMA((9,)),
        ],
    )


def project_out(place, q, carried, c_gate, conv_weight, w_out, after):
    def body(at, q_ref, carried_ref, c_ref, cw, w, conv_out, y_out, own, one, two, three, pad):
        z = at[0]
        for seq in range(2):
            rows = slice(seq * 128, seq * 128 + 128)
            pad[0:8] = carried_ref[seq]
            pad[8:136] = q_ref[rows].astype(f32)
            conv_out[rows] = cw[0:1] * pad[6:134] + cw[1:2] * pad[7:135] + cw[2:3] * pad[8:136]
        for piece in range(4):
            start = rotated(z, piece)
            y_out[piece * PIECE : (piece + 1) * PIECE] = (
                c_ref[pl.ds(start, PIECE)] * conv_out[pl.ds(start, PIECE)]
            ).astype(bf16)
        for cols in spans(D, 512):
            cut(matmul(y_out[...], w[:, cols]), own, one, two, three, cols)

    return call(
        body,
        "project_out",
        [q, carried, c_gate, conv_weight, w_out],
        [((ROWS, 512), f32), ((ROWS, 512), bf16)] + PIECE_OUTS,
        numbers=[place],
        scratch=[pltpu.VMEM((136, 512), f32)],
        after=after,
    )


def activation_grad(grad_low, w_down):
    def body(grad, w_far, out, w, sems):
        stream = Stream(
            [
                pltpu.make_async_copy(w_far.at[rows], w.at[rows], sems.at[n])
                for n, rows in enumerate(spans(2048, 512))
            ]
        )
        for n, rows in enumerate(spans(2048, 512)):
            stream.wait(n)
            out[:, rows] = matmul_t(grad[...], w[rows])

    return call(
        body,
        "activation_grad",
        [grad_low, Far(w_down)],
        [((ROWS, 2048), f32)],
        scratch=[pltpu.VMEM((2048, D), bf16), pltpu.SemaphoreType.DMA((4,))],
    )[0]


def residual_norm(place, own, received, tokens, gain, after):
    def body(at, own_ref, r1, r2, r3, tok, gain_ref, hidden, normed):
        values = tok[pl.ds(rotated(at[0], 0), PIECE)].astype(f32) + added(own_ref[...], r1[...], r2[...], r3[...])
        hidden[...] = values
        normed[...] = (values * normalize(values) * gain_ref[...]).astype(bf16)

    return call(
        body,
        "residual_norm",
        [own, *received, tokens, gain],
        [((PIECE, D), f32), ((PIECE, D), bf16)],
        numbers=[place],
        after=after,
    )


def bring(name, weights, after=()):
    count = len(weights)

    def body(*refs):
        copies = [pltpu.make_async_copy(refs[n], refs[count + n], refs[-1].at[n]) for n in range(count)]
        for copy in copies:
            copy.start()
        for copy in copies:
            copy.wait()

    return call(
        body,
        name,
        [Far(weight) for weight in weights],
        [(weight.shape, weight.dtype) for weight in weights],
        scratch=[pltpu.SemaphoreType.DMA((count,))],
        after=after,
        more=1,
    )


def feed_forward(pieces, w_gate, w_up, grad_act, mixed):
    def body(n0, n1, n2, n3, gates, ups, ga, mix, mid, normed):
        for piece, ref in enumerate((n0, n1, n2, n3)):
            normed[piece * PIECE : (piece + 1) * PIECE] = ref[...]
        mid[:, 6144:6656] = mix[...]
        for cols in spans(2048, 256):
            gate = matmul(normed[...], gates[:, cols])
            up = matmul(normed[...], ups[:, cols])
            sigma = jax.nn.sigmoid(gate)
            swish = gate * sigma
            grad = ga[:, cols]
            first = cols.start
            mid[:, cols] = (swish * up).astype(bf16)
            mid[:, 2048 + first : 2304 + first] = (grad * up * sigma * (1.0 + gate * (1.0 - sigma))).astype(bf16)
            mid[:, 4096 + first : 4352 + first] = (grad * swish).astype(bf16)

    return call(
        body,
        "feed_forward",
        [*pieces, w_gate, w_up, grad_act, mixed],
        [((ROWS, 6656), bf16), ((ROWS, D), bf16)],
    )


def turn(place, value, after=()):
    def body(at, tall, mine, other, flat):
        flat[...] = tall[...].T
        turn_into(at[2], flat, mine, other)

    return call(
        body,
        "turn",
        [value],
        [((1024, ROWS), bf16), ((1024, ROWS), bf16)],
        numbers=[place],
        scratch=[pltpu.VMEM((D, ROWS), bf16)],
        after=after,
    )


def feed_back(mid, w_gate, w_up, after=()):
    def body(mid_ref, gates, ups, own, one, two, three):
        for rows in spans(D, 256):
            total = matmul_t(mid_ref[:, 2048:4096], gates[rows]) + matmul_t(mid_ref[:, 4096:6144], ups[rows])
            cut(total, own, one, two, three, rows)

    return call(body, "feed_back", [mid, w_gate, w_up], PIECE_OUTS, after=after)


def down(mid, w_down, after=()):
    def body(mid_ref, w_far, own, one, two, three, w, sems):
        stream = Stream(
            [
                pltpu.make_async_copy(w_far.at[:, cols], w.at[:, cols], sems.at[n])
                for n, cols in enumerate(spans(D, 512))
            ]
        )
        for n, cols in enumerate(spans(D, 512)):
            stream.wait(n)
            cut(matmul(mid_ref[:, 0:2048], w[:, cols]), own, one, two, three, cols)

    return call(
        body,
        "down",
        [mid, Far(w_down)],
        PIECE_OUTS,
        scratch=[pltpu.VMEM((2048, D), bf16), pltpu.SemaphoreType.DMA((4,))],
        after=after,
    )


def hidden_grad(own, received, hidden, gain, grad_low, after):
    def body(own_ref, r1, r2, r3, h, gain_ref, grad, out, gain_part):
        total = added(own_ref[...], r1[...], r2[...], r3[...])
        values = h[...]
        rate = normalize(values)
        unit = values * rate
        gain_part[...] = jnp.sum(total * unit, axis=0, keepdims=True)
        scaled = total * gain_ref[...]
        inner = jnp.mean(scaled * unit, -1, keepdims=True)
        out[...] = (grad[0:PIECE].astype(f32) + rate * (scaled - unit * inner)).astype(bf16)

    return call(
        body,
        "hidden_grad",
        [own, *received, hidden, gain, grad_low],
        [((PIECE, D), bf16), ((1, D), f32)],
        after=after,
        weight=LONG,
    )


def mixed_grad(place, pieces, w_out, convolved, c_gate, q, carried, after):
    def body(at, h0, h1, h2, h3, w, conv, c_ref, q_ref, carried_ref, dconv, dc, head, taps, mine, other, hidden, tall, pad, flat):
        z = at[0]
        for piece, ref in enumerate((h0, h1, h2, h3)):
            hidden[pl.ds(rotated(z, piece), PIECE)] = ref[...]
            tall[piece * PIECE : (piece + 1) * PIECE] = ref[...]
        for cols in spans(512, 256):
            mixed = matmul_t(hidden[...], w[cols])
            dc[:, cols] = (mixed * conv[:, cols]).astype(bf16)
            dconv[:, cols] = mixed * c_ref[:, cols]
        flat[...] = tall[...].T
        turn_into(at[2], flat, mine, other)
        sums = []
        for seq in range(2):
            rows = slice(seq * 128, seq * 128 + 128)
            head[seq] = dconv[seq * 128 : seq * 128 + 8]
            pad[0:8] = carried_ref[seq]
            pad[8:136] = q_ref[rows].astype(f32)
            here = dconv[rows]
            sums.append([jnp.sum(here * pad[6 + tap : 134 + tap], axis=0, keepdims=True) for tap in range(3)])
        for tap in range(3):
            taps[tap : tap + 1] = sums[0][tap] + sums[1][tap]

    return call(
        body,
        "mixed_grad",
        [*pieces, w_out, convolved, c_gate, q, carried],
        [
            ((ROWS, 512), f32),
            ((ROWS, 512), bf16),
            ((2, 8, 512), f32),
            ((3, 512), f32),
            ((1024, ROWS), bf16),
            ((1024, ROWS), bf16),
        ],
        numbers=[place],
        scratch=[
            pltpu.VMEM((ROWS, D), bf16),
            pltpu.VMEM((ROWS, D), bf16),
            pltpu.VMEM((136, 512), f32),
            pltpu.VMEM((D, ROWS), bf16),
        ],
        after=after,
        weight=LONG,
    )


def input_grad(place, dconv, returned, dc, b_gate, x_part, conv_weight, w_in, tokens, gain_part, taps, after):
    def body(at, dk, ret, dc_ref, b, v, cw, w, tok, gains, taps_ref, dp0, dp1, own, one, two, three, sums, pad, total, dp):
        z = at[0]
        for seq in range(2):
            rows = slice(seq * 128, seq * 128 + 128)
            pad[0:128] = dk[rows]
            pad[128:136] = ret[seq]
            dq = cw[2:3] * pad[0:128] + cw[1:2] * pad[1:129] + cw[0:1] * pad[2:130]
            dp[rows, 0:512] = (dq * v[rows]).astype(bf16)
            dp[rows, 512:1024] = dc_ref[rows]
            dp[rows, 1024:1536] = (dq * b[rows]).astype(bf16)
        rate = normalize(tok[...].astype(f32))
        sums[...] = jnp.zeros(SUMS, f32)
        for cols in spans(D, 256):
            part = (
                matmul_t(dp[:, 0:512], w[0, cols])
                + matmul_t(dp[:, 512:1024], w[1, cols])
                + matmul_t(dp[:, 1024:1536], w[2, cols])
            )
            row, first = cols.start // 512, cols.start % 512
            sums[row : row + 1, first : first + 256] = jnp.sum(
                part * (tok[:, cols].astype(f32) * rate), axis=0, keepdims=True
            )
            total[...] = part
            own[:, cols] = total[pl.ds(rotated(z, 0), PIECE)]
            one[:, cols] = total[pl.ds(rotated(z, 1), PIECE)].astype(bf16)
            two[:, cols] = total[pl.ds(rotated(z, 2), PIECE)].astype(bf16)
            three[:, cols] = total[pl.ds(rotated(z, 3), PIECE)].astype(bf16)
        for row in range(4):
            sums[4 + row : 5 + row] = gains[:, row * 512 : row * 512 + 512]
        sums[8:11] = taps_ref[...]
        dp0[...] = dp[:, 0:768]
        dp1[0:ROWS] = dp[:, 768:1536]
        high = sums[...].astype(bf16)
        dp1[ROWS : ROWS + 16, 0:512] = high
        dp1[ROWS + 16 : ROWS + 32, 0:512] = (sums[...] - high.astype(f32)).astype(bf16)

    return call(
        body,
        "input_grad",
        [dconv, returned, dc, b_gate, x_part, conv_weight, w_in, tokens, gain_part, taps],
        [((ROWS, 768), bf16), ((ROWS + 32, 768), bf16)] + PIECE_OUTS + [(SUMS, f32)],
        numbers=[place],
        scratch=[pltpu.VMEM((136, 512), f32), pltpu.VMEM((ROWS, 256), f32), pltpu.VMEM((ROWS, 1536), bf16)],
        after=after,
    )


def last_shards(place, own, received, tokens, gain, grad_hidden, own_out, out_received, hidden, sums, after=()):
    def body(at, own_ref, r1, r2, r3, tok, gain_ref, grad, own_o, o1, o2, o3, h, sums_ref, out):
        rows = slice(0, PIECE)
        total = added(own_ref[...], r1[...], r2[...], r3[...])
        values = tok[pl.ds(rotated(at[0], 0), PIECE)].astype(f32)
        rate = normalize(values)
        unit = values * rate
        scaled = total * gain_ref[...]
        inner = jnp.mean(scaled * unit, -1, keepdims=True)
        out[rows] = (grad[...].astype(f32) + rate * (scaled - unit * inner)).astype(bf16)
        out[PIECE : 2 * PIECE] = (h[...] + added(own_o[...], o1[...], o2[...], o3[...])).astype(bf16)
        pack(out, 2 * PIECE, sums_ref[...])

    return call(
        body,
        "last_shards",
        [own, *received, tokens, gain, grad_hidden, own_out, *out_received, hidden, sums],
        [((2 * PIECE + 16, D), bf16)],
        numbers=[place],
        after=after,
        weight=LONG,
    )[0]


def in_place(place, pieces, weight=1, after=()):
    def body(at, p0, p1, p2, p3, grad, out, done):
        for piece, ref in enumerate((p0, p1, p2, p3)):
            rows = pl.ds(rotated(at[0], piece), PIECE)
            grad[rows] = ref[0:PIECE]
            out[rows] = ref[PIECE : 2 * PIECE]
        done[...] = jnp.zeros((8, 128), f32)

    return call(
        body,
        "in_place",
        [*pieces],
        [Free(((ROWS, D), bf16))] * 2 + [((8, 128), f32)],
        numbers=[place],
        after=after,
        weight=weight,
    )


def weight_grad(place, name, width, plan, sums=None, after=()):
    flat = [part for half in plan for part in half]
    arrays = []
    for mine, other, _, right_mine, right_other, _, _ in flat:
        for array in (mine, other, right_mine, right_other):
            if not any(array is known for known in arrays):
                arrays.append(array)
    count = len(arrays) + (sums is not None)

    def body(order, *refs):
        def ref(array):
            return refs[[known is array for known in arrays].index(True)]

        outs = refs[count : count + 4]
        left, right = refs[-2:]
        if sums is not None:
            came = ref(plan[1][0][4])
            total = refs[count - 1][...] + came[256:272, 0:512].astype(f32) + came[272:288, 0:512].astype(f32)
            refs[count + 4][...] = total
            pack(outs[1], 512, total)
        for half in range(2):
            keep, send = outs[2 * half : 2 * half + 2]
            to = 0
            for mine, other, base, right_mine, right_other, first, columns in plan[half]:
                mine, other, right_mine, right_other = map(ref, (mine, other, right_mine, right_other))
                for position in range(16):
                    start = order[TABLE + half * 16 + position] * 64
                    rows = slice(position * 64, position * 64 + 64)
                    left[rows, 0:256] = mine[pl.ds(pl.multiple_of(start, 64), 64)]
                    left[rows, 256:512] = other[pl.ds(pl.multiple_of(base + start, 64), 64)]
                for step, cols in enumerate(spans(columns, 256)):
                    at = slice(first + cols.start, first + cols.stop)
                    room = right.at[step % 2]
                    room[0:256] = right_mine[0:256, at]
                    room[256:512] = right_other[0:256, at]
                    to_cols = slice(to + cols.start, to + cols.stop)
                    total = matmul(left[...], room[...]).astype(bf16)
                    keep[:, to_cols] = total[0:512]
                    send[0:512, to_cols] = total[512:1024]
                to += columns

    shapes = [((512, width), bf16)] * 4
    if sums is not None:
        shapes = [shapes[0], ((528, width), bf16), *shapes[2:], (SUMS, f32)]
    keep0, send0, keep1, send1, *total = call(
        body,
        name,
        arrays + ([] if sums is None else [sums]),
        shapes,
        numbers=[place],
        scratch=[pltpu.VMEM((1024, 512), bf16), pltpu.VMEM((2, 512, 256), bf16)],
        after=after,
    )
    return [keep0, keep1], [send0, send1], *total


def halve(name, keeps, cames, moves, outs, sums=None, along=False, after=()):
    counts = [len(keep) for keep in keeps]
    ins = [array for keep, came in zip(keeps, cames) for array in (*keep, *came)]
    starts = [2 * sum(counts[:n]) for n in range(len(counts))]
    rows = keeps[0][0].shape[0]
    middle = rows // 2
    width = sum(move[3] for move in moves) // outs
    each = min(64, middle)
    extra = [] if sums is None else [sums]
    count = len(ins) + len(extra)

    def body(*refs):
        keep, send = refs[count : count + outs], refs[count + outs : count + 2 * outs]
        if sums is not None:
            total = refs[len(ins)][...]
            if rows < cames[0][-1].shape[0]:
                total = total + unpack(refs[2 * counts[0] - 1], rows)
            refs[count + 2 * outs][...] = total
            if along:
                pack(send[0], middle, total)

        @pl.loop(0, middle // each)
        def _(step):
            low = pl.ds(pl.multiple_of(step * each, each), each)
            high = pl.ds(pl.multiple_of(middle + step * each, each), each)
            for group, part, first, columns, out, to in moves:
                k, c = refs[starts[group] + part], refs[starts[group] + counts[group] + part]
                take, put = slice(first, first + columns), slice(to, to + columns)
                keep[out][low, put] = k[low, take] + c[low, take]
                send[out][low, put] = k[high, take] + c[high, take]

    sends = [((middle + 16 * (along and n == 0), width), bf16) for n in range(outs)]
    shapes = [((middle, width), bf16)] * outs + sends + ([] if sums is None else [(SUMS, f32)])
    results = call(body, name, ins + extra, shapes, after=after)
    return results[:outs], results[outs : 2 * outs], *results[2 * outs :]


def sum_gains(own, pieces, after):
    def body(sums, r1, r2, r3, out):
        out[...] = sums[...]
        out[0:8] = (sums[0:8] + unpack(r1, 128)[0:8]) + (unpack(r2, 128)[0:8] + unpack(r3, 128)[0:8])

    return call(body, "sum_gains", [own, *pieces[1:]], [(SUMS, f32)], after=after)[0]


def sum_over_stage(value, stage, after=()):
    def body(a, b, out):
        out[...] = a[...] + b[...]

    came = lax.ppermute(value, "seq", stage_pairs(0, stage))
    return call(body, "sum_stage", [value, came], [(SUMS, f32)], after=after)[0]


def finish(keeps, cames, sums, after=()):
    def body(k0, k1, c0, c1, sums_ref, down_out, gate, up, grad_in, grad_out, mix, ffn, conv):
        for half, (k, c, pair) in enumerate(((k0, c0, gate), (k1, c1, up))):

            def total(first, count, k=k, c=c):
                cols = slice(first, first + count)
                return k[:, cols].astype(f32) + c[:, cols].astype(f32)

            down_out[:, half * 1024 : half * 1024 + 1024] = total(0, 1024)
            pair[...] = total(1024, 2048)
            if half == 0:
                grad_in[0] = total(3072, 512)
                grad_in[1, :, 0:256] = total(3584, 256)
            else:
                grad_in[1, :, 256:512] = total(3072, 256)
                grad_in[2] = total(3328, 512)
            grad_out[:, half * 256 : half * 256 + 256] = total(3840, 256)
        sums_all = sums_ref[...]
        for row in range(4):
            mix[:, row * 512 : row * 512 + 512] = sums_all[row : row + 1]
            ffn[:, row * 512 : row * 512 + 512] = sums_all[4 + row : 5 + row]
        conv[...] = sums_all[8:11]

    return call(
        body,
        "finish",
        [*keeps, *cames, sums],
        [Free(((64, 2048), f32))] * 3
        + [Free(((3, 64, 512), f32)), Free(((64, 512), f32))]
        + [Free(((1, D), f32))] * 2
        + [Free(((3, 512), f32))],
        after=after,
    )


def to_next(value, axis, steps):
    count = lax.axis_size(axis)
    first, last = (max(0, -steps), min(count, count - steps))
    return lax.ppermute(value, axis, [(source, source + steps) for source in range(first, last)])


def around(value, steps):
    return lax.ppermute(value, "tp", [(source, (source + steps) % 4) for source in range(4)])


def scattered(pieces):
    far = around(pieces[1], 2)
    return [far, around(pieces[0], 1), around(pieces[2], 3)]


def gathered(shard):
    far = around(shard, 2)
    return [shard, around(shard, 3), far, around(shard, 1)]


def other_core(value):
    return lax.ppermute(value, "seq", CORE_PAIRS)


def exchange(stage, sends):
    return [lax.ppermute(send, "seq", stage_pairs(half, stage)) for half, send in enumerate(sends)]


def per_device(
    tokens, gain_mix, w_in, conv_weight, w_out, gain_ffn, w_gate, w_up, w_down, cotangent, lengths
):
    seq, z = lax.axis_index("seq"), lax.axis_index("tp")
    place = jnp.concatenate(
        [jnp.stack([z, seq, lax.rem(seq, 2), z]).astype(jnp.int32), jnp.asarray(BLOCKS.reshape(32, 32))[seq]]
    )
    tokens = tokens.reshape(ROWS, D)
    cotangent = cotangent.reshape(ROWS, D)
    w_in = jnp.transpose(w_in, (1, 0, 2))

    first = project_in(
        place, lengths, tokens, gain_mix.reshape(1, D), gain_ffn.reshape(1, D), conv_weight, w_in, cotangent, w_out
    )
    tokens, gain_mix, gain_ffn, conv_weight, normed, b_gate, c_gate, x_part, q, tail = first[:10]
    grad_low, near_out, grad_turned, one_turned, turned = first[10:]
    carried = to_next(tail, "seq", 1)
    turned_other = other_core(turned)
    convolved, mixed, own, *pieces = project_out(
        place, q, carried, c_gate, conv_weight, near_out, after=[turned_other]
    )
    received = scattered(pieces)
    grad_act = activation_grad(grad_low, w_down)
    hidden, shard = residual_norm(place, own, received, tokens, gain_ffn, after=[grad_act])
    normed_two = gathered(shard)
    gates, ups = bring("bring_ffn", [w_gate, w_up], after=[grad_act])

    mid, normed_two = feed_forward(normed_two, gates, ups, grad_act, mixed)
    mid_other = other_core(mid)
    own, *pieces = feed_back(mid, gates, ups)
    received = scattered(pieces)

    two_turned, two_sent = turn(place, normed_two, after=[own])
    two_other = other_core(two_sent)
    keep_a, send_a = weight_grad(
        place,
        "weight_grad_a",
        1024,
        [[(grad_turned, turned_other, 0, mid, mid_other, 1024 * half, 1024)] for half in range(2)],
        after=[two_sent],
    )
    came_a = exchange(0, send_a)

    def weight_grad_b(part, after):
        return weight_grad(
            place,
            "weight_grad_b",
            1024,
            [
                [(two_turned, two_other, 0, mid, mid_other, 2048 + 2048 * half + 1024 * part, 1024)]
                for half in range(2)
            ],
            after=after,
        )

    keep_b, send_b = weight_grad_b(0, [send_a[0]])
    hidden_low, gain_part = hidden_grad(own, received, hidden, gain_ffn, grad_low, after=[send_b[0]])
    hidden_pieces = gathered(hidden_low)
    near_out, near_in = bring("bring_mixer", [w_out, w_in], after=[hidden_low])
    send_b = release("release_b", send_b, after=[*came_a, near_in])
    came_b = exchange(0, send_b)
    keep_d, send_d = weight_grad_b(1, [send_b[0]])
    own_out, *out_pieces = down(mid, w_down, after=[send_d[0]])

    dconv, dc, head, taps, hidden_turned, hidden_sent = mixed_grad(
        place, hidden_pieces, near_out, convolved, c_gate, q, carried, after=[near_in, own_out]
    )
    returned = to_next(head, "seq", -1)
    send_d = release("release_d", send_d, after=[*came_b, returned])
    came_d = exchange(0, send_d)
    hidden_other = other_core(hidden_sent)
    *dp, own, one, two, three, sums = input_grad(
        place, dconv, returned, dc, b_gate, x_part, conv_weight, near_in, tokens, gain_part, taps,
        after=[hidden_other, send_d[0]],
    )
    dp_other = [other_core(part) for part in dp]
    keep_c, send_c, sums = weight_grad(
        place,
        "weight_grad_c",
        1024,
        [
            [
                (one_turned, turned_other, 1024, dp[half], dp_other[half], 0, 768),
                (hidden_turned, hidden_other, 0, mid, mid_other, 6144 + 256 * half, 256),
            ]
            for half in range(2)
        ],
        sums=sums,
        after=[own],
    )
    pieces = release("release_z", [one, two, three], after=[*dp_other, send_c[0]])
    received = release("hold", scattered(pieces), weight=LONG)
    send_c = release("release_c", send_c, after=came_d)
    came_c = exchange(0, send_c)

    keep, send, sums = halve(
        "halve_abc",
        list(zip(keep_a, keep_b, keep_d, keep_c)),
        list(zip(came_a, came_b, came_d, came_c)),
        [(half, part, 0, 1024, half, 1024 * part) for half in range(2) for part in range(4)],
        2,
        sums=sums,
        after=received,
    )
    came = exchange(1, send)
    out_received = scattered(release("release_out", out_pieces, after=received))
    shards = last_shards(
        place, own, received, tokens, gain_mix, hidden_low, own_out, out_received, hidden, sums, after=[]
    )
    pieces = gathered(shards)
    grad_tokens, output, done = in_place(place, pieces, LONG)
    whole = [(half, 0, 0, 4096, half, 0) for half in range(2)]
    keep, send = halve("halve_d", [[k] for k in keep], [[c] for c in came], whole, 2, after=[shards])
    came = exchange(2, send)
    sums = sum_gains(sums, pieces, after=[send[0], done])
    keep, send = halve("halve_e", [[k] for k in keep], [[c] for c in came], whole, 2, after=[done])
    came = exchange(3, send)
    for stage in (1, 2, 3):
        sums = sum_over_stage(sums, stage, after=[send[0]])
    grad_down, grad_gate, grad_up, grad_in, grad_out, gain_mix_sum, gain_ffn_sum, conv_sum = finish(keep, came, sums)

    return (
        output.reshape(2, 128, D),
        grad_tokens.reshape(2, 128, D),
        gain_mix_sum.reshape(D),
        jnp.transpose(grad_in, (1, 0, 2)),
        conv_sum,
        grad_out.T,
        gain_ffn_sum.reshape(D),
        grad_gate,
        grad_up,
        grad_down.T,
    )


def solution(mesh):
    placed = (
        P(None, "seq", None),
        P(),
        P(None, None, "tp"),
        P(None, "tp"),
        P("tp", None),
        P(),
        P(None, "tp"),
        P(None, "tp"),
        P("tp", None),
        P(None, "seq", None),
        P(),
    )
    return jax.shard_map(
        per_device,
        mesh=mesh,
        in_specs=placed,
        out_specs=(
            P(None, "seq", None),
            P(None, "seq", None),
            P(),
            P("seq", None, "tp"),
            P(None, "tp"),
            P("tp", "seq"),
            P(),
            P("seq", "tp"),
            P("seq", "tp"),
            P("tp", "seq"),
        ),
        check_vma=False,
    )
```

```python
import jax
import jax.numpy as jnp
import numpy as np
from jax import lax
from jax.experimental import pallas as pl
from jax.experimental.pallas import tpu as pltpu
from jax.sharding import PartitionSpec as P

epsilon = 1e-05
f32 = jnp.float32
bf16 = jnp.bfloat16

ROWS = 256
PIECE = 64
D = 2048
MiB = 1 << 20

FLIP = {"a": (1, 0, 3, 2), "b": (3, 2, 1, 0)}
CODE = {0: (0, 0), 1: (1, 0), 2: (1, 1), 3: (0, 1)}
PLACE = {bits: at for at, bits in CODE.items()}
ORDER = (
    (("xa", "xb", "ya", "yb"), ("ya", "yb", "xa", "xb")),
    (("xb", "xa", "yb", "ya"), ("yb", "ya", "xb", "xa")),
)


def seq_index(x, y, core):
    return (x * 4 + y) * 2 + core


def flipped(x, y, dim):
    ring = FLIP[dim[1]]
    return (ring[x], y) if dim[0] == "x" else (x, ring[y])


def stage_pairs(half, stage):
    pairs = []
    for x in range(4):
        for y in range(4):
            for core in range(2):
                to = flipped(x, y, ORDER[half][core][stage])
                pairs.append((seq_index(x, y, core), seq_index(*to, core)))
    return pairs


CORE_PAIRS = [(i, i ^ 1) for i in range(32)]


FULL = pl.BlockSpec(memory_space=pltpu.VMEM)
FAR = pl.BlockSpec(memory_space=pl.ANY)
NUMBERS = pl.BlockSpec(memory_space=pltpu.SMEM)


class Far:
    def __init__(self, array):
        self.array = array


class Free:
    def __init__(self, array):
        self.array = array


def size(shape, kind):
    return int(np.prod(shape)) * jnp.dtype(kind).itemsize


def call(body, name, ins, outs, numbers=(), scratch=(), after=(), more=4, weight=1):
    room = more * MiB
    operands, specs = list(numbers), [NUMBERS] * len(numbers)
    for array in ins:
        if isinstance(array, Far):
            operands.append(pltpu.with_memory_space_constraint(array.array, pltpu.HBM))
            specs.append(FAR)
        else:
            operands.append(pltpu.with_memory_space_constraint(array, pltpu.VMEM))
            specs.append(FULL)
    count = len(operands)
    shapes = []
    for out in outs:
        if isinstance(out, Free):
            room += size(*out.array)
            shapes.append(jax.ShapeDtypeStruct(*out.array))
        else:
            shapes.append(pltpu.VMEM(*out))
    for kept in scratch:
        if kept.memory_space == pltpu.VMEM:
            room += size(kept.inner_aval.shape, kept.inner_aval.dtype)

    def run(*refs):
        body(*refs[:count], *refs[count + len(after) :])

    return pl.pallas_call(
        run,
        in_specs=specs + [FAR] * len(after),
        out_specs=[FULL] * len(outs),
        out_shape=shapes,
        scratch_shapes=list(scratch),
        compiler_params=pltpu.CompilerParams(vmem_limit_bytes=int(room)),
        cost_estimate=pl.CostEstimate(flops=weight, bytes_accessed=1, transcendentals=0),
        name=name,
    )(*operands, *after)


def matmul(left, right):
    return lax.dot_general(left, right, (((1,), (0,)), ((), ())), preferred_element_type=f32)


def matmul_t(left, right):
    return lax.dot_general(left, right, (((1,), (1,)), ((), ())), preferred_element_type=f32)


def normalize(values):
    return lax.rsqrt(jnp.mean(values * values, -1, keepdims=True) + epsilon)


def spans(total, each):
    return [slice(at, at + each) for at in range(0, total, each)]


def rotated(z, piece):
    return pl.multiple_of(lax.rem(z + piece, 4) * PIECE, PIECE)


PIECE_OUTS = [((PIECE, D), f32)] + [((PIECE, D), bf16)] * 3


def cut(total, own, one, two, three, cols=slice(None)):
    own[:, cols] = total[0:64]
    one[:, cols] = total[64:128].astype(bf16)
    two[:, cols] = total[128:192].astype(bf16)
    three[:, cols] = total[192:256].astype(bf16)


def added(own, r1, r2, r3):
    return own + (r1.astype(f32) + r2.astype(f32) + r3.astype(f32))


def release(name, arrays, after=(), weight=1):
    count = len(arrays)
    return pl.pallas_call(
        lambda *refs: None,
        in_specs=[FAR] * (count + len(after)),
        out_specs=[FAR] * count,
        out_shape=[jax.ShapeDtypeStruct(array.shape, array.dtype) for array in arrays],
        input_output_aliases={n: n for n in range(count)},
        compiler_params=pltpu.CompilerParams(vmem_limit_bytes=MiB),
        cost_estimate=pl.CostEstimate(flops=weight, bytes_accessed=1, transcendentals=0),
        name=name,
    )(*arrays, *after)


LONG = 4 * 10**10


class Stream:
    def __init__(self, copies, depth=3):
        self.copies, self.started = copies, 0
        for _ in range(depth):
            self.more()

    def more(self):
        if self.started < len(self.copies):
            self.copies[self.started].start()
            self.started += 1

    def wait(self, n):
        self.copies[n].wait()
        self.more()


SUMS = (16, 512)


def pack(to, row, sums):
    high = sums.astype(bf16)
    to[row : row + 16, 0:512] = high
    to[row : row + 16, 512:1024] = (sums - high.astype(f32)).astype(bf16)


def unpack(came, row):
    return came[row : row + 16, 0:512].astype(f32) + came[row : row + 16, 512:1024].astype(f32)


def block_at(at, half, position):
    core, seq = at[2], at[1]
    owner = []
    for axis, here in (("x", seq // 8), ("y", lax.rem(seq // 2, 4))):
        flips = {"a": 0, "b": 0}
        for stage in range(4):
            if (position >> (3 - stage)) & 1:
                dims = [ORDER[half][n][stage] for n in range(2)]
                for n, dim in enumerate(dims):
                    if dim[0] == axis:
                        flips[dim[1]] = flips[dim[1]] + (core if n else 1 - core)
        a = lax.rem(lax.rem((here + 1) // 2, 2) + flips["a"], 2)
        b = lax.rem(here // 2 + flips["b"], 2)
        owner.append(2 * b + lax.rem(a + b, 2))
    return 4 * owner[0] + owner[1]


def turn_into(core, flat, mine, other, base=0):
    for block in range(16):
        rows = slice(block * 64, block * 64 + 64)
        mine[rows] = flat[pl.ds(pl.multiple_of(block * 128 + core * 64, 64), 64)]
        other[base + block * 64 : base + block * 64 + 64] = flat[
            pl.ds(pl.multiple_of(block * 128 + (1 - core) * 64, 64), 64)
        ]


def project_in(place, lengths, tokens, gain_mix, gain_ffn, conv_weight, w_in, cotangent, w_out):
    order = (0, 2, 1)

    def body(at, *refs):
        tok_far, mix_far, ffn_far, conv_far, w_far, cot_far, out_far, len_far = refs[:8]
        tok, mix, ffn, conv, normed, b_out, c_out, v_out, q_out, tail = refs[8:18]
        out, w_o, grad_mine, one_mine, other, w, cot, flat, len_ref, sems = refs[18:]
        z, position, core = at[0], at[1] * 128, at[2]
        small = [
            pltpu.make_async_copy(far, near, sems.at[n])
            for n, (far, near) in enumerate(((tok_far, tok), (mix_far, mix), (ffn_far, ffn), (conv_far, conv)))
        ]
        for copy in small:
            copy.start()
        cot_copy = pltpu.make_async_copy(cot_far, cot, sems.at[7])
        cot_copy.start()
        len_copy = pltpu.make_async_copy(len_far, len_ref, sems.at[9])
        len_copy.start()
        copies = [pltpu.make_async_copy(w_far.at[part], w.at[part], sems.at[4 + part]) for part in order]
        stream = Stream(copies + [pltpu.make_async_copy(out_far, w_o, sems.at[8])], 2)
        for copy in small:
            copy.wait()
        values = tok[...].astype(f32)
        normed[...] = (values * normalize(values) * mix[...]).astype(bf16)
        flat[...] = normed[...].T
        turn_into(core, flat, one_mine, other, 1024)
        cot_copy.wait()
        len_copy.wait()
        for piece in range(4):
            block = lax.rem(z + piece, 4)
            seq, half = block // 2, lax.rem(block, 2)
            first = position + half * PIECE
            rows = first + lax.broadcasted_iota(jnp.int32, (PIECE, D), 0)
            values = cot[pl.ds(rotated(z, piece), PIECE)].astype(f32)
            out[piece * PIECE : (piece + 1) * PIECE] = jnp.where(rows < len_ref[seq], values, 0.0).astype(bf16)
        flat[...] = out[...].T
        turn_into(core, flat, grad_mine, other, 0)
        for n, part in enumerate(order):
            stream.wait(n)
            (b_out, c_out, v_out)[part][...] = matmul(normed[...], w[part])
            if part == 2:
                q = (b_out[...] * v_out[...]).astype(bf16)
                q_out[...] = q
                tail[0] = q[112:128].astype(f32)[8:16]
                tail[1] = q[240:256].astype(f32)[8:16]
        stream.wait(3)

    return call(
        body,
        "project_in",
        [
            Far(tokens),
            Far(gain_mix),
            Far(gain_ffn),
            Far(conv_weight),
            Far(w_in),
            Far(cotangent),
            Far(w_out),
            Far(lengths),
        ],
        [
            ((ROWS, D), bf16),
            ((1, D), f32),
            ((1, D), f32),
            ((3, 512), f32),
            ((ROWS, D), bf16),
            ((ROWS, 512), f32),
            ((ROWS, 512), f32),
            ((ROWS, 512), f32),
            ((ROWS, 512), bf16),
            ((2, 8, 512), f32),
            ((ROWS, D), bf16),
            ((512, D), bf16),
            ((1024, ROWS), bf16),
            ((1024, ROWS), bf16),
            ((2048, ROWS), bf16),
        ],
        numbers=[place],
        scratch=[
            pltpu.VMEM((3, D, 512), bf16),
            pltpu.VMEM((ROWS, D), bf16),
            pltpu.VMEM((D, ROWS), bf16),
            pltpu.SMEM((2,), jnp.int32),
            pltpu.SemaphoreType.DMA((10,)),
        ],
    )


def project_out(place, q, carried, c_gate, conv_weight, w_out, after):
    def body(at, q_ref, carried_ref, c_ref, cw, w, conv_out, y_out, own, one, two, three, pad):
        z = at[0]
        for seq in range(2):
            rows = slice(seq * 128, seq * 128 + 128)
            pad[0:8] = carried_ref[seq]
            pad[8:136] = q_ref[rows].astype(f32)
            conv_out[rows] = cw[0:1] * pad[6:134] + cw[1:2] * pad[7:135] + cw[2:3] * pad[8:136]
        for piece in range(4):
            start = rotated(z, piece)
            y_out[piece * PIECE : (piece + 1) * PIECE] = (
                c_ref[pl.ds(start, PIECE)] * conv_out[pl.ds(start, PIECE)]
            ).astype(bf16)
        for cols in spans(D, 512):
            cut(matmul(y_out[...], w[:, cols]), own, one, two, three, cols)

    return call(
        body,
        "project_out",
        [q, carried, c_gate, conv_weight, w_out],
        [((ROWS, 512), f32), ((ROWS, 512), bf16)] + PIECE_OUTS,
        numbers=[place],
        scratch=[pltpu.VMEM((136, 512), f32)],
        after=after,
    )


def activation_grad(grad_low, w_down):
    def body(grad, w_far, out, w, sems):
        stream = Stream(
            [
                pltpu.make_async_copy(w_far.at[rows], w.at[rows], sems.at[n])
                for n, rows in enumerate(spans(2048, 512))
            ]
        )
        for n, rows in enumerate(spans(2048, 512)):
            stream.wait(n)
            out[:, rows] = matmul_t(grad[...], w[rows])

    return call(
        body,
        "activation_grad",
        [grad_low, Far(w_down)],
        [((ROWS, 2048), f32)],
        scratch=[pltpu.VMEM((2048, D), bf16), pltpu.SemaphoreType.DMA((4,))],
    )[0]


def residual_norm(place, own, received, tokens, gain, after):
    def body(at, own_ref, r1, r2, r3, tok, gain_ref, hidden, normed):
        values = tok[pl.ds(rotated(at[0], 0), PIECE)].astype(f32) + added(own_ref[...], r1[...], r2[...], r3[...])
        hidden[...] = values
        normed[...] = (values * normalize(values) * gain_ref[...]).astype(bf16)

    return call(
        body,
        "residual_norm",
        [own, *received, tokens, gain],
        [((PIECE, D), f32), ((PIECE, D), bf16)],
        numbers=[place],
        after=after,
    )


def bring(name, weights, after=()):
    count = len(weights)

    def body(*refs):
        copies = [pltpu.make_async_copy(refs[n], refs[count + n], refs[-1].at[n]) for n in range(count)]
        for copy in copies:
            copy.start()
        for copy in copies:
            copy.wait()

    return call(
        body,
        name,
        [Far(weight) for weight in weights],
        [(weight.shape, weight.dtype) for weight in weights],
        scratch=[pltpu.SemaphoreType.DMA((count,))],
        after=after,
        more=1,
    )


def feed_forward(pieces, w_gate, w_up, grad_act, mixed):
    def body(n0, n1, n2, n3, gates, ups, ga, mix, mid, normed):
        for piece, ref in enumerate((n0, n1, n2, n3)):
            normed[piece * PIECE : (piece + 1) * PIECE] = ref[...]
        mid[:, 6144:6656] = mix[...]
        for cols in spans(2048, 256):
            gate = matmul(normed[...], gates[:, cols])
            up = matmul(normed[...], ups[:, cols])
            sigma = jax.nn.sigmoid(gate)
            swish = gate * sigma
            grad = ga[:, cols]
            first = cols.start
            mid[:, cols] = (swish * up).astype(bf16)
            mid[:, 2048 + first : 2304 + first] = (grad * up * sigma * (1.0 + gate * (1.0 - sigma))).astype(bf16)
            mid[:, 4096 + first : 4352 + first] = (grad * swish).astype(bf16)

    return call(
        body,
        "feed_forward",
        [*pieces, w_gate, w_up, grad_act, mixed],
        [((ROWS, 6656), bf16), ((ROWS, D), bf16)],
    )


def turn(place, value, after=()):
    def body(at, tall, mine, other, flat):
        flat[...] = tall[...].T
        turn_into(at[2], flat, mine, other)

    return call(
        body,
        "turn",
        [value],
        [((1024, ROWS), bf16), ((1024, ROWS), bf16)],
        numbers=[place],
        scratch=[pltpu.VMEM((D, ROWS), bf16)],
        after=after,
    )


def feed_back(mid, w_gate, w_up, after=()):
    def body(mid_ref, gates, ups, own, one, two, three):
        for rows in spans(D, 256):
            total = matmul_t(mid_ref[:, 2048:4096], gates[rows]) + matmul_t(mid_ref[:, 4096:6144], ups[rows])
            cut(total, own, one, two, three, rows)

    return call(body, "feed_back", [mid, w_gate, w_up], PIECE_OUTS, after=after)


def down(mid, w_down, after=()):
    def body(mid_ref, w_far, own, one, two, three, w, sems):
        stream = Stream(
            [
                pltpu.make_async_copy(w_far.at[:, cols], w.at[:, cols], sems.at[n])
                for n, cols in enumerate(spans(D, 512))
            ]
        )
        for n, cols in enumerate(spans(D, 512)):
            stream.wait(n)
            cut(matmul(mid_ref[:, 0:2048], w[:, cols]), own, one, two, three, cols)

    return call(
        body,
        "down",
        [mid, Far(w_down)],
        PIECE_OUTS,
        scratch=[pltpu.VMEM((2048, D), bf16), pltpu.SemaphoreType.DMA((4,))],
        after=after,
    )


def hidden_grad(own, received, hidden, gain, grad_low, after):
    def body(own_ref, r1, r2, r3, h, gain_ref, grad, out, gain_part):
        total = added(own_ref[...], r1[...], r2[...], r3[...])
        values = h[...]
        rate = normalize(values)
        unit = values * rate
        gain_part[...] = jnp.sum(total * unit, axis=0, keepdims=True)
        scaled = total * gain_ref[...]
        inner = jnp.mean(scaled * unit, -1, keepdims=True)
        out[...] = (grad[0:PIECE].astype(f32) + rate * (scaled - unit * inner)).astype(bf16)

    return call(
        body,
        "hidden_grad",
        [own, *received, hidden, gain, grad_low],
        [((PIECE, D), bf16), ((1, D), f32)],
        after=after,
        weight=LONG,
    )


def mixed_grad(place, pieces, w_out, convolved, c_gate, q, carried, after):
    def body(at, h0, h1, h2, h3, w, conv, c_ref, q_ref, carried_ref, dconv, dc, head, taps, mine, other, hidden, tall, pad, flat):
        z = at[0]
        for piece, ref in enumerate((h0, h1, h2, h3)):
            hidden[pl.ds(rotated(z, piece), PIECE)] = ref[...]
            tall[piece * PIECE : (piece + 1) * PIECE] = ref[...]
        for cols in spans(512, 256):
            mixed = matmul_t(hidden[...], w[cols])
            dc[:, cols] = (mixed * conv[:, cols]).astype(bf16)
            dconv[:, cols] = mixed * c_ref[:, cols]
        flat[...] = tall[...].T
        turn_into(at[2], flat, mine, other)
        sums = []
        for seq in range(2):
            rows = slice(seq * 128, seq * 128 + 128)
            head[seq] = dconv[seq * 128 : seq * 128 + 8]
            pad[0:8] = carried_ref[seq]
            pad[8:136] = q_ref[rows].astype(f32)
            here = dconv[rows]
            sums.append([jnp.sum(here * pad[6 + tap : 134 + tap], axis=0, keepdims=True) for tap in range(3)])
        for tap in range(3):
            taps[tap : tap + 1] = sums[0][tap] + sums[1][tap]

    return call(
        body,
        "mixed_grad",
        [*pieces, w_out, convolved, c_gate, q, carried],
        [
            ((ROWS, 512), f32),
            ((ROWS, 512), bf16),
            ((2, 8, 512), f32),
            ((3, 512), f32),
            ((1024, ROWS), bf16),
            ((1024, ROWS), bf16),
        ],
        numbers=[place],
        scratch=[
            pltpu.VMEM((ROWS, D), bf16),
            pltpu.VMEM((ROWS, D), bf16),
            pltpu.VMEM((136, 512), f32),
            pltpu.VMEM((D, ROWS), bf16),
        ],
        after=after,
        weight=LONG,
    )


def input_grad(place, dconv, returned, dc, b_gate, x_part, conv_weight, w_in, tokens, gain_part, taps, after):
    def body(at, dk, ret, dc_ref, b, v, cw, w, tok, gains, taps_ref, dp0, dp1, own, one, two, three, sums, pad, total, dp):
        z = at[0]
        for seq in range(2):
            rows = slice(seq * 128, seq * 128 + 128)
            pad[0:128] = dk[rows]
            pad[128:136] = ret[seq]
            dq = cw[2:3] * pad[0:128] + cw[1:2] * pad[1:129] + cw[0:1] * pad[2:130]
            dp[rows, 0:512] = (dq * v[rows]).astype(bf16)
            dp[rows, 512:1024] = dc_ref[rows]
            dp[rows, 1024:1536] = (dq * b[rows]).astype(bf16)
        rate = normalize(tok[...].astype(f32))
        sums[...] = jnp.zeros(SUMS, f32)
        for cols in spans(D, 256):
            part = (
                matmul_t(dp[:, 0:512], w[0, cols])
                + matmul_t(dp[:, 512:1024], w[1, cols])
                + matmul_t(dp[:, 1024:1536], w[2, cols])
            )
            row, first = cols.start // 512, cols.start % 512
            sums[row : row + 1, first : first + 256] = jnp.sum(
                part * (tok[:, cols].astype(f32) * rate), axis=0, keepdims=True
            )
            total[...] = part
            own[:, cols] = total[pl.ds(rotated(z, 0), PIECE)]
            one[:, cols] = total[pl.ds(rotated(z, 1), PIECE)].astype(bf16)
            two[:, cols] = total[pl.ds(rotated(z, 2), PIECE)].astype(bf16)
            three[:, cols] = total[pl.ds(rotated(z, 3), PIECE)].astype(bf16)
        for row in range(4):
            sums[4 + row : 5 + row] = gains[:, row * 512 : row * 512 + 512]
        sums[8:11] = taps_ref[...]
        dp0[...] = dp[:, 0:768]
        dp1[0:ROWS] = dp[:, 768:1536]
        high = sums[...].astype(bf16)
        dp1[ROWS : ROWS + 16, 0:512] = high
        dp1[ROWS + 16 : ROWS + 32, 0:512] = (sums[...] - high.astype(f32)).astype(bf16)

    return call(
        body,
        "input_grad",
        [dconv, returned, dc, b_gate, x_part, conv_weight, w_in, tokens, gain_part, taps],
        [((ROWS, 768), bf16), ((ROWS + 32, 768), bf16)] + PIECE_OUTS + [(SUMS, f32)],
        numbers=[place],
        scratch=[pltpu.VMEM((136, 512), f32), pltpu.VMEM((ROWS, 256), f32), pltpu.VMEM((ROWS, 1536), bf16)],
        after=after,
    )


def last_shards(place, own, received, tokens, gain, grad_hidden, own_out, out_received, hidden, sums, after=()):
    def body(at, own_ref, r1, r2, r3, tok, gain_ref, grad, own_o, o1, o2, o3, h, sums_ref, out):
        rows = slice(0, PIECE)
        total = added(own_ref[...], r1[...], r2[...], r3[...])
        values = tok[pl.ds(rotated(at[0], 0), PIECE)].astype(f32)
        rate = normalize(values)
        unit = values * rate
        scaled = total * gain_ref[...]
        inner = jnp.mean(scaled * unit, -1, keepdims=True)
        out[rows] = (grad[...].astype(f32) + rate * (scaled - unit * inner)).astype(bf16)
        out[PIECE : 2 * PIECE] = (h[...] + added(own_o[...], o1[...], o2[...], o3[...])).astype(bf16)
        pack(out, 2 * PIECE, sums_ref[...])

    return call(
        body,
        "last_shards",
        [own, *received, tokens, gain, grad_hidden, own_out, *out_received, hidden, sums],
        [((2 * PIECE + 16, D), bf16)],
        numbers=[place],
        after=after,
        weight=LONG,
    )[0]


def in_place(place, pieces, weight=1, after=()):
    def body(at, p0, p1, p2, p3, grad, out, done):
        for piece, ref in enumerate((p0, p1, p2, p3)):
            rows = pl.ds(rotated(at[0], piece), PIECE)
            grad[rows] = ref[0:PIECE]
            out[rows] = ref[PIECE : 2 * PIECE]
        done[...] = jnp.zeros((8, 128), f32)

    return call(
        body,
        "in_place",
        [*pieces],
        [Free(((ROWS, D), bf16))] * 2 + [((8, 128), f32)],
        numbers=[place],
        after=after,
        weight=weight,
    )


def weight_grad(place, name, width, plan, sums=None, after=()):
    flat = [part for half in plan for part in half]
    arrays = []
    for mine, other, _, right_mine, right_other, _, _ in flat:
        for array in (mine, other, right_mine, right_other):
            if not any(array is known for known in arrays):
                arrays.append(array)
    count = len(arrays) + (sums is not None)

    def body(order, *refs):
        def ref(array):
            return refs[[known is array for known in arrays].index(True)]

        outs = refs[count : count + 4]
        left, right = refs[-2:]
        if sums is not None:
            came = ref(plan[1][0][4])
            total = refs[count - 1][...] + came[256:272, 0:512].astype(f32) + came[272:288, 0:512].astype(f32)
            refs[count + 4][...] = total
            pack(outs[1], 512, total)
        for half in range(2):
            keep, send = outs[2 * half : 2 * half + 2]
            to = 0
            for mine, other, base, right_mine, right_other, first, columns in plan[half]:
                mine, other, right_mine, right_other = map(ref, (mine, other, right_mine, right_other))
                for position in range(16):
                    start = block_at(order, half, position) * 64
                    rows = slice(position * 64, position * 64 + 64)
                    left[rows, 0:256] = mine[pl.ds(pl.multiple_of(start, 64), 64)]
                    left[rows, 256:512] = other[pl.ds(pl.multiple_of(base + start, 64), 64)]
                for step, cols in enumerate(spans(columns, 256)):
                    at = slice(first + cols.start, first + cols.stop)
                    room = right.at[step % 2]
                    room[0:256] = right_mine[0:256, at]
                    room[256:512] = right_other[0:256, at]
                    to_cols = slice(to + cols.start, to + cols.stop)
                    total = matmul(left[...], room[...]).astype(bf16)
                    keep[:, to_cols] = total[0:512]
                    send[0:512, to_cols] = total[512:1024]
                to += columns

    shapes = [((512, width), bf16)] * 4
    if sums is not None:
        shapes = [shapes[0], ((528, width), bf16), *shapes[2:], (SUMS, f32)]
    keep0, send0, keep1, send1, *total = call(
        body,
        name,
        arrays + ([] if sums is None else [sums]),
        shapes,
        numbers=[place],
        scratch=[pltpu.VMEM((1024, 512), bf16), pltpu.VMEM((2, 512, 256), bf16)],
        after=after,
    )
    return [keep0, keep1], [send0, send1], *total


def halve(name, keeps, cames, moves, outs, sums=None, along=False, after=()):
    counts = [len(keep) for keep in keeps]
    ins = [array for keep, came in zip(keeps, cames) for array in (*keep, *came)]
    starts = [2 * sum(counts[:n]) for n in range(len(counts))]
    rows = keeps[0][0].shape[0]
    middle = rows // 2
    width = sum(move[3] for move in moves) // outs
    each = min(64, middle)
    extra = [] if sums is None else [sums]
    count = len(ins) + len(extra)

    def body(*refs):
        keep, send = refs[count : count + outs], refs[count + outs : count + 2 * outs]
        if sums is not None:
            total = refs[len(ins)][...]
            if rows < cames[0][-1].shape[0]:
                total = total + unpack(refs[2 * counts[0] - 1], rows)
            refs[count + 2 * outs][...] = total
            if along:
                pack(send[0], middle, total)

        @pl.loop(0, middle // each)
        def _(step):
            low = pl.ds(pl.multiple_of(step * each, each), each)
            high = pl.ds(pl.multiple_of(middle + step * each, each), each)
            for group, part, first, columns, out, to in moves:
                k, c = refs[starts[group] + part], refs[starts[group] + counts[group] + part]
                take, put = slice(first, first + columns), slice(to, to + columns)
                keep[out][low, put] = k[low, take] + c[low, take]
                send[out][low, put] = k[high, take] + c[high, take]

    sends = [((middle + 16 * (along and n == 0), width), bf16) for n in range(outs)]
    shapes = [((middle, width), bf16)] * outs + sends + ([] if sums is None else [(SUMS, f32)])
    results = call(body, name, ins + extra, shapes, after=after)
    return results[:outs], results[outs : 2 * outs], *results[2 * outs :]


def sum_gains(own, pieces, after):
    def body(sums, r1, r2, r3, out):
        out[...] = sums[...]
        out[0:8] = (sums[0:8] + unpack(r1, 128)[0:8]) + (unpack(r2, 128)[0:8] + unpack(r3, 128)[0:8])

    return call(body, "sum_gains", [own, *pieces[1:]], [(SUMS, f32)], after=after)[0]


def sum_over_stage(value, stage, weight=1, after=()):
    def body(a, b, out):
        out[...] = a[...] + b[...]

    came = lax.ppermute(value, "seq", stage_pairs(0, stage))
    return call(body, "sum_stage", [value, came], [(SUMS, f32)], after=after, weight=weight)[0]


def finish(keeps, cames, sums, after=()):
    def body(k0, k1, c0, c1, sums_ref, down_out, gate, up, grad_in, grad_out, mix, ffn, conv):
        for half, (k, c, pair) in enumerate(((k0, c0, gate), (k1, c1, up))):

            def total(first, count, k=k, c=c):
                cols = slice(first, first + count)
                return k[:, cols].astype(f32) + c[:, cols].astype(f32)

            down_out[:, half * 1024 : half * 1024 + 1024] = total(0, 1024)
            pair[...] = total(1024, 2048)
            if half == 0:
                grad_in[0] = total(3072, 512)
                grad_in[1, :, 0:256] = total(3584, 256)
            else:
                grad_in[1, :, 256:512] = total(3072, 256)
                grad_in[2] = total(3328, 512)
            grad_out[:, half * 256 : half * 256 + 256] = total(3840, 256)
        sums_all = sums_ref[...]
        for row in range(4):
            mix[:, row * 512 : row * 512 + 512] = sums_all[row : row + 1]
            ffn[:, row * 512 : row * 512 + 512] = sums_all[4 + row : 5 + row]
        conv[...] = sums_all[8:11]

    return call(
        body,
        "finish",
        [*keeps, *cames, sums],
        [Free(((64, 2048), f32))] * 3
        + [Free(((3, 64, 512), f32)), Free(((64, 512), f32))]
        + [Free(((1, D), f32))] * 2
        + [Free(((3, 512), f32))],
        after=after,
    )


def to_next(value, axis, steps):
    count = lax.axis_size(axis)
    first, last = (max(0, -steps), min(count, count - steps))
    return lax.ppermute(value, axis, [(source, source + steps) for source in range(first, last)])


def around(value, steps):
    return lax.ppermute(value, "tp", [(source, (source + steps) % 4) for source in range(4)])


def scattered(pieces):
    far = around(pieces[1], 2)
    return [far, around(pieces[0], 1), around(pieces[2], 3)]


def gathered(shard):
    far = around(shard, 2)
    return [shard, around(shard, 3), far, around(shard, 1)]


def other_core(value):
    return lax.ppermute(value, "seq", CORE_PAIRS)


def exchange(stage, sends):
    return [lax.ppermute(send, "seq", stage_pairs(half, stage)) for half, send in enumerate(sends)]


def per_device(
    tokens, gain_mix, w_in, conv_weight, w_out, gain_ffn, w_gate, w_up, w_down, cotangent, lengths
):
    seq, z = lax.axis_index("seq"), lax.axis_index("tp")
    place = jnp.stack([z, seq, lax.rem(seq, 2)]).astype(jnp.int32)
    tokens = tokens.reshape(ROWS, D)
    cotangent = cotangent.reshape(ROWS, D)
    w_in = jnp.transpose(w_in, (1, 0, 2))

    first = project_in(
        place, lengths, tokens, gain_mix.reshape(1, D), gain_ffn.reshape(1, D), conv_weight, w_in, cotangent, w_out
    )
    tokens, gain_mix, gain_ffn, conv_weight, normed, b_gate, c_gate, x_part, q, tail = first[:10]
    grad_low, near_out, grad_turned, one_turned, turned = first[10:]
    carried = to_next(tail, "seq", 1)
    turned_other = other_core(turned)
    convolved, mixed, own, *pieces = project_out(
        place, q, carried, c_gate, conv_weight, near_out, after=[turned_other]
    )
    received = scattered(pieces)
    grad_act = activation_grad(grad_low, w_down)
    hidden, shard = residual_norm(place, own, received, tokens, gain_ffn, after=[grad_act])
    normed_two = gathered(shard)
    gates, ups = bring("bring_ffn", [w_gate, w_up], after=[grad_act])

    mid, normed_two = feed_forward(normed_two, gates, ups, grad_act, mixed)
    mid_other = other_core(mid)
    own, *pieces = feed_back(mid, gates, ups)
    received = scattered(pieces)

    two_turned, two_sent = turn(place, normed_two, after=[own])
    two_other = other_core(two_sent)
    keep_a, send_a = weight_grad(
        place,
        "weight_grad_a",
        1024,
        [[(grad_turned, turned_other, 0, mid, mid_other, 1024 * half, 1024)] for half in range(2)],
        after=[two_sent],
    )
    came_a = exchange(0, send_a)

    def weight_grad_b(part, after):
        return weight_grad(
            place,
            "weight_grad_b",
            1024,
            [
                [(two_turned, two_other, 0, mid, mid_other, 2048 + 2048 * half + 1024 * part, 1024)]
                for half in range(2)
            ],
            after=after,
        )

    keep_b, send_b = weight_grad_b(0, [send_a[0]])
    hidden_low, gain_part = hidden_grad(own, received, hidden, gain_ffn, grad_low, after=[send_b[0]])
    hidden_pieces = gathered(hidden_low)
    near_out, near_in = bring("bring_mixer", [w_out, w_in], after=[hidden_low])
    send_b = release("release_b", send_b, after=[*came_a, near_in])
    came_b = exchange(0, send_b)
    keep_d, send_d = weight_grad_b(1, [send_b[0]])
    own_out, *out_pieces = down(mid, w_down, after=[send_d[0]])

    dconv, dc, head, taps, hidden_turned, hidden_sent = mixed_grad(
        place, hidden_pieces, near_out, convolved, c_gate, q, carried, after=[near_in, own_out]
    )
    returned = to_next(head, "seq", -1)
    send_d = release("release_d", send_d, after=[*came_b, returned])
    came_d = exchange(0, send_d)
    hidden_other = other_core(hidden_sent)
    *dp, own, one, two, three, sums = input_grad(
        place, dconv, returned, dc, b_gate, x_part, conv_weight, near_in, tokens, gain_part, taps,
        after=[hidden_other, send_d[0]],
    )
    dp_other = [other_core(part) for part in dp]
    keep_c, send_c, sums = weight_grad(
        place,
        "weight_grad_c",
        1024,
        [
            [
                (one_turned, turned_other, 1024, dp[half], dp_other[half], 0, 768),
                (hidden_turned, hidden_other, 0, mid, mid_other, 6144 + 256 * half, 256),
            ]
            for half in range(2)
        ],
        sums=sums,
        after=[own],
    )
    pieces = release("release_z", [one, two, three], after=[*dp_other, send_c[0]])
    received = release("hold", scattered(pieces), weight=LONG)
    send_c = release("release_c", send_c, after=came_d)
    came_c = exchange(0, send_c)

    keep, send, sums = halve(
        "halve_abc",
        list(zip(keep_a, keep_b, keep_d, keep_c)),
        list(zip(came_a, came_b, came_d, came_c)),
        [(half, part, 0, 1024, half, 1024 * part) for half in range(2) for part in range(4)],
        2,
        sums=sums,
        after=received,
    )
    came = exchange(1, send)
    out_received = scattered(release("release_out", out_pieces, after=received))
    shards = last_shards(
        place, own, received, tokens, gain_mix, hidden_low, own_out, out_received, hidden, sums, after=[]
    )
    pieces = gathered(shards)
    grad_tokens, output, done = in_place(place, pieces, LONG)
    whole = [(half, 0, 0, 4096, half, 0) for half in range(2)]
    keep, send = halve("halve_d", [[k] for k in keep], [[c] for c in came], whole, 2, after=[shards])
    came = exchange(2, send)
    sums = sum_gains(sums, pieces, after=[send[0], done])
    keep, send = halve("halve_e", [[k] for k in keep], [[c] for c in came], whole, 2, after=[done])
    came = exchange(3, send)
    for stage in (1, 2, 3):
        sums = sum_over_stage(sums, stage, LONG if stage == 1 else 1, after=[send[0]])
    grad_down, grad_gate, grad_up, grad_in, grad_out, gain_mix_sum, gain_ffn_sum, conv_sum = finish(keep, came, sums)

    return (
        output.reshape(2, 128, D),
        grad_tokens.reshape(2, 128, D),
        gain_mix_sum.reshape(D),
        jnp.transpose(grad_in, (1, 0, 2)),
        conv_sum,
        grad_out.T,
        gain_ffn_sum.reshape(D),
        grad_gate,
        grad_up,
        grad_down.T,
    )


def solution(mesh):
    placed = (
        P(None, "seq", None),
        P(),
        P(None, None, "tp"),
        P(None, "tp"),
        P("tp", None),
        P(),
        P(None, "tp"),
        P(None, "tp"),
        P("tp", None),
        P(None, "seq", None),
        P(),
    )
    return jax.shard_map(
        per_device,
        mesh=mesh,
        in_specs=placed,
        out_specs=(
            P(None, "seq", None),
            P(None, "seq", None),
            P(),
            P("seq", None, "tp"),
            P(None, "tp"),
            P("tp", "seq"),
            P(),
            P("seq", "tp"),
            P("seq", "tp"),
            P("tp", "seq"),
        ),
        check_vma=False,
    )
```

```python
import jax
import jax.numpy as jnp
import numpy as np
from jax import lax
from jax.experimental import pallas as pl
from jax.experimental.pallas import tpu as pltpu
from jax.sharding import PartitionSpec as P

epsilon = 1e-05
f32 = jnp.float32
bf16 = jnp.bfloat16

ROWS = 256
PIECE = 64
D = 2048
MiB = 1 << 20

FLIP = {"a": (1, 0, 3, 2), "b": (3, 2, 1, 0)}
CODE = {0: (0, 0), 1: (1, 0), 2: (1, 1), 3: (0, 1)}
PLACE = {bits: at for at, bits in CODE.items()}
ORDER = (
    (("xa", "xb", "ya", "yb"), ("ya", "yb", "xa", "xb")),
    (("xb", "xa", "yb", "ya"), ("yb", "ya", "xb", "xa")),
)


def seq_index(x, y, core):
    return (x * 4 + y) * 2 + core


def flipped(x, y, dim):
    ring = FLIP[dim[1]]
    return (ring[x], y) if dim[0] == "x" else (x, ring[y])


def stage_pairs(half, stage):
    pairs = []
    for x in range(4):
        for y in range(4):
            for core in range(2):
                to = flipped(x, y, ORDER[half][core][stage])
                pairs.append((seq_index(x, y, core), seq_index(*to, core)))
    return pairs


CORE_PAIRS = [(i, i ^ 1) for i in range(32)]


FULL = pl.BlockSpec(memory_space=pltpu.VMEM)
FAR = pl.BlockSpec(memory_space=pl.ANY)
NUMBERS = pl.BlockSpec(memory_space=pltpu.SMEM)


class Far:
    def __init__(self, array):
        self.array = array


class Free:
    def __init__(self, array):
        self.array = array


def size(shape, kind):
    return int(np.prod(shape)) * jnp.dtype(kind).itemsize


def call(body, name, ins, outs, numbers=(), scratch=(), after=(), more=4, weight=1):
    room = more * MiB
    operands, specs = list(numbers), [NUMBERS] * len(numbers)
    for array in ins:
        if isinstance(array, Far):
            operands.append(pltpu.with_memory_space_constraint(array.array, pltpu.HBM))
            specs.append(FAR)
        else:
            operands.append(pltpu.with_memory_space_constraint(array, pltpu.VMEM))
            specs.append(FULL)
    count = len(operands)
    shapes = []
    for out in outs:
        if isinstance(out, Free):
            room += size(*out.array)
            shapes.append(jax.ShapeDtypeStruct(*out.array))
        else:
            shapes.append(pltpu.VMEM(*out))
    for kept in scratch:
        if kept.memory_space == pltpu.VMEM:
            room += size(kept.inner_aval.shape, kept.inner_aval.dtype)

    def run(*refs):
        body(*refs[:count], *refs[count + len(after) :])

    return pl.pallas_call(
        run,
        in_specs=specs + [FAR] * len(after),
        out_specs=[FULL] * len(outs),
        out_shape=shapes,
        scratch_shapes=list(scratch),
        compiler_params=pltpu.CompilerParams(vmem_limit_bytes=int(room)),
        cost_estimate=pl.CostEstimate(flops=weight, bytes_accessed=1, transcendentals=0),
        name=name,
    )(*operands, *after)


def matmul(left, right):
    return lax.dot_general(left, right, (((1,), (0,)), ((), ())), preferred_element_type=f32)


def matmul_t(left, right):
    return lax.dot_general(left, right, (((1,), (1,)), ((), ())), preferred_element_type=f32)


def normalize(values):
    return lax.rsqrt(jnp.mean(values * values, -1, keepdims=True) + epsilon)


def spans(total, each):
    return [slice(at, at + each) for at in range(0, total, each)]


def rotated(z, piece):
    return pl.multiple_of(lax.rem(z + piece, 4) * PIECE, PIECE)


PIECE_OUTS = [((PIECE, D), f32)] + [((PIECE, D), bf16)] * 3


def cut(total, own, one, two, three, cols=slice(None)):
    own[:, cols] = total[0:64]
    one[:, cols] = total[64:128].astype(bf16)
    two[:, cols] = total[128:192].astype(bf16)
    three[:, cols] = total[192:256].astype(bf16)


def added(own, r1, r2, r3):
    return own + (r1.astype(f32) + r2.astype(f32) + r3.astype(f32))


def release(name, arrays, after=(), weight=1):
    count = len(arrays)
    return pl.pallas_call(
        lambda *refs: None,
        in_specs=[FAR] * (count + len(after)),
        out_specs=[FAR] * count,
        out_shape=[jax.ShapeDtypeStruct(array.shape, array.dtype) for array in arrays],
        input_output_aliases={n: n for n in range(count)},
        compiler_params=pltpu.CompilerParams(vmem_limit_bytes=MiB),
        cost_estimate=pl.CostEstimate(flops=weight, bytes_accessed=1, transcendentals=0),
        name=name,
    )(*arrays, *after)


LONG = 4 * 10**10


class Stream:
    def __init__(self, copies, depth=3):
        self.copies, self.started = copies, 0
        for _ in range(depth):
            self.more()

    def more(self):
        if self.started < len(self.copies):
            self.copies[self.started].start()
            self.started += 1

    def wait(self, n):
        self.copies[n].wait()
        self.more()


SUMS = (16, 512)


def pack(to, row, sums):
    high = sums.astype(bf16)
    to[row : row + 16, 0:512] = high
    to[row : row + 16, 512:1024] = (sums - high.astype(f32)).astype(bf16)


def unpack(came, row):
    return came[row : row + 16, 0:512].astype(f32) + came[row : row + 16, 512:1024].astype(f32)


def block_at(at, half, position):
    core, seq = at[2], at[1]
    owner = []
    for axis, here in (("x", seq // 8), ("y", lax.rem(seq // 2, 4))):
        flips = {"a": 0, "b": 0}
        for stage in range(4):
            if (position >> (3 - stage)) & 1:
                dims = [ORDER[half][n][stage] for n in range(2)]
                for n, dim in enumerate(dims):
                    if dim[0] == axis:
                        flips[dim[1]] = flips[dim[1]] + (core if n else 1 - core)
        a = lax.rem(lax.rem((here + 1) // 2, 2) + flips["a"], 2)
        b = lax.rem(here // 2 + flips["b"], 2)
        owner.append(2 * b + lax.rem(a + b, 2))
    return 4 * owner[0] + owner[1]


def turn_into(core, flat, mine, other, base=0):
    for block in range(16):
        rows = slice(block * 64, block * 64 + 64)
        mine[rows] = flat[pl.ds(pl.multiple_of(block * 128 + core * 64, 64), 64)]
        other[base + block * 64 : base + block * 64 + 64] = flat[
            pl.ds(pl.multiple_of(block * 128 + (1 - core) * 64, 64), 64)
        ]


def project_in(place, tokens, gain_mix, gain_ffn, conv_weight, w_in, w_out):
    order = (0, 2, 1)

    def body(at, tok_far, mix_far, ffn_far, conv_far, w_far, out_far, *refs):
        tok, mix, ffn, conv, normed, b_out, c_out, v_out, q_out, tail, w_o, w, sems = refs
        small = [
            pltpu.make_async_copy(far, near, sems.at[n])
            for n, (far, near) in enumerate(((tok_far, tok), (mix_far, mix), (ffn_far, ffn), (conv_far, conv)))
        ]
        for copy in small:
            copy.start()
        copies = [pltpu.make_async_copy(w_far.at[part], w.at[part], sems.at[4 + part]) for part in order]
        stream = Stream(copies + [pltpu.make_async_copy(out_far, w_o, sems.at[7])], 2)
        for copy in small:
            copy.wait()
        values = tok[...].astype(f32)
        normed[...] = (values * normalize(values) * mix[...]).astype(bf16)
        for n, part in enumerate(order):
            stream.wait(n)
            (b_out, c_out, v_out)[part][...] = matmul(normed[...], w[part])
            if part == 2:
                q = (b_out[...] * v_out[...]).astype(bf16)
                q_out[...] = q
                tail[0] = q[112:128].astype(f32)[8:16]
                tail[1] = q[240:256].astype(f32)[8:16]
        stream.wait(3)

    return call(
        body,
        "project_in",
        [Far(tokens), Far(gain_mix), Far(gain_ffn), Far(conv_weight), Far(w_in), Far(w_out)],
        [
            ((ROWS, D), bf16),
            ((1, D), f32),
            ((1, D), f32),
            ((3, 512), f32),
            ((ROWS, D), bf16),
            ((ROWS, 512), f32),
            ((ROWS, 512), f32),
            ((ROWS, 512), f32),
            ((ROWS, 512), bf16),
            ((2, 8, 512), f32),
            ((512, D), bf16),
        ],
        numbers=[place],
        scratch=[pltpu.VMEM((3, D, 512), bf16), pltpu.SemaphoreType.DMA((8,))],
    )


def prepare(place, lengths, cotangent, normed, after):
    def body(at, cot_far, len_far, one, out, grad_mine, one_mine, other, cot, flat, len_ref, sems):
        z, position, core = at[0], at[1] * 128, at[2]
        copies = [pltpu.make_async_copy(cot_far, cot, sems.at[0]), pltpu.make_async_copy(len_far, len_ref, sems.at[1])]
        for copy in copies:
            copy.start()
        flat[...] = one[...].T
        turn_into(core, flat, one_mine, other, 1024)
        for copy in copies:
            copy.wait()
        for piece in range(4):
            block = lax.rem(z + piece, 4)
            seq, half = block // 2, lax.rem(block, 2)
            first = position + half * PIECE
            rows = first + lax.broadcasted_iota(jnp.int32, (PIECE, D), 0)
            values = cot[pl.ds(rotated(z, piece), PIECE)].astype(f32)
            out[piece * PIECE : (piece + 1) * PIECE] = jnp.where(rows < len_ref[seq], values, 0.0).astype(bf16)
        flat[...] = out[...].T
        turn_into(core, flat, grad_mine, other, 0)

    return call(
        body,
        "prepare",
        [Far(cotangent), Far(lengths), normed],
        [((ROWS, D), bf16), ((1024, ROWS), bf16), ((1024, ROWS), bf16), ((2048, ROWS), bf16)],
        numbers=[place],
        scratch=[
            pltpu.VMEM((ROWS, D), bf16),
            pltpu.VMEM((D, ROWS), bf16),
            pltpu.SMEM((2,), jnp.int32),
            pltpu.SemaphoreType.DMA((2,)),
        ],
        after=after,
    )


def project_out(place, q, carried, c_gate, conv_weight, w_out, after):
    def body(at, q_ref, carried_ref, c_ref, cw, w, conv_out, y_out, own, one, two, three, pad):
        z = at[0]
        for seq in range(2):
            rows = slice(seq * 128, seq * 128 + 128)
            pad[0:8] = carried_ref[seq]
            pad[8:136] = q_ref[rows].astype(f32)
            conv_out[rows] = cw[0:1] * pad[6:134] + cw[1:2] * pad[7:135] + cw[2:3] * pad[8:136]
        for piece in range(4):
            start = rotated(z, piece)
            y_out[piece * PIECE : (piece + 1) * PIECE] = (
                c_ref[pl.ds(start, PIECE)] * conv_out[pl.ds(start, PIECE)]
            ).astype(bf16)
        for cols in spans(D, 512):
            cut(matmul(y_out[...], w[:, cols]), own, one, two, three, cols)

    return call(
        body,
        "project_out",
        [q, carried, c_gate, conv_weight, w_out],
        [((ROWS, 512), f32), ((ROWS, 512), bf16)] + PIECE_OUTS,
        numbers=[place],
        scratch=[pltpu.VMEM((136, 512), f32)],
        after=after,
    )


def activation_grad(grad_low, w_down):
    def body(grad, w_far, out, w, sems):
        stream = Stream(
            [
                pltpu.make_async_copy(w_far.at[rows], w.at[rows], sems.at[n])
                for n, rows in enumerate(spans(2048, 512))
            ]
        )
        for n, rows in enumerate(spans(2048, 512)):
            stream.wait(n)
            out[:, rows] = matmul_t(grad[...], w[rows])

    return call(
        body,
        "activation_grad",
        [grad_low, Far(w_down)],
        [((ROWS, 2048), f32)],
        scratch=[pltpu.VMEM((2048, D), bf16), pltpu.SemaphoreType.DMA((4,))],
    )[0]


def residual_norm(place, own, received, tokens, gain, after):
    def body(at, own_ref, r1, r2, r3, tok, gain_ref, hidden, normed):
        values = tok[pl.ds(rotated(at[0], 0), PIECE)].astype(f32) + added(own_ref[...], r1[...], r2[...], r3[...])
        hidden[...] = values
        normed[...] = (values * normalize(values) * gain_ref[...]).astype(bf16)

    return call(
        body,
        "residual_norm",
        [own, *received, tokens, gain],
        [((PIECE, D), f32), ((PIECE, D), bf16)],
        numbers=[place],
        after=after,
    )


def bring(name, weights, after=()):
    count = len(weights)

    def body(*refs):
        copies = [pltpu.make_async_copy(refs[n], refs[count + n], refs[-1].at[n]) for n in range(count)]
        for copy in copies:
            copy.start()
        for copy in copies:
            copy.wait()

    return call(
        body,
        name,
        [Far(weight) for weight in weights],
        [(weight.shape, weight.dtype) for weight in weights],
        scratch=[pltpu.SemaphoreType.DMA((count,))],
        after=after,
        more=1,
    )


def feed_forward(pieces, w_gate, w_up, grad_act, mixed, after):
    def body(n0, n1, n2, n3, gates, ups, ga, mix, mid, normed):
        for piece, ref in enumerate((n0, n1, n2, n3)):
            normed[piece * PIECE : (piece + 1) * PIECE] = ref[...]
        mid[:, 6144:6656] = mix[...]
        for cols in spans(2048, 256):
            gate = matmul(normed[...], gates[:, cols])
            up = matmul(normed[...], ups[:, cols])
            sigma = jax.nn.sigmoid(gate)
            swish = gate * sigma
            grad = ga[:, cols]
            first = cols.start
            mid[:, cols] = (swish * up).astype(bf16)
            mid[:, 2048 + first : 2304 + first] = (grad * up * sigma * (1.0 + gate * (1.0 - sigma))).astype(bf16)
            mid[:, 4096 + first : 4352 + first] = (grad * swish).astype(bf16)

    return call(
        body,
        "feed_forward",
        [*pieces, w_gate, w_up, grad_act, mixed],
        [((ROWS, 6656), bf16), ((ROWS, D), bf16)],
        after=after,
    )


def turn(place, value, after=()):
    def body(at, tall, mine, other, flat):
        flat[...] = tall[...].T
        turn_into(at[2], flat, mine, other)

    return call(
        body,
        "turn",
        [value],
        [((1024, ROWS), bf16), ((1024, ROWS), bf16)],
        numbers=[place],
        scratch=[pltpu.VMEM((D, ROWS), bf16)],
        after=after,
    )


def feed_back(mid, w_gate, w_up, after=()):
    def body(mid_ref, gates, ups, own, one, two, three):
        for rows in spans(D, 256):
            total = matmul_t(mid_ref[:, 2048:4096], gates[rows]) + matmul_t(mid_ref[:, 4096:6144], ups[rows])
            cut(total, own, one, two, three, rows)

    return call(body, "feed_back", [mid, w_gate, w_up], PIECE_OUTS, after=after)


def down(mid, w_down, after=()):
    def body(mid_ref, w_far, own, one, two, three, w, sems):
        stream = Stream(
            [
                pltpu.make_async_copy(w_far.at[:, cols], w.at[:, cols], sems.at[n])
                for n, cols in enumerate(spans(D, 512))
            ]
        )
        for n, cols in enumerate(spans(D, 512)):
            stream.wait(n)
            cut(matmul(mid_ref[:, 0:2048], w[:, cols]), own, one, two, three, cols)

    return call(
        body,
        "down",
        [mid, Far(w_down)],
        PIECE_OUTS,
        scratch=[pltpu.VMEM((2048, D), bf16), pltpu.SemaphoreType.DMA((4,))],
        after=after,
    )


def hidden_grad(own, received, hidden, gain, grad_low, after):
    def body(own_ref, r1, r2, r3, h, gain_ref, grad, out, gain_part):
        total = added(own_ref[...], r1[...], r2[...], r3[...])
        values = h[...]
        rate = normalize(values)
        unit = values * rate
        gain_part[...] = jnp.sum(total * unit, axis=0, keepdims=True)
        scaled = total * gain_ref[...]
        inner = jnp.mean(scaled * unit, -1, keepdims=True)
        out[...] = (grad[0:PIECE].astype(f32) + rate * (scaled - unit * inner)).astype(bf16)

    return call(
        body,
        "hidden_grad",
        [own, *received, hidden, gain, grad_low],
        [((PIECE, D), bf16), ((1, D), f32)],
        after=after,
        weight=LONG,
    )


def mixed_grad(place, pieces, w_out, convolved, c_gate, q, carried, after):
    def body(at, h0, h1, h2, h3, w, conv, c_ref, q_ref, carried_ref, dconv, dc, head, taps, mine, other, hidden, tall, pad, flat):
        z = at[0]
        for piece, ref in enumerate((h0, h1, h2, h3)):
            hidden[pl.ds(rotated(z, piece), PIECE)] = ref[...]
            tall[piece * PIECE : (piece + 1) * PIECE] = ref[...]
        for cols in spans(512, 256):
            mixed = matmul_t(hidden[...], w[cols])
            dc[:, cols] = (mixed * conv[:, cols]).astype(bf16)
            dconv[:, cols] = mixed * c_ref[:, cols]
        flat[...] = tall[...].T
        turn_into(at[2], flat, mine, other)
        sums = []
        for seq in range(2):
            rows = slice(seq * 128, seq * 128 + 128)
            head[seq] = dconv[seq * 128 : seq * 128 + 8]
            pad[0:8] = carried_ref[seq]
            pad[8:136] = q_ref[rows].astype(f32)
            here = dconv[rows]
            sums.append([jnp.sum(here * pad[6 + tap : 134 + tap], axis=0, keepdims=True) for tap in range(3)])
        for tap in range(3):
            taps[tap : tap + 1] = sums[0][tap] + sums[1][tap]

    return call(
        body,
        "mixed_grad",
        [*pieces, w_out, convolved, c_gate, q, carried],
        [
            ((ROWS, 512), f32),
            ((ROWS, 512), bf16),
            ((2, 8, 512), f32),
            ((3, 512), f32),
            ((1024, ROWS), bf16),
            ((1024, ROWS), bf16),
        ],
        numbers=[place],
        scratch=[
            pltpu.VMEM((ROWS, D), bf16),
            pltpu.VMEM((ROWS, D), bf16),
            pltpu.VMEM((136, 512), f32),
            pltpu.VMEM((D, ROWS), bf16),
        ],
        after=after,
        weight=LONG,
    )


def input_grad(place, dconv, returned, dc, b_gate, x_part, conv_weight, w_in, tokens, gain_part, taps, after):
    def body(at, dk, ret, dc_ref, b, v, cw, w, tok, gains, taps_ref, dp0, dp1, own, one, two, three, sums, pad, total, dp):
        z = at[0]
        for seq in range(2):
            rows = slice(seq * 128, seq * 128 + 128)
            pad[0:128] = dk[rows]
            pad[128:136] = ret[seq]
            dq = cw[2:3] * pad[0:128] + cw[1:2] * pad[1:129] + cw[0:1] * pad[2:130]
            dp[rows, 0:512] = (dq * v[rows]).astype(bf16)
            dp[rows, 512:1024] = dc_ref[rows]
            dp[rows, 1024:1536] = (dq * b[rows]).astype(bf16)
        rate = normalize(tok[...].astype(f32))
        sums[...] = jnp.zeros(SUMS, f32)
        for cols in spans(D, 256):
            part = (
                matmul_t(dp[:, 0:512], w[0, cols])
                + matmul_t(dp[:, 512:1024], w[1, cols])
                + matmul_t(dp[:, 1024:1536], w[2, cols])
            )
            row, first = cols.start // 512, cols.start % 512
            sums[row : row + 1, first : first + 256] = jnp.sum(
                part * (tok[:, cols].astype(f32) * rate), axis=0, keepdims=True
            )
            total[...] = part
            own[:, cols] = total[pl.ds(rotated(z, 0), PIECE)]
            one[:, cols] = total[pl.ds(rotated(z, 1), PIECE)].astype(bf16)
            two[:, cols] = total[pl.ds(rotated(z, 2), PIECE)].astype(bf16)
            three[:, cols] = total[pl.ds(rotated(z, 3), PIECE)].astype(bf16)
        for row in range(4):
            sums[4 + row : 5 + row] = gains[:, row * 512 : row * 512 + 512]
        sums[8:11] = taps_ref[...]
        dp0[...] = dp[:, 0:768]
        dp1[0:ROWS] = dp[:, 768:1536]
        high = sums[...].astype(bf16)
        dp1[ROWS : ROWS + 16, 0:512] = high
        dp1[ROWS + 16 : ROWS + 32, 0:512] = (sums[...] - high.astype(f32)).astype(bf16)

    return call(
        body,
        "input_grad",
        [dconv, returned, dc, b_gate, x_part, conv_weight, w_in, tokens, gain_part, taps],
        [((ROWS, 768), bf16), ((ROWS + 32, 768), bf16)] + PIECE_OUTS + [(SUMS, f32)],
        numbers=[place],
        scratch=[pltpu.VMEM((136, 512), f32), pltpu.VMEM((ROWS, 256), f32), pltpu.VMEM((ROWS, 1536), bf16)],
        after=after,
    )


def last_shards(place, own, received, tokens, gain, grad_hidden, own_out, out_received, hidden, sums, after=()):
    def body(at, own_ref, r1, r2, r3, tok, gain_ref, grad, own_o, o1, o2, o3, h, sums_ref, out):
        rows = slice(0, PIECE)
        total = added(own_ref[...], r1[...], r2[...], r3[...])
        values = tok[pl.ds(rotated(at[0], 0), PIECE)].astype(f32)
        rate = normalize(values)
        unit = values * rate
        scaled = total * gain_ref[...]
        inner = jnp.mean(scaled * unit, -1, keepdims=True)
        out[rows] = (grad[...].astype(f32) + rate * (scaled - unit * inner)).astype(bf16)
        out[PIECE : 2 * PIECE] = (h[...] + added(own_o[...], o1[...], o2[...], o3[...])).astype(bf16)
        pack(out, 2 * PIECE, sums_ref[...])

    return call(
        body,
        "last_shards",
        [own, *received, tokens, gain, grad_hidden, own_out, *out_received, hidden, sums],
        [((2 * PIECE + 16, D), bf16)],
        numbers=[place],
        after=after,
        weight=LONG,
    )[0]


def in_place(place, pieces, weight=1, after=()):
    def body(at, p0, p1, p2, p3, grad, out, done):
        for piece, ref in enumerate((p0, p1, p2, p3)):
            rows = pl.ds(rotated(at[0], piece), PIECE)
            grad[rows] = ref[0:PIECE]
            out[rows] = ref[PIECE : 2 * PIECE]
        done[...] = jnp.zeros((8, 128), f32)

    return call(
        body,
        "in_place",
        [*pieces],
        [Free(((ROWS, D), bf16))] * 2 + [((8, 128), f32)],
        numbers=[place],
        after=after,
        weight=weight,
    )


def weight_grad(place, name, width, plan, sums=None, after=()):
    flat = [part for half in plan for part in half]
    arrays = []
    for mine, other, _, right_mine, right_other, _, _ in flat:
        for array in (mine, other, right_mine, right_other):
            if not any(array is known for known in arrays):
                arrays.append(array)
    count = len(arrays) + (sums is not None)

    def body(order, *refs):
        def ref(array):
            return refs[[known is array for known in arrays].index(True)]

        outs = refs[count : count + 4]
        left, right = refs[-2:]
        if sums is not None:
            came = ref(plan[1][0][4])
            total = refs[count - 1][...] + came[256:272, 0:512].astype(f32) + came[272:288, 0:512].astype(f32)
            refs[count + 4][...] = total
            pack(outs[1], 512, total)
        for half in range(2):
            keep, send = outs[2 * half : 2 * half + 2]
            to = 0
            for mine, other, base, right_mine, right_other, first, columns in plan[half]:
                mine, other, right_mine, right_other = map(ref, (mine, other, right_mine, right_other))
                for position in range(16):
                    start = block_at(order, half, position) * 64
                    rows = slice(position * 64, position * 64 + 64)
                    left[rows, 0:256] = mine[pl.ds(pl.multiple_of(start, 64), 64)]
                    left[rows, 256:512] = other[pl.ds(pl.multiple_of(base + start, 64), 64)]
                for step, cols in enumerate(spans(columns, 256)):
                    at = slice(first + cols.start, first + cols.stop)
                    room = right.at[step % 2]
                    room[0:256] = right_mine[0:256, at]
                    room[256:512] = right_other[0:256, at]
                    to_cols = slice(to + cols.start, to + cols.stop)
                    total = matmul(left[...], room[...]).astype(bf16)
                    keep[:, to_cols] = total[0:512]
                    send[0:512, to_cols] = total[512:1024]
                to += columns

    shapes = [((512, width), bf16)] * 4
    if sums is not None:
        shapes = [shapes[0], ((528, width), bf16), *shapes[2:], (SUMS, f32)]
    keep0, send0, keep1, send1, *total = call(
        body,
        name,
        arrays + ([] if sums is None else [sums]),
        shapes,
        numbers=[place],
        scratch=[pltpu.VMEM((1024, 512), bf16), pltpu.VMEM((2, 512, 256), bf16)],
        after=after,
    )
    return [keep0, keep1], [send0, send1], *total


def halve(name, keeps, cames, moves, outs, sums=None, along=False, after=()):
    counts = [len(keep) for keep in keeps]
    ins = [array for keep, came in zip(keeps, cames) for array in (*keep, *came)]
    starts = [2 * sum(counts[:n]) for n in range(len(counts))]
    rows = keeps[0][0].shape[0]
    middle = rows // 2
    width = sum(move[3] for move in moves) // outs
    each = min(64, middle)
    extra = [] if sums is None else [sums]
    count = len(ins) + len(extra)

    def body(*refs):
        keep, send = refs[count : count + outs], refs[count + outs : count + 2 * outs]
        if sums is not None:
            total = refs[len(ins)][...]
            if rows < cames[0][-1].shape[0]:
                total = total + unpack(refs[2 * counts[0] - 1], rows)
            refs[count + 2 * outs][...] = total
            if along:
                pack(send[0], middle, total)

        @pl.loop(0, middle // each)
        def _(step):
            low = pl.ds(pl.multiple_of(step * each, each), each)
            high = pl.ds(pl.multiple_of(middle + step * each, each), each)
            for group, part, first, columns, out, to in moves:
                k, c = refs[starts[group] + part], refs[starts[group] + counts[group] + part]
                take, put = slice(first, first + columns), slice(to, to + columns)
                keep[out][low, put] = k[low, take] + c[low, take]
                send[out][low, put] = k[high, take] + c[high, take]

    sends = [((middle + 16 * (along and n == 0), width), bf16) for n in range(outs)]
    shapes = [((middle, width), bf16)] * outs + sends + ([] if sums is None else [(SUMS, f32)])
    results = call(body, name, ins + extra, shapes, after=after)
    return results[:outs], results[outs : 2 * outs], *results[2 * outs :]


def sum_gains(own, pieces, after):
    def body(sums, r1, r2, r3, out):
        out[...] = sums[...]
        out[0:8] = (sums[0:8] + unpack(r1, 128)[0:8]) + (unpack(r2, 128)[0:8] + unpack(r3, 128)[0:8])

    return call(body, "sum_gains", [own, *pieces[1:]], [(SUMS, f32)], after=after)[0]


def sum_over_stage(value, stage, weight=1, after=()):
    def body(a, b, out):
        out[...] = a[...] + b[...]

    came = lax.ppermute(value, "seq", stage_pairs(0, stage))
    return call(body, "sum_stage", [value, came], [(SUMS, f32)], after=after, weight=weight)[0]


def finish(keeps, cames, sums, after=()):
    def body(k0, k1, c0, c1, sums_ref, down_out, gate, up, grad_in, grad_out, mix, ffn, conv):
        for half, (k, c, pair) in enumerate(((k0, c0, gate), (k1, c1, up))):

            def total(first, count, k=k, c=c):
                cols = slice(first, first + count)
                return k[:, cols].astype(f32) + c[:, cols].astype(f32)

            down_out[:, half * 1024 : half * 1024 + 1024] = total(0, 1024)
            pair[...] = total(1024, 2048)
            if half == 0:
                grad_in[0] = total(3072, 512)
                grad_in[1, :, 0:256] = total(3584, 256)
            else:
                grad_in[1, :, 256:512] = total(3072, 256)
                grad_in[2] = total(3328, 512)
            grad_out[:, half * 256 : half * 256 + 256] = total(3840, 256)
        sums_all = sums_ref[...]
        for row in range(4):
            mix[:, row * 512 : row * 512 + 512] = sums_all[row : row + 1]
            ffn[:, row * 512 : row * 512 + 512] = sums_all[4 + row : 5 + row]
        conv[...] = sums_all[8:11]

    return call(
        body,
        "finish",
        [*keeps, *cames, sums],
        [Free(((64, 2048), f32))] * 3
        + [Free(((3, 64, 512), f32)), Free(((64, 512), f32))]
        + [Free(((1, D), f32))] * 2
        + [Free(((3, 512), f32))],
        after=after,
    )


def to_next(value, axis, steps):
    count = lax.axis_size(axis)
    first, last = (max(0, -steps), min(count, count - steps))
    return lax.ppermute(value, axis, [(source, source + steps) for source in range(first, last)])


def around(value, steps):
    return lax.ppermute(value, "tp", [(source, (source + steps) % 4) for source in range(4)])


def scattered(pieces):
    far = around(pieces[1], 2)
    return [far, around(pieces[0], 1), around(pieces[2], 3)]


def gathered(shard):
    far = around(shard, 2)
    return [shard, around(shard, 3), far, around(shard, 1)]


def other_core(value):
    return lax.ppermute(value, "seq", CORE_PAIRS)


def exchange(stage, sends):
    return [lax.ppermute(send, "seq", stage_pairs(half, stage)) for half, send in enumerate(sends)]


def per_device(
    tokens, gain_mix, w_in, conv_weight, w_out, gain_ffn, w_gate, w_up, w_down, cotangent, lengths
):
    seq, z = lax.axis_index("seq"), lax.axis_index("tp")
    place = jnp.stack([z, seq, lax.rem(seq, 2)]).astype(jnp.int32)
    tokens = tokens.reshape(ROWS, D)
    cotangent = cotangent.reshape(ROWS, D)
    w_in = jnp.transpose(w_in, (1, 0, 2))

    tokens, gain_mix, gain_ffn, conv_weight, normed, b_gate, c_gate, x_part, q, tail, near_out = project_in(
        place, tokens, gain_mix.reshape(1, D), gain_ffn.reshape(1, D), conv_weight, w_in, w_out
    )
    carried = to_next(tail, "seq", 1)
    convolved, mixed, own, *pieces = project_out(place, q, carried, c_gate, conv_weight, near_out, after=[])
    received = scattered(pieces)
    grad_low, grad_turned, one_turned, turned = prepare(place, lengths, cotangent, normed, after=[own])
    grad_act = activation_grad(grad_low, w_down)
    hidden, shard = residual_norm(place, own, received, tokens, gain_ffn, after=[grad_act])
    (turned,) = release("release_turned", [turned], after=[shard])
    turned_other = other_core(turned)
    normed_two = gathered(shard)
    gates, ups = bring("bring_ffn", [w_gate, w_up], after=[grad_act])

    mid, normed_two = feed_forward(normed_two, gates, ups, grad_act, mixed, after=[turned_other])
    mid_other = other_core(mid)
    own, *pieces = feed_back(mid, gates, ups)
    received = scattered(pieces)

    two_turned, two_sent = turn(place, normed_two, after=[own])
    two_other = other_core(two_sent)
    keep_a, send_a = weight_grad(
        place,
        "weight_grad_a",
        1024,
        [[(grad_turned, turned_other, 0, mid, mid_other, 1024 * half, 1024)] for half in range(2)],
        after=[two_sent],
    )
    came_a = exchange(0, send_a)

    def weight_grad_b(part, after):
        return weight_grad(
            place,
            "weight_grad_b",
            1024,
            [
                [(two_turned, two_other, 0, mid, mid_other, 2048 + 2048 * half + 1024 * part, 1024)]
                for half in range(2)
            ],
            after=after,
        )

    keep_b, send_b = weight_grad_b(0, [send_a[0]])
    hidden_low, gain_part = hidden_grad(own, received, hidden, gain_ffn, grad_low, after=[send_b[0]])
    hidden_pieces = gathered(hidden_low)
    near_out, near_in = bring("bring_mixer", [w_out, w_in], after=[hidden_low])
    send_b = release("release_b", send_b, after=[*came_a, near_in])
    came_b = exchange(0, send_b)
    keep_d, send_d = weight_grad_b(1, [send_b[0]])
    own_out, *out_pieces = down(mid, w_down, after=[send_d[0]])

    dconv, dc, head, taps, hidden_turned, hidden_sent = mixed_grad(
        place, hidden_pieces, near_out, convolved, c_gate, q, carried, after=[near_in, own_out]
    )
    returned = to_next(head, "seq", -1)
    send_d = release("release_d", send_d, after=[*came_b, returned])
    came_d = exchange(0, send_d)
    hidden_other = other_core(hidden_sent)
    *dp, own, one, two, three, sums = input_grad(
        place, dconv, returned, dc, b_gate, x_part, conv_weight, near_in, tokens, gain_part, taps,
        after=[hidden_other, send_d[0]],
    )
    dp_other = [other_core(part) for part in dp]
    keep_c, send_c, sums = weight_grad(
        place,
        "weight_grad_c",
        1024,
        [
            [
                (one_turned, turned_other, 1024, dp[half], dp_other[half], 0, 768),
                (hidden_turned, hidden_other, 0, mid, mid_other, 6144 + 256 * half, 256),
            ]
            for half in range(2)
        ],
        sums=sums,
        after=[own],
    )
    pieces = release("release_z", [one, two, three], after=[*dp_other, send_c[0]])
    received = release("hold", scattered(pieces), weight=LONG)
    send_c = release("release_c", send_c, after=came_d)
    came_c = exchange(0, send_c)

    keep, send, sums = halve(
        "halve_abc",
        list(zip(keep_a, keep_b, keep_d, keep_c)),
        list(zip(came_a, came_b, came_d, came_c)),
        [(half, part, 0, 1024, half, 1024 * part) for half in range(2) for part in range(4)],
        2,
        sums=sums,
        after=received,
    )
    came = exchange(1, send)
    out_received = scattered(release("release_out", out_pieces, after=received))
    shards = last_shards(
        place, own, received, tokens, gain_mix, hidden_low, own_out, out_received, hidden, sums, after=[]
    )
    pieces = gathered(shards)
    grad_tokens, output, done = in_place(place, pieces, LONG)
    whole = [(half, 0, 0, 4096, half, 0) for half in range(2)]
    keep, send = halve("halve_d", [[k] for k in keep], [[c] for c in came], whole, 2, after=[shards])
    came = exchange(2, send)
    sums = sum_gains(sums, pieces, after=[send[0], done])
    keep, send = halve("halve_e", [[k] for k in keep], [[c] for c in came], whole, 2, after=[done])
    came = exchange(3, send)
    for stage in (1, 2, 3):
        sums = sum_over_stage(sums, stage, LONG if stage == 1 else 1, after=[send[0]])
    grad_down, grad_gate, grad_up, grad_in, grad_out, gain_mix_sum, gain_ffn_sum, conv_sum = finish(keep, came, sums)

    return (
        output.reshape(2, 128, D),
        grad_tokens.reshape(2, 128, D),
        gain_mix_sum.reshape(D),
        jnp.transpose(grad_in, (1, 0, 2)),
        conv_sum,
        grad_out.T,
        gain_ffn_sum.reshape(D),
        grad_gate,
        grad_up,
        grad_down.T,
    )


def solution(mesh):
    placed = (
        P(None, "seq", None),
        P(),
        P(None, None, "tp"),
        P(None, "tp"),
        P("tp", None),
        P(),
        P(None, "tp"),
        P(None, "tp"),
        P("tp", None),
        P(None, "seq", None),
        P(),
    )
    return jax.shard_map(
        per_device,
        mesh=mesh,
        in_specs=placed,
        out_specs=(
            P(None, "seq", None),
            P(None, "seq", None),
            P(),
            P("seq", None, "tp"),
            P(None, "tp"),
            P("tp", "seq"),
            P(),
            P("seq", "tp"),
            P("seq", "tp"),
            P("tp", "seq"),
        ),
        check_vma=False,
    )
```

```python
import jax
import jax.numpy as jnp
import numpy as np
from jax import lax
from jax.experimental import pallas as pl
from jax.experimental.pallas import tpu as pltpu
from jax.sharding import PartitionSpec as P

epsilon = 1e-05
f32 = jnp.float32
bf16 = jnp.bfloat16

ROWS = 256
PIECE = 64
D = 2048
MiB = 1 << 20

FLIP = {"a": (1, 0, 3, 2), "b": (3, 2, 1, 0)}
CODE = {0: (0, 0), 1: (1, 0), 2: (1, 1), 3: (0, 1)}
PLACE = {bits: at for at, bits in CODE.items()}
ORDER = (
    (("xa", "xb", "ya", "yb"), ("ya", "yb", "xa", "xb")),
    (("xb", "xa", "yb", "ya"), ("yb", "ya", "xb", "xa")),
)


def seq_index(x, y, core):
    return (x * 4 + y) * 2 + core


def flipped(x, y, dim):
    ring = FLIP[dim[1]]
    return (ring[x], y) if dim[0] == "x" else (x, ring[y])


def stage_pairs(half, stage):
    pairs = []
    for x in range(4):
        for y in range(4):
            for core in range(2):
                to = flipped(x, y, ORDER[half][core][stage])
                pairs.append((seq_index(x, y, core), seq_index(*to, core)))
    return pairs


CORE_PAIRS = [(i, i ^ 1) for i in range(32)]


FULL = pl.BlockSpec(memory_space=pltpu.VMEM)
FAR = pl.BlockSpec(memory_space=pl.ANY)
NUMBERS = pl.BlockSpec(memory_space=pltpu.SMEM)


class Far:
    def __init__(self, array):
        self.array = array


class Free:
    def __init__(self, array):
        self.array = array


def size(shape, kind):
    return int(np.prod(shape)) * jnp.dtype(kind).itemsize


def call(body, name, ins, outs, numbers=(), scratch=(), after=(), more=4, weight=1):
    room = more * MiB
    operands, specs = list(numbers), [NUMBERS] * len(numbers)
    for array in ins:
        if isinstance(array, Far):
            operands.append(pltpu.with_memory_space_constraint(array.array, pltpu.HBM))
            specs.append(FAR)
        else:
            operands.append(pltpu.with_memory_space_constraint(array, pltpu.VMEM))
            specs.append(FULL)
    count = len(operands)
    shapes = []
    for out in outs:
        if isinstance(out, Free):
            room += size(*out.array)
            shapes.append(jax.ShapeDtypeStruct(*out.array))
        else:
            shapes.append(pltpu.VMEM(*out))
    for kept in scratch:
        if kept.memory_space == pltpu.VMEM:
            room += size(kept.inner_aval.shape, kept.inner_aval.dtype)

    def run(*refs):
        body(*refs[:count], *refs[count + len(after) :])

    return pl.pallas_call(
        run,
        in_specs=specs + [FAR] * len(after),
        out_specs=[FULL] * len(outs),
        out_shape=shapes,
        scratch_shapes=list(scratch),
        compiler_params=pltpu.CompilerParams(vmem_limit_bytes=int(room)),
        cost_estimate=pl.CostEstimate(flops=weight, bytes_accessed=1, transcendentals=0),
        name=name,
    )(*operands, *after)


def matmul(left, right):
    return lax.dot_general(left, right, (((1,), (0,)), ((), ())), preferred_element_type=f32)


def matmul_t(left, right):
    return lax.dot_general(left, right, (((1,), (1,)), ((), ())), preferred_element_type=f32)


def normalize(values):
    return lax.rsqrt(jnp.mean(values * values, -1, keepdims=True) + epsilon)


def spans(total, each):
    return [slice(at, at + each) for at in range(0, total, each)]


def rotated(z, piece):
    return pl.multiple_of(lax.rem(z + piece, 4) * PIECE, PIECE)


PIECE_OUTS = [((PIECE, D), f32)] + [((PIECE, D), bf16)] * 3


def cut(total, own, one, two, three, cols=slice(None)):
    own[:, cols] = total[0:64]
    one[:, cols] = total[64:128].astype(bf16)
    two[:, cols] = total[128:192].astype(bf16)
    three[:, cols] = total[192:256].astype(bf16)


def added(own, r1, r2, r3):
    return own + (r1.astype(f32) + r2.astype(f32) + r3.astype(f32))


def release(name, arrays, after=(), weight=1):
    count = len(arrays)
    return pl.pallas_call(
        lambda *refs: None,
        in_specs=[FAR] * (count + len(after)),
        out_specs=[FAR] * count,
        out_shape=[jax.ShapeDtypeStruct(array.shape, array.dtype) for array in arrays],
        input_output_aliases={n: n for n in range(count)},
        compiler_params=pltpu.CompilerParams(vmem_limit_bytes=MiB),
        cost_estimate=pl.CostEstimate(flops=weight, bytes_accessed=1, transcendentals=0),
        name=name,
    )(*arrays, *after)


LONG = 4 * 10**10


class Stream:
    def __init__(self, copies, depth=3):
        self.copies, self.started = copies, 0
        for _ in range(depth):
            self.more()

    def more(self):
        if self.started < len(self.copies):
            self.copies[self.started].start()
            self.started += 1

    def wait(self, n):
        self.copies[n].wait()
        self.more()


SUMS = (16, 512)


def pack(to, row, sums):
    high = sums.astype(bf16)
    to[row : row + 16, 0:512] = high
    to[row : row + 16, 512:1024] = (sums - high.astype(f32)).astype(bf16)


def unpack(came, row):
    return came[row : row + 16, 0:512].astype(f32) + came[row : row + 16, 512:1024].astype(f32)


def block_at(at, half, position):
    core, seq = at[2], at[1]
    owner = []
    for axis, here in (("x", seq // 8), ("y", lax.rem(seq // 2, 4))):
        flips = {"a": 0, "b": 0}
        for stage in range(4):
            if (position >> (3 - stage)) & 1:
                dims = [ORDER[half][n][stage] for n in range(2)]
                for n, dim in enumerate(dims):
                    if dim[0] == axis:
                        flips[dim[1]] = flips[dim[1]] + (core if n else 1 - core)
        a = lax.rem(lax.rem((here + 1) // 2, 2) + flips["a"], 2)
        b = lax.rem(here // 2 + flips["b"], 2)
        owner.append(2 * b + lax.rem(a + b, 2))
    return 4 * owner[0] + owner[1]


def turn_into(core, flat, mine, other, base=0):
    for block in range(16):
        rows = slice(block * 64, block * 64 + 64)
        mine[rows] = flat[pl.ds(pl.multiple_of(block * 128 + core * 64, 64), 64)]
        other[base + block * 64 : base + block * 64 + 64] = flat[
            pl.ds(pl.multiple_of(block * 128 + (1 - core) * 64, 64), 64)
        ]


def project_in(place, tokens, gain_mix, gain_ffn, conv_weight, w_in, w_out):
    order = (0, 2, 1)

    def body(at, tok_far, mix_far, ffn_far, conv_far, w_far, out_far, *refs):
        tok, mix, ffn, conv, normed, b_out, c_out, v_out, q_out, tail, w_o, w, sems = refs
        small = [
            pltpu.make_async_copy(far, near, sems.at[n])
            for n, (far, near) in enumerate(((tok_far, tok), (mix_far, mix), (ffn_far, ffn), (conv_far, conv)))
        ]
        for copy in small:
            copy.start()
        copies = [pltpu.make_async_copy(w_far.at[part], w.at[part], sems.at[4 + part]) for part in order]
        stream = Stream(copies + [pltpu.make_async_copy(out_far, w_o, sems.at[7])], 2)
        for copy in small:
            copy.wait()
        values = tok[...].astype(f32)
        normed[...] = (values * normalize(values) * mix[...]).astype(bf16)
        for n, part in enumerate(order):
            stream.wait(n)
            (b_out, c_out, v_out)[part][...] = matmul(normed[...], w[part])
            if part == 2:
                q = (b_out[...] * v_out[...]).astype(bf16)
                q_out[...] = q
                tail[0] = q[112:128].astype(f32)[8:16]
                tail[1] = q[240:256].astype(f32)[8:16]
        stream.wait(3)

    return call(
        body,
        "project_in",
        [Far(tokens), Far(gain_mix), Far(gain_ffn), Far(conv_weight), Far(w_in), Far(w_out)],
        [
            ((ROWS, D), bf16),
            ((1, D), f32),
            ((1, D), f32),
            ((3, 512), f32),
            ((ROWS, D), bf16),
            ((ROWS, 512), f32),
            ((ROWS, 512), f32),
            ((ROWS, 512), f32),
            ((ROWS, 512), bf16),
            ((2, 8, 512), f32),
            ((512, D), bf16),
        ],
        numbers=[place],
        scratch=[pltpu.VMEM((3, D, 512), bf16), pltpu.SemaphoreType.DMA((8,))],
    )


def prepare(place, lengths, cotangent, normed, after):
    def body(at, cot_far, len_far, one, out, grad_mine, one_mine, other, cot, flat, len_ref, sems):
        z, position, core = at[0], at[1] * 128, at[2]
        copies = [pltpu.make_async_copy(cot_far, cot, sems.at[0]), pltpu.make_async_copy(len_far, len_ref, sems.at[1])]
        for copy in copies:
            copy.start()
        flat[...] = one[...].T
        turn_into(core, flat, one_mine, other, 1024)
        for copy in copies:
            copy.wait()
        for piece in range(4):
            block = lax.rem(z + piece, 4)
            seq, half = block // 2, lax.rem(block, 2)
            first = position + half * PIECE
            rows = first + lax.broadcasted_iota(jnp.int32, (PIECE, D), 0)
            values = cot[pl.ds(rotated(z, piece), PIECE)].astype(f32)
            out[piece * PIECE : (piece + 1) * PIECE] = jnp.where(rows < len_ref[seq], values, 0.0).astype(bf16)
        flat[...] = out[...].T
        turn_into(core, flat, grad_mine, other, 0)

    return call(
        body,
        "prepare",
        [Far(cotangent), Far(lengths), normed],
        [((ROWS, D), bf16), ((1024, ROWS), bf16), ((1024, ROWS), bf16), ((2048, ROWS), bf16)],
        numbers=[place],
        scratch=[
            pltpu.VMEM((ROWS, D), bf16),
            pltpu.VMEM((D, ROWS), bf16),
            pltpu.SMEM((2,), jnp.int32),
            pltpu.SemaphoreType.DMA((2,)),
        ],
        after=after,
    )


def project_out(place, q, carried, c_gate, conv_weight, w_out, after):
    def body(at, q_ref, carried_ref, c_ref, cw, w, conv_out, y_out, own, one, two, three, pad):
        z = at[0]
        for seq in range(2):
            rows = slice(seq * 128, seq * 128 + 128)
            pad[0:8] = carried_ref[seq]
            pad[8:136] = q_ref[rows].astype(f32)
            conv_out[rows] = cw[0:1] * pad[6:134] + cw[1:2] * pad[7:135] + cw[2:3] * pad[8:136]
        for piece in range(4):
            start = rotated(z, piece)
            y_out[piece * PIECE : (piece + 1) * PIECE] = (
                c_ref[pl.ds(start, PIECE)] * conv_out[pl.ds(start, PIECE)]
            ).astype(bf16)
        for cols in spans(D, 512):
            cut(matmul(y_out[...], w[:, cols]), own, one, two, three, cols)

    return call(
        body,
        "project_out",
        [q, carried, c_gate, conv_weight, w_out],
        [((ROWS, 512), f32), ((ROWS, 512), bf16)] + PIECE_OUTS,
        numbers=[place],
        scratch=[pltpu.VMEM((136, 512), f32)],
        after=after,
    )


def activation_grad(grad_low, w_down):
    def body(grad, w_far, out, w, sems):
        stream = Stream(
            [
                pltpu.make_async_copy(w_far.at[rows], w.at[rows], sems.at[n])
                for n, rows in enumerate(spans(2048, 512))
            ]
        )
        for n, rows in enumerate(spans(2048, 512)):
            stream.wait(n)
            out[:, rows] = matmul_t(grad[...], w[rows])

    return call(
        body,
        "activation_grad",
        [grad_low, Far(w_down)],
        [((ROWS, 2048), f32)],
        scratch=[pltpu.VMEM((2048, D), bf16), pltpu.SemaphoreType.DMA((4,))],
    )[0]


def residual_norm(place, own, received, tokens, gain, after):
    def body(at, own_ref, r1, r2, r3, tok, gain_ref, hidden, normed):
        values = tok[pl.ds(rotated(at[0], 0), PIECE)].astype(f32) + added(own_ref[...], r1[...], r2[...], r3[...])
        hidden[...] = values
        normed[...] = (values * normalize(values) * gain_ref[...]).astype(bf16)

    return call(
        body,
        "residual_norm",
        [own, *received, tokens, gain],
        [((PIECE, D), f32), ((PIECE, D), bf16)],
        numbers=[place],
        after=after,
    )


def bring(name, weights, after=()):
    count = len(weights)

    def body(*refs):
        copies = [pltpu.make_async_copy(refs[n], refs[count + n], refs[-1].at[n]) for n in range(count)]
        for copy in copies:
            copy.start()
        for copy in copies:
            copy.wait()

    return call(
        body,
        name,
        [Far(weight) for weight in weights],
        [(weight.shape, weight.dtype) for weight in weights],
        scratch=[pltpu.SemaphoreType.DMA((count,))],
        after=after,
        more=1,
    )


def feed_forward(pieces, w_gate, w_up, grad_act, mixed, after):
    def body(n0, n1, n2, n3, gates, ups, ga, mix, mid, normed):
        for piece, ref in enumerate((n0, n1, n2, n3)):
            normed[piece * PIECE : (piece + 1) * PIECE] = ref[...]
        mid[:, 6144:6656] = mix[...]
        for cols in spans(2048, 256):
            gate = matmul(normed[...], gates[:, cols])
            up = matmul(normed[...], ups[:, cols])
            sigma = jax.nn.sigmoid(gate)
            swish = gate * sigma
            grad = ga[:, cols]
            first = cols.start
            mid[:, cols] = (swish * up).astype(bf16)
            mid[:, 2048 + first : 2304 + first] = (grad * up * sigma * (1.0 + gate * (1.0 - sigma))).astype(bf16)
            mid[:, 4096 + first : 4352 + first] = (grad * swish).astype(bf16)

    return call(
        body,
        "feed_forward",
        [*pieces, w_gate, w_up, grad_act, mixed],
        [((ROWS, 6656), bf16), ((ROWS, D), bf16)],
        after=after,
    )


def turn(place, value, after=()):
    def body(at, tall, mine, other, flat):
        flat[...] = tall[...].T
        turn_into(at[2], flat, mine, other)

    return call(
        body,
        "turn",
        [value],
        [((1024, ROWS), bf16), ((1024, ROWS), bf16)],
        numbers=[place],
        scratch=[pltpu.VMEM((D, ROWS), bf16)],
        after=after,
    )


def feed_back(mid, w_gate, w_up, after=()):
    def body(mid_ref, gates, ups, own, one, two, three):
        for rows in spans(D, 256):
            total = matmul_t(mid_ref[:, 2048:4096], gates[rows]) + matmul_t(mid_ref[:, 4096:6144], ups[rows])
            cut(total, own, one, two, three, rows)

    return call(body, "feed_back", [mid, w_gate, w_up], PIECE_OUTS, after=after)


def down(mid, w_down, after=()):
    def body(mid_ref, w_far, own, one, two, three, w, sems):
        stream = Stream(
            [
                pltpu.make_async_copy(w_far.at[:, cols], w.at[:, cols], sems.at[n])
                for n, cols in enumerate(spans(D, 512))
            ]
        )
        for n, cols in enumerate(spans(D, 512)):
            stream.wait(n)
            cut(matmul(mid_ref[:, 0:2048], w[:, cols]), own, one, two, three, cols)

    return call(
        body,
        "down",
        [mid, Far(w_down)],
        PIECE_OUTS,
        scratch=[pltpu.VMEM((2048, D), bf16), pltpu.SemaphoreType.DMA((4,))],
        after=after,
    )


def hidden_grad(own, received, hidden, gain, grad_low, after):
    def body(own_ref, r1, r2, r3, h, gain_ref, grad, out, gain_part):
        total = added(own_ref[...], r1[...], r2[...], r3[...])
        values = h[...]
        rate = normalize(values)
        unit = values * rate
        gain_part[...] = jnp.sum(total * unit, axis=0, keepdims=True)
        scaled = total * gain_ref[...]
        inner = jnp.mean(scaled * unit, -1, keepdims=True)
        out[...] = (grad[0:PIECE].astype(f32) + rate * (scaled - unit * inner)).astype(bf16)

    return call(
        body,
        "hidden_grad",
        [own, *received, hidden, gain, grad_low],
        [((PIECE, D), bf16), ((1, D), f32)],
        after=after,
        weight=LONG,
    )


def mixed_grad(place, pieces, w_out, convolved, c_gate, q, carried, after):
    def body(at, h0, h1, h2, h3, w, conv, c_ref, q_ref, carried_ref, dconv, dc, head, taps, mine, other, hidden, tall, pad, flat):
        z = at[0]
        for piece, ref in enumerate((h0, h1, h2, h3)):
            hidden[pl.ds(rotated(z, piece), PIECE)] = ref[...]
            tall[piece * PIECE : (piece + 1) * PIECE] = ref[...]
        for cols in spans(512, 256):
            mixed = matmul_t(hidden[...], w[cols])
            dc[:, cols] = (mixed * conv[:, cols]).astype(bf16)
            dconv[:, cols] = mixed * c_ref[:, cols]
        flat[...] = tall[...].T
        turn_into(at[2], flat, mine, other)
        sums = []
        for seq in range(2):
            rows = slice(seq * 128, seq * 128 + 128)
            head[seq] = dconv[seq * 128 : seq * 128 + 8]
            pad[0:8] = carried_ref[seq]
            pad[8:136] = q_ref[rows].astype(f32)
            here = dconv[rows]
            sums.append([jnp.sum(here * pad[6 + tap : 134 + tap], axis=0, keepdims=True) for tap in range(3)])
        for tap in range(3):
            taps[tap : tap + 1] = sums[0][tap] + sums[1][tap]

    return call(
        body,
        "mixed_grad",
        [*pieces, w_out, convolved, c_gate, q, carried],
        [
            ((ROWS, 512), f32),
            ((ROWS, 512), bf16),
            ((2, 8, 512), f32),
            ((3, 512), f32),
            ((1024, ROWS), bf16),
            ((1024, ROWS), bf16),
        ],
        numbers=[place],
        scratch=[
            pltpu.VMEM((ROWS, D), bf16),
            pltpu.VMEM((ROWS, D), bf16),
            pltpu.VMEM((136, 512), f32),
            pltpu.VMEM((D, ROWS), bf16),
        ],
        after=after,
        weight=LONG,
    )


def input_grad(place, dconv, returned, dc, b_gate, x_part, conv_weight, w_in, tokens, gain_part, taps, after):
    def body(at, dk, ret, dc_ref, b, v, cw, w, tok, gains, taps_ref, dp0, dp1, own, one, two, three, sums, pad, total, dp):
        z = at[0]
        for seq in range(2):
            rows = slice(seq * 128, seq * 128 + 128)
            pad[0:128] = dk[rows]
            pad[128:136] = ret[seq]
            dq = cw[2:3] * pad[0:128] + cw[1:2] * pad[1:129] + cw[0:1] * pad[2:130]
            dp[rows, 0:512] = (dq * v[rows]).astype(bf16)
            dp[rows, 512:1024] = dc_ref[rows]
            dp[rows, 1024:1536] = (dq * b[rows]).astype(bf16)
        rate = normalize(tok[...].astype(f32))
        sums[...] = jnp.zeros(SUMS, f32)
        for cols in spans(D, 256):
            part = (
                matmul_t(dp[:, 0:512], w[0, cols])
                + matmul_t(dp[:, 512:1024], w[1, cols])
                + matmul_t(dp[:, 1024:1536], w[2, cols])
            )
            row, first = cols.start // 512, cols.start % 512
            sums[row : row + 1, first : first + 256] = jnp.sum(
                part * (tok[:, cols].astype(f32) * rate), axis=0, keepdims=True
            )
            total[...] = part
            own[:, cols] = total[pl.ds(rotated(z, 0), PIECE)]
            one[:, cols] = total[pl.ds(rotated(z, 1), PIECE)].astype(bf16)
            two[:, cols] = total[pl.ds(rotated(z, 2), PIECE)].astype(bf16)
            three[:, cols] = total[pl.ds(rotated(z, 3), PIECE)].astype(bf16)
        for row in range(4):
            sums[4 + row : 5 + row] = gains[:, row * 512 : row * 512 + 512]
        sums[8:11] = taps_ref[...]
        dp0[...] = dp[:, 0:768]
        dp1[0:ROWS] = dp[:, 768:1536]
        high = sums[...].astype(bf16)
        dp1[ROWS : ROWS + 16, 0:512] = high
        dp1[ROWS + 16 : ROWS + 32, 0:512] = (sums[...] - high.astype(f32)).astype(bf16)

    return call(
        body,
        "input_grad",
        [dconv, returned, dc, b_gate, x_part, conv_weight, w_in, tokens, gain_part, taps],
        [((ROWS, 768), bf16), ((ROWS + 32, 768), bf16)] + PIECE_OUTS + [(SUMS, f32)],
        numbers=[place],
        scratch=[pltpu.VMEM((136, 512), f32), pltpu.VMEM((ROWS, 256), f32), pltpu.VMEM((ROWS, 1536), bf16)],
        after=after,
    )


def last_shards(place, own, received, tokens, gain, grad_hidden, own_out, out_received, hidden, sums, after=()):
    def body(at, own_ref, r1, r2, r3, tok, gain_ref, grad, own_o, o1, o2, o3, h, sums_ref, out):
        rows = slice(0, PIECE)
        total = added(own_ref[...], r1[...], r2[...], r3[...])
        values = tok[pl.ds(rotated(at[0], 0), PIECE)].astype(f32)
        rate = normalize(values)
        unit = values * rate
        scaled = total * gain_ref[...]
        inner = jnp.mean(scaled * unit, -1, keepdims=True)
        out[rows] = (grad[...].astype(f32) + rate * (scaled - unit * inner)).astype(bf16)
        out[PIECE : 2 * PIECE] = (h[...] + added(own_o[...], o1[...], o2[...], o3[...])).astype(bf16)
        pack(out, 2 * PIECE, sums_ref[...])

    return call(
        body,
        "last_shards",
        [own, *received, tokens, gain, grad_hidden, own_out, *out_received, hidden, sums],
        [((2 * PIECE + 16, D), bf16)],
        numbers=[place],
        after=after,
        weight=LONG,
    )[0]


def in_place(place, pieces, weight=1, after=()):
    def body(at, p0, p1, p2, p3, grad, out, done):
        for piece, ref in enumerate((p0, p1, p2, p3)):
            rows = pl.ds(rotated(at[0], piece), PIECE)
            grad[rows] = ref[0:PIECE]
            out[rows] = ref[PIECE : 2 * PIECE]
        done[...] = jnp.zeros((8, 128), f32)

    return call(
        body,
        "in_place",
        [*pieces],
        [Free(((ROWS, D), bf16))] * 2 + [((8, 128), f32)],
        numbers=[place],
        after=after,
        weight=weight,
    )


def weight_grad(place, name, width, plan, sums=None, after=()):
    flat = [part for half in plan for part in half]
    arrays = []
    for mine, other, _, right_mine, right_other, _, _ in flat:
        for array in (mine, other, right_mine, right_other):
            if not any(array is known for known in arrays):
                arrays.append(array)
    count = len(arrays) + (sums is not None)

    def body(order, *refs):
        def ref(array):
            return refs[[known is array for known in arrays].index(True)]

        outs = refs[count : count + 4]
        left, right = refs[-2:]
        if sums is not None:
            came = ref(plan[1][0][4])
            total = refs[count - 1][...] + came[256:272, 0:512].astype(f32) + came[272:288, 0:512].astype(f32)
            refs[count + 4][...] = total
            pack(outs[1], 512, total)
        for half in range(2):
            keep, send = outs[2 * half : 2 * half + 2]
            to = 0
            for mine, other, base, right_mine, right_other, first, columns in plan[half]:
                mine, other, right_mine, right_other = map(ref, (mine, other, right_mine, right_other))
                for position in range(16):
                    start = block_at(order, half, position) * 64
                    rows = slice(position * 64, position * 64 + 64)
                    left[rows, 0:256] = mine[pl.ds(pl.multiple_of(start, 64), 64)]
                    left[rows, 256:512] = other[pl.ds(pl.multiple_of(base + start, 64), 64)]
                for step, cols in enumerate(spans(columns, 256)):
                    at = slice(first + cols.start, first + cols.stop)
                    room = right.at[step % 2]
                    room[0:256] = right_mine[0:256, at]
                    room[256:512] = right_other[0:256, at]
                    to_cols = slice(to + cols.start, to + cols.stop)
                    total = matmul(left[...], room[...]).astype(bf16)
                    keep[:, to_cols] = total[0:512]
                    send[0:512, to_cols] = total[512:1024]
                to += columns

    shapes = [((512, width), bf16)] * 4
    if sums is not None:
        shapes = [shapes[0], ((528, width), bf16), *shapes[2:], (SUMS, f32)]
    keep0, send0, keep1, send1, *total = call(
        body,
        name,
        arrays + ([] if sums is None else [sums]),
        shapes,
        numbers=[place],
        scratch=[pltpu.VMEM((1024, 512), bf16), pltpu.VMEM((2, 512, 256), bf16)],
        after=after,
    )
    return [keep0, keep1], [send0, send1], *total


def halve(name, keeps, cames, moves, outs, sums=None, along=False, after=()):
    counts = [len(keep) for keep in keeps]
    ins = [array for keep, came in zip(keeps, cames) for array in (*keep, *came)]
    starts = [2 * sum(counts[:n]) for n in range(len(counts))]
    rows = keeps[0][0].shape[0]
    middle = rows // 2
    width = sum(move[3] for move in moves) // outs
    each = min(64, middle)
    extra = [] if sums is None else [sums]
    count = len(ins) + len(extra)

    def body(*refs):
        keep, send = refs[count : count + outs], refs[count + outs : count + 2 * outs]
        if sums is not None:
            total = refs[len(ins)][...]
            if rows < cames[0][-1].shape[0]:
                total = total + unpack(refs[2 * counts[0] - 1], rows)
            refs[count + 2 * outs][...] = total
            if along:
                pack(send[0], middle, total)

        @pl.loop(0, middle // each)
        def _(step):
            low = pl.ds(pl.multiple_of(step * each, each), each)
            high = pl.ds(pl.multiple_of(middle + step * each, each), each)
            for group, part, first, columns, out, to in moves:
                k, c = refs[starts[group] + part], refs[starts[group] + counts[group] + part]
                take, put = slice(first, first + columns), slice(to, to + columns)
                keep[out][low, put] = k[low, take] + c[low, take]
                send[out][low, put] = k[high, take] + c[high, take]

    sends = [((middle + 16 * (along and n == 0), width), bf16) for n in range(outs)]
    shapes = [((middle, width), bf16)] * outs + sends + ([] if sums is None else [(SUMS, f32)])
    results = call(body, name, ins + extra, shapes, after=after)
    return results[:outs], results[outs : 2 * outs], *results[2 * outs :]


def sum_gains(own, pieces, after):
    def body(sums, r1, r2, r3, out):
        out[...] = sums[...]
        out[0:8] = (sums[0:8] + unpack(r1, 128)[0:8]) + (unpack(r2, 128)[0:8] + unpack(r3, 128)[0:8])

    return call(body, "sum_gains", [own, *pieces[1:]], [(SUMS, f32)], after=after)[0]


def sum_over_stage(value, stage, weight=1, after=()):
    def body(a, b, out):
        out[...] = a[...] + b[...]

    came = lax.ppermute(value, "seq", stage_pairs(0, stage))
    return call(body, "sum_stage", [value, came], [(SUMS, f32)], after=after, weight=weight)[0]


def finish(keeps, cames, sums, after=()):
    def body(k0, k1, c0, c1, sums_ref, down_out, gate, up, grad_in, grad_out, mix, ffn, conv):
        for half, (k, c, pair) in enumerate(((k0, c0, gate), (k1, c1, up))):

            def total(first, count, k=k, c=c):
                cols = slice(first, first + count)
                return k[:, cols].astype(f32) + c[:, cols].astype(f32)

            down_out[:, half * 1024 : half * 1024 + 1024] = total(0, 1024)
            pair[...] = total(1024, 2048)
            if half == 0:
                grad_in[0] = total(3072, 512)
                grad_in[1, :, 0:256] = total(3584, 256)
            else:
                grad_in[1, :, 256:512] = total(3072, 256)
                grad_in[2] = total(3328, 512)
            grad_out[:, half * 256 : half * 256 + 256] = total(3840, 256)
        sums_all = sums_ref[...]
        for row in range(4):
            mix[:, row * 512 : row * 512 + 512] = sums_all[row : row + 1]
            ffn[:, row * 512 : row * 512 + 512] = sums_all[4 + row : 5 + row]
        conv[...] = sums_all[8:11]

    return call(
        body,
        "finish",
        [*keeps, *cames, sums],
        [Free(((64, 2048), f32))] * 3
        + [Free(((3, 64, 512), f32)), Free(((64, 512), f32))]
        + [Free(((1, D), f32))] * 2
        + [Free(((3, 512), f32))],
        after=after,
    )


def to_next(value, axis, steps):
    count = lax.axis_size(axis)
    first, last = (max(0, -steps), min(count, count - steps))
    return lax.ppermute(value, axis, [(source, source + steps) for source in range(first, last)])


def around(value, steps):
    return lax.ppermute(value, "tp", [(source, (source + steps) % 4) for source in range(4)])


def scattered(pieces):
    far = around(pieces[1], 2)
    return [far, around(pieces[0], 1), around(pieces[2], 3)]


def gathered(shard):
    far = around(shard, 2)
    return [shard, around(shard, 3), far, around(shard, 1)]


def other_core(value):
    return lax.ppermute(value, "seq", CORE_PAIRS)


def exchange(stage, sends):
    return [lax.ppermute(send, "seq", stage_pairs(half, stage)) for half, send in enumerate(sends)]


def per_device(
    tokens, gain_mix, w_in, conv_weight, w_out, gain_ffn, w_gate, w_up, w_down, cotangent, lengths
):
    seq, z = lax.axis_index("seq"), lax.axis_index("tp")
    place = jnp.stack([z, seq, lax.rem(seq, 2)]).astype(jnp.int32)
    tokens = tokens.reshape(ROWS, D)
    cotangent = cotangent.reshape(ROWS, D)
    w_in = jnp.transpose(w_in, (1, 0, 2))

    tokens, gain_mix, gain_ffn, conv_weight, normed, b_gate, c_gate, x_part, q, tail, near_out = project_in(
        place, tokens, gain_mix.reshape(1, D), gain_ffn.reshape(1, D), conv_weight, w_in, w_out
    )
    carried = to_next(tail, "seq", 1)
    convolved, mixed, own, *pieces = project_out(place, q, carried, c_gate, conv_weight, near_out, after=[])
    received = scattered(pieces)
    grad_low, grad_turned, one_turned, turned = prepare(place, lengths, cotangent, normed, after=[own])
    grad_act = activation_grad(grad_low, w_down)
    hidden, shard = residual_norm(place, own, received, tokens, gain_ffn, after=[grad_act])
    normed_two = gathered(shard)
    gates, ups = bring("bring_ffn", [w_gate, w_up], after=[shard])
    (turned,) = release("release_turned", [turned], after=[ups])
    turned_other = other_core(turned)

    mid, normed_two = feed_forward(normed_two, gates, ups, grad_act, mixed, after=[turned_other])
    mid_other = other_core(mid)
    own, *pieces = feed_back(mid, gates, ups)
    received = scattered(pieces)

    two_turned, two_sent = turn(place, normed_two, after=[own])
    two_other = other_core(two_sent)
    keep_a, send_a = weight_grad(
        place,
        "weight_grad_a",
        1024,
        [[(grad_turned, turned_other, 0, mid, mid_other, 1024 * half, 1024)] for half in range(2)],
        after=[two_sent],
    )
    came_a = exchange(0, send_a)

    def weight_grad_b(part, after):
        return weight_grad(
            place,
            "weight_grad_b",
            1024,
            [
                [(two_turned, two_other, 0, mid, mid_other, 2048 + 2048 * half + 1024 * part, 1024)]
                for half in range(2)
            ],
            after=after,
        )

    keep_b, send_b = weight_grad_b(0, [send_a[0]])
    hidden_low, gain_part = hidden_grad(own, received, hidden, gain_ffn, grad_low, after=[send_b[0]])
    hidden_pieces = gathered(hidden_low)
    near_out, near_in = bring("bring_mixer", [w_out, w_in], after=[hidden_low])
    send_b = release("release_b", send_b, after=[*came_a, near_in])
    came_b = exchange(0, send_b)
    keep_d, send_d = weight_grad_b(1, [send_b[0]])
    own_out, *out_pieces = down(mid, w_down, after=[send_d[0]])

    dconv, dc, head, taps, hidden_turned, hidden_sent = mixed_grad(
        place, hidden_pieces, near_out, convolved, c_gate, q, carried, after=[near_in, own_out]
    )
    returned = to_next(head, "seq", -1)
    send_d = release("release_d", send_d, after=[*came_b, returned])
    came_d = exchange(0, send_d)
    hidden_other = other_core(hidden_sent)
    *dp, own, one, two, three, sums = input_grad(
        place, dconv, returned, dc, b_gate, x_part, conv_weight, near_in, tokens, gain_part, taps,
        after=[hidden_other, send_d[0]],
    )
    dp_other = [other_core(part) for part in dp]
    keep_c, send_c, sums = weight_grad(
        place,
        "weight_grad_c",
        1024,
        [
            [
                (one_turned, turned_other, 1024, dp[half], dp_other[half], 0, 768),
                (hidden_turned, hidden_other, 0, mid, mid_other, 6144 + 256 * half, 256),
            ]
            for half in range(2)
        ],
        sums=sums,
        after=[own],
    )
    pieces = release("release_z", [one, two, three], after=[*dp_other, send_c[0]])
    received = release("hold", scattered(pieces), weight=LONG)
    send_c = release("release_c", send_c, after=came_d)
    came_c = exchange(0, send_c)

    keep, send, sums = halve(
        "halve_abc",
        list(zip(keep_a, keep_b, keep_d, keep_c)),
        list(zip(came_a, came_b, came_d, came_c)),
        [(half, part, 0, 1024, half, 1024 * part) for half in range(2) for part in range(4)],
        2,
        sums=sums,
        after=received,
    )
    came = exchange(1, send)
    out_received = scattered(release("release_out", out_pieces, after=received))
    shards = last_shards(
        place, own, received, tokens, gain_mix, hidden_low, own_out, out_received, hidden, sums, after=[]
    )
    pieces = gathered(shards)
    grad_tokens, output, done = in_place(place, pieces, LONG)
    whole = [(half, 0, 0, 4096, half, 0) for half in range(2)]
    keep, send = halve("halve_d", [[k] for k in keep], [[c] for c in came], whole, 2, after=[shards])
    came = exchange(2, send)
    sums = sum_gains(sums, pieces, after=[send[0], done])
    keep, send = halve("halve_e", [[k] for k in keep], [[c] for c in came], whole, 2, after=[done])
    came = exchange(3, send)
    for stage in (1, 2, 3):
        sums = sum_over_stage(sums, stage, LONG if stage == 1 else 1, after=[send[0]])
    grad_down, grad_gate, grad_up, grad_in, grad_out, gain_mix_sum, gain_ffn_sum, conv_sum = finish(keep, came, sums)

    return (
        output.reshape(2, 128, D),
        grad_tokens.reshape(2, 128, D),
        gain_mix_sum.reshape(D),
        jnp.transpose(grad_in, (1, 0, 2)),
        conv_sum,
        grad_out.T,
        gain_ffn_sum.reshape(D),
        grad_gate,
        grad_up,
        grad_down.T,
    )


def solution(mesh):
    placed = (
        P(None, "seq", None),
        P(),
        P(None, None, "tp"),
        P(None, "tp"),
        P("tp", None),
        P(),
        P(None, "tp"),
        P(None, "tp"),
        P("tp", None),
        P(None, "seq", None),
        P(),
    )
    return jax.shard_map(
        per_device,
        mesh=mesh,
        in_specs=placed,
        out_specs=(
            P(None, "seq", None),
            P(None, "seq", None),
            P(),
            P("seq", None, "tp"),
            P(None, "tp"),
            P("tp", "seq"),
            P(),
            P("seq", "tp"),
            P("seq", "tp"),
            P("tp", "seq"),
        ),
        check_vma=False,
    )
```
